32 devices in a mesh: batch: 2 (over x), head: 2 (over y), blk: 8 (over z, core).
Axes of the slice: x: 2, y: 2, z: 4, core: 2. Of those that a mesh axis runs over, the one named last changes fastest.
Arguments:
- tokens: bfloat16 [16, 2048, 1024], P(('batch', 'blk'), 'head'), parts along dimension 0, may hold values from -10.5 to 10.5
- proj_weight: bfloat16 [1024, 3072], replicated, may hold values from -0.1875 to 0.1875
- out_weight: bfloat16 [1024, 1024], replicated, may hold values from -1.5 to 1.5
- pattern: int32 [256, 16], P(('batch', 'blk')), parts along dimension 0, may hold values from 0 to 127, as said below
Outputs:
- mixed_out: bfloat16 [16, 2048, 1024], P(('batch', 'blk'), 'head'), parts along dimension 0
The draws below stay inside these ranges and needn't reach their ends.
There are 2 independent parts, one for each index of `batch`. The reference program is written for one: setup_inputs(seed, part) draws one part's arguments, and reference() takes and returns one part's arrays. A program takes and returns all parts, laid end to end along the dimension named above; an argument that names none is the same for every part. Nothing has to cross between parts.
Inputs may be any that keep to these rules, and one draw needn't show every extreme that they name: `pattern`: row i lists first 6 distinct blocks j with |j - i| <= 8, among them i itself, then 10 distinct summary blocks j (j % 16 >= 12) with |j - i| > 8. Every row with 8 <= i < 120 lists i - 8 and i + 8.
All inputs are finite; a program needn't handle non-finite values.
Results may differ from the reference program's by a relative error of at most 0.0095.
Values may be sent and summed in bfloat16 or wider, within the bound.
No kernel may reach another device: no remote copies, remote signals or barrier semaphores. Data moves between devices by JAX's collectives and lax.ppermute only.
A program may use at most 128 MiB of HBM per device.

```python
import jax
import jax.numpy as jnp
from jax import lax

D = 1024
H = 16
HD = 64
BLK = 128
TOK_DEV = 2048
REACH = 8
LSEL = 6
SSEL = 10
SUMB = 4
SB = 16
KSEL = 16
TOKENS = 16384
NBLOCKS = 128
NSUM = 32
N_BLK = 8


def draw_tokens(key, part):
    shape = (N_BLK, TOK_DEV, D)
    keys = jax.random.split(key, 1)
    return jnp.clip(1.25 * jax.random.normal(keys[0], shape, jnp.float32), -7.5, 7.5).astype(jnp.bfloat16)


def draw_proj_weight(key, part):
    weight = jnp.clip(jax.random.normal(key, (D, 3 * D), jnp.float32), -6.0, 6.0) * D ** (-0.5)
    return weight.astype(jnp.bfloat16)


def draw_pattern(key, part):
    keys = jax.random.split(key, 2)
    span = 2 * REACH + 1
    rows = jnp.arange(NBLOCKS, dtype=jnp.int32)[:, None]
    offsets = jnp.arange(span, dtype=jnp.int32)[None, :] - REACH
    target = rows + offsets
    valid = jnp.logical_and(target >= 0, target < NBLOCKS)
    forced = jnp.logical_or(offsets == 0, jnp.logical_or(offsets == -REACH, offsets == REACH))
    column = jnp.arange(span, dtype=jnp.int32)[None, :]
    noise = jax.random.randint(keys[0], (NBLOCKS, span), 0, 2 ** 20)
    ranked = 64 + noise * span + column
    ranked = jnp.where(forced, column, ranked)
    ranked = jnp.where(valid, ranked, 2 ** 30 + column)
    order = jnp.argsort(ranked, axis=1)[:, :LSEL]
    near_ids = jnp.take_along_axis(target, order, axis=1)
    counter = jnp.arange(NSUM, dtype=jnp.int32)
    summary_ids = counter // SUMB * SB + SB - SUMB + counter % SUMB
    too_near = jnp.abs(summary_ids[None, :] - rows) <= REACH
    noise_far = jax.random.randint(keys[1], (NBLOCKS, NSUM), 0, 2 ** 20)
    ranked_far = jnp.where(too_near, 2 ** 30 + counter[None, :], noise_far * NSUM + counter[None, :])
    order_far = jnp.argsort(ranked_far, axis=1)[:, :SSEL]
    far_ids = summary_ids[order_far]
    return jnp.concatenate([near_ids, far_ids], axis=1).astype(jnp.int32)


def scatter_about(key, shape, deviation, bound, kind=jnp.bfloat16):
    entries = deviation * jax.random.normal(key, shape, jnp.float32)
    return jnp.clip(entries, min=-bound, max=bound).astype(kind)


def setup_inputs(seed: int = 0, part: int = 0) -> dict:
    splits = jax.random.split(jax.random.key(seed), 5)
    own_keys = jax.random.split(jax.random.fold_in(splits[4], part), 5)
    return {
        "tokens": draw_tokens(jax.random.fold_in(jax.random.fold_in(splits[4], part), 71), part),
        "proj_weight": draw_proj_weight(jax.random.fold_in(splits[4], 71), part),
        "out_weight": scatter_about(splits[2], (D, D), (8.0 / D ** 0.5), 1.5),
        "pattern": draw_pattern(jax.random.fold_in(jax.random.fold_in(splits[4], part), 71), part),
    }


def attend_block(queries, key_rows, value_rows):
    scores = jnp.einsum("qhe,khe->hqk", queries.astype(jnp.float32), key_rows.astype(jnp.float32)) * (HD ** -0.5)
    row_max = jnp.max(scores, axis=-1, keepdims=True)
    raised = jnp.exp(scores - row_max)
    weights = (raised / jnp.sum(raised, axis=-1, keepdims=True)).astype(jnp.bfloat16)
    result = jnp.einsum("hqk,khe->qhe", weights.astype(jnp.float32), value_rows.astype(jnp.float32))
    return result.astype(jnp.bfloat16)


def reference(tokens, proj_weight, out_weight, pattern):
    flat = tokens.reshape(TOKENS, D)
    projected = jnp.dot(flat, proj_weight, preferred_element_type=jnp.float32).astype(jnp.bfloat16)
    shaped = projected.reshape(NBLOCKS, BLK, H, 3, HD)
    queries = shaped[:, :, :, 0]
    keys_all = shaped[:, :, :, 1]
    values_all = shaped[:, :, :, 2]

    def one_block(index):
        chosen = pattern[index]
        key_rows = keys_all[chosen].reshape(KSEL * BLK, H, HD)
        value_rows = values_all[chosen].reshape(KSEL * BLK, H, HD)
        return attend_block(queries[index], key_rows, value_rows)

    heads = lax.map(one_block, jnp.arange(NBLOCKS, dtype=jnp.int32))
    heads = heads.reshape(TOKENS, D)
    mixed_out = jnp.dot(heads, out_weight, preferred_element_type=jnp.float32).astype(jnp.bfloat16)
    return mixed_out.reshape(N_BLK, TOK_DEV, D)
```

```python
import functools

import jax
import jax.numpy as jnp
from jax import lax
from jax.experimental import pallas as pl
from jax.experimental.pallas import tpu as pltpu
from jax.sharding import PartitionSpec as P

D = 1024
H = 16
HD = 64
BLK = 128
REACH = 8
LSEL = 6
SUMB = 4
SB = 16
KSEL = 16
PAIRS = H // 2
LANES = 2 * HD
LOG2E = 1.4426950408889634
TOTAL_CAP = 2.0**100


def split_kernel(weight_ref, query_ref, key_ref, value_ref):
    both = weight_ref[...]
    first, second = both[:, : 3 * HD], both[:, 3 * HD :]

    def columns(which):
        lo = which * HD
        return jnp.concatenate([first[:, lo : lo + HD], second[:, lo : lo + HD]], axis=1)

    query_ref[...] = columns(0).T
    key_ref[...] = columns(1)
    value_ref[...] = columns(2).T


def split_weights(proj_weight):
    wide = jax.ShapeDtypeStruct((D, D), jnp.bfloat16)
    across = pl.BlockSpec((LANES, D), lambda p: (p, 0))
    down = pl.BlockSpec((D, LANES), lambda p: (0, p))
    return pl.pallas_call(
        split_kernel,
        grid=(PAIRS,),
        in_specs=[pl.BlockSpec((D, 3 * LANES), lambda p: (0, p))],
        out_specs=[across, down, across],
        out_shape=[wide, wide, wide],
        cost_estimate=pl.CostEstimate(flops=0, bytes_accessed=4 * D * 3 * D, transcendentals=0),
        name="split_weights",
    )(proj_weight)


def attend_kernel(
    blocks, table_ref, query_ref, near_key_ref, near_value_ref, far_key_ref, far_value_ref, out_ref, peak_ref
):
    f32, bf16 = jnp.float32, jnp.bfloat16
    row = lax.broadcasted_iota(jnp.int32, (LANES, BLK), 0)
    ones = jnp.ones((16, 2 * BLK), bf16)

    def queries(index):
        own = query_ref[:, pl.ds(pl.multiple_of(index * BLK, BLK), BLK)]
        zero = jnp.zeros_like(own)
        return jnp.concatenate([jnp.where(row < HD, own, zero), jnp.where(row < HD, zero, own)], axis=1)

    def place(index, which):
        return pl.multiple_of(table_ref[index, which] * BLK, BLK)

    def keys(ref, index, which):
        return jnp.concatenate([ref[pl.ds(place(index, which + n), BLK), :] for n in range(2)], axis=0)

    def values(ref, index, which):
        picked = [ref[:, pl.ds(place(index, which + n), BLK)] for n in range(2)]
        return jnp.concatenate([jnp.concatenate(picked, axis=1), ones], axis=0)

    def score(ref, index, which, query):
        return jnp.dot(keys(ref, index, which), query, preferred_element_type=f32)

    def gather(ref, index, which, scores, shift):
        raised = jnp.exp2(scores - shift).astype(bf16)
        return jnp.dot(values(ref, index, which), raised, preferred_element_type=f32)

    def finish(index, total):
        scaled = total[:LANES] / total[LANES : LANES + 1]
        mine = jnp.concatenate([scaled[:HD, :BLK], scaled[HD:, BLK:]], axis=0)
        out_ref[pl.ds(pl.multiple_of(index * BLK, BLK), BLK), :] = mine.T.astype(bf16)

    def refs(which):
        return (near_key_ref, near_value_ref) if which < LSEL else (far_key_ref, far_value_ref)

    peak_ref[...] = jnp.zeros_like(peak_ref)

    def one(index):
        query = queries(index)
        total = None
        for which in range(0, KSEL, 2):
            key_ref, value_ref = refs(which)
            scores = score(key_ref, index, which, query)
            if which == 0:
                shift = jnp.max(scores, axis=0, keepdims=True)
            part = gather(value_ref, index, which, scores, shift)
            total = part if total is None else total + part
        peak_ref[...] = jnp.maximum(peak_ref[...], total[LANES : LANES + 8])
        finish(index, total)

    def step(number, carry):
        for n in range(2):
            one(2 * number + n)
        return carry

    if blocks % 2:
        lax.fori_loop(0, blocks, lambda index, carry: (one(index), carry)[1], 0)
    else:
        lax.fori_loop(0, blocks // 2, step, 0)

    @pl.when(jnp.logical_not(jnp.max(peak_ref[...]) <= TOTAL_CAP))
    def _():
        def whole_row(index, carry):
            query = queries(index)
            shift = jnp.full((1, 2 * BLK), -jnp.inf, f32)
            for which in range(0, KSEL, 2):
                scores = score(refs(which)[0], index, which, query)
                shift = jnp.maximum(shift, jnp.max(scores, axis=0, keepdims=True))
            total = jnp.zeros((LANES + 16, 2 * BLK), f32)
            for which in range(0, KSEL, 2):
                key_ref, value_ref = refs(which)
                total += gather(value_ref, index, which, score(key_ref, index, which, query), shift)
            finish(index, total)
            return carry

        lax.fori_loop(0, blocks, whole_row, 0)


def attend(table, query, near_key, near_value, far_key, far_value):
    rows = query.shape[1]
    blocks = rows // BLK
    pair_rows = lambda array: pl.BlockSpec((LANES, array.shape[1]), lambda p: (p, 0))
    pair_columns = lambda array: pl.BlockSpec((array.shape[0], LANES), lambda p: (0, p))
    scores = rows * KSEL * BLK * H
    moved = 2 * (near_key.size + near_value.size + far_key.size + far_value.size + 2 * query.size)
    return pl.pallas_call(
        functools.partial(attend_kernel, blocks),
        grid=(PAIRS,),
        in_specs=[
            pl.BlockSpec(memory_space=pltpu.SMEM),
            pair_rows(query),
            pair_columns(near_key),
            pair_rows(near_value),
            pair_columns(far_key),
            pair_rows(far_value),
        ],
        out_specs=pl.BlockSpec((rows, LANES), lambda p: (0, p)),
        out_shape=jax.ShapeDtypeStruct((rows, D), jnp.bfloat16),
        scratch_shapes=[pltpu.VMEM((8, 2 * BLK), jnp.float32)],
        compiler_params=pltpu.CompilerParams(vmem_limit_bytes=48 * 2**20),
        cost_estimate=pl.CostEstimate(
            flops=4 * scores * HD * 4, bytes_accessed=moved, transcendentals=scores
        ),
        name="attend",
    )(table, query, near_key, near_value, far_key, far_value)


def project_rows(rows, weight):
    return jnp.dot(rows, weight, preferred_element_type=jnp.float32).astype(jnp.bfloat16)


def project_columns(weight, rows, scale=None):
    wide = lax.dot_general(weight, rows, (((1,), (1,)), ((), ())), preferred_element_type=jnp.float32)
    return (wide if scale is None else wide * scale).astype(jnp.bfloat16)


def on_device(tokens, proj_weight, out_weight, pattern):
    heads = lax.axis_size("head")
    strides = lax.axis_size("blk")
    place = lax.axis_index("head")
    stride = lax.axis_index("blk")
    own = tokens[0]
    blocks = own.shape[0] // BLK
    lower = place < heads // 2

    whole = lax.all_gather(own, "head", axis=0, tiled=True)
    half = whole.shape[0] // 2
    leaving = jnp.where(lower, whole[half:], whole[:half])
    steps = []
    for h in range(heads):
        for s in range(strides - 1):
            ends = (h * strides + s, h * strides + s + 1)
            steps.append(ends if h < heads // 2 else ends[::-1])
    arriving = lax.ppermute(leaving, ("head", "blk"), steps)
    near_rows = jnp.concatenate([whole, arriving], axis=0)
    far_rows = lax.all_gather(whole[-SUMB * BLK :], "blk", axis=0, tiled=True)

    query_weight, key_weight, value_weight = split_weights(proj_weight)
    query = project_columns(query_weight, own, LOG2E * HD**-0.5)
    near_key = project_rows(near_rows, key_weight)
    near_value = project_columns(value_weight, near_rows)
    far_key = project_rows(far_rows, key_weight)
    far_value = project_columns(value_weight, far_rows)

    listed = lax.dynamic_slice_in_dim(pattern, place * blocks, blocks, 0)
    near = listed[:, :LSEL] - stride * SB
    near = jnp.where(near < 0, near + SB + REACH, near)
    far = listed[:, LSEL:]
    far = far // SB * SUMB + far % SB - (SB - SUMB)
    table = jnp.concatenate([near, far], axis=1)

    mixed = attend(table, query, near_key, near_value, far_key, far_value)
    out = project_rows(mixed, out_weight)
    return out.reshape(tokens.shape)


def solution(mesh):
    return jax.shard_map(
        on_device,
        mesh=mesh,
        in_specs=(P(("batch", "blk"), "head", None), P(), P(), P(("batch", "blk"), None)),
        out_specs=P(("batch", "blk"), "head", None),
        check_vma=False,
    )
```

```python
import functools

import jax
import jax.numpy as jnp
from jax import lax
from jax.experimental import pallas as pl
from jax.experimental.pallas import tpu as pltpu
from jax.sharding import PartitionSpec as P

D = 1024
H = 16
HD = 64
BLK = 128
REACH = 8
LSEL = 6
SUMB = 4
SB = 16
KSEL = 16
PAIRS = H // 2
LANES = 2 * HD
TILE = 512
TOTAL_CAP = 2.0**100


def split_kernel(weight_ref, query_ref, both_ref):
    both = weight_ref[...]
    first, second = both[:, : 3 * HD], both[:, 3 * HD :]

    def columns(which):
        lo = which * HD
        return jnp.concatenate([first[:, lo : lo + HD], second[:, lo : lo + HD]], axis=1)

    query_ref[...] = columns(0).T
    both_ref[...] = jnp.concatenate([columns(1), columns(2)], axis=1)


def split_weights(proj_weight):
    return pl.pallas_call(
        split_kernel,
        grid=(PAIRS,),
        in_specs=[pl.BlockSpec((D, 3 * LANES), lambda p: (0, p))],
        out_specs=[pl.BlockSpec((LANES, D), lambda p: (p, 0)), pl.BlockSpec((D, 2 * LANES), lambda p: (0, p))],
        out_shape=[jax.ShapeDtypeStruct((D, D), jnp.bfloat16), jax.ShapeDtypeStruct((D, 2 * D), jnp.bfloat16)],
        cost_estimate=pl.CostEstimate(flops=0, bytes_accessed=4 * D * 3 * D, transcendentals=0),
        name="split_weights",
    )(proj_weight)


def attend_kernel(first, last, blocks, count, sources, *refs):
    f32, bf16 = jnp.float32, jnp.bfloat16
    refs = list(refs)
    table_ref, query_ref, weight_ref = refs[:3]
    source_refs = refs[3 : 3 + sources]
    refs = refs[3 + sources :]
    if not first:
        sum_in_ref, row_in_ref = refs[:2]
        refs = refs[2:]
    if last:
        out_ref = refs.pop(0)
    else:
        sum_out_ref, row_out_ref = refs[:2]
        refs = refs[2:]
    slots = [(refs[0], refs[1]), (refs[2], refs[3])]

    row = lax.broadcasted_iota(jnp.int32, (LANES, BLK), 0)
    ones = jnp.ones((16, 2 * BLK), bf16)

    def at(index, size=BLK):
        return pl.ds(pl.multiple_of(index * size, size), size)

    def project_rows(pair, pieces, slot):
        key_ref, value_ref = slot
        weight = weight_ref[:, at(pair, 2 * LANES)]
        parts = [ref[pl.ds(start, size), :] for ref, start, size, _ in pieces]
        rows = parts[0] if len(parts) == 1 else jnp.concatenate(parts, axis=0)
        both = jnp.dot(rows, weight, preferred_element_type=f32).astype(bf16)
        done = 0
        for _, _, size, target in pieces:
            part = both[done : done + size]
            key_ref[pl.ds(target, size), :] = part[:, :LANES]
            value_ref[:, pl.ds(target, size)] = part[:, LANES:].T
            done += size

    def project(pair, index, slot):
        offset = 0
        small = []
        for ref in source_refs:
            size = ref.shape[0] // blocks
            start = pl.multiple_of(index * size, BLK)
            if size <= TILE:
                small.append((ref, start, size, pl.multiple_of(offset + start, BLK)))
            else:

                def tile(n, carry, ref=ref, start=start, offset=offset):
                    begin = pl.multiple_of(start + n * TILE, BLK)
                    project_rows(pair, [(ref, begin, TILE, pl.multiple_of(offset + begin, BLK))], slot)
                    return carry

                lax.fori_loop(0, size // TILE, tile, 0)
            offset += ref.shape[0]
        if small:
            project_rows(pair, small, slot)

    def queries(half, index):
        own = query_ref[half * LANES : (half + 1) * LANES, at(index)]
        zero = jnp.zeros_like(own)
        return jnp.concatenate([jnp.where(row < HD, own, zero), jnp.where(row < HD, zero, own)], axis=1)

    def places(index, which):
        return [pl.multiple_of(table_ref[index, which + n] * BLK, BLK) for n in range(2)]

    def score(slot, index, which, query):
        keys = [slot[0][pl.ds(place, BLK), :] for place in places(index, which)]
        return jnp.dot(jnp.concatenate(keys, axis=0), query, preferred_element_type=f32)

    def gather(slot, index, which, scores, shift):
        raised = jnp.exp(scores - shift).astype(bf16)
        picked = jnp.concatenate([slot[1][:, pl.ds(place, BLK)] for place in places(index, which)], axis=1)
        return jnp.dot(jnp.concatenate([picked, ones], axis=0), raised, preferred_element_type=f32)

    def by_head(rows):
        return jnp.where(row < HD, rows[:, :BLK], rows[:, BLK:])

    def finish(half, index, shift, total, rescale=None):
        mine = jnp.concatenate([total[:HD, :BLK], total[HD:LANES, BLK:]], axis=0)
        count_all = total[LANES : LANES + 1]
        span = slice(half * LANES, (half + 1) * LANES)
        if not first:
            before = sum_in_ref[span, at(index)]
            count_before = row_in_ref[half, 1:2, at(index, 2 * BLK)]
            if rescale is not None:
                before = before * by_head(rescale)
                count_before = count_before * rescale
            mine = mine + before
            count_all = count_all + count_before
        if last:
            out_ref[at(index), span] = (mine * by_head(1.0 / count_all)).T.astype(bf16)
        else:
            sum_out_ref[span, at(index)] = mine
            row_out_ref[half, 0:1, at(index, 2 * BLK)] = shift
            row_out_ref[half, 1:2, at(index, 2 * BLK)] = count_all
        return count_all

    def one(half, index):
        query = queries(half, index)
        slot = slots[half]
        total = None
        shift = None if first else row_in_ref[half, 0:1, at(index, 2 * BLK)]
        for which in range(0, count, 2):
            scores = score(slot, index, which, query)
            if shift is None:
                shift = jnp.max(scores, axis=0, keepdims=True)
            part = gather(slot, index, which, scores, shift)
            total = part if total is None else total + part
        return finish(half, index, shift, total)

    def whole_row(half, index):
        query = queries(half, index)
        slot = slots[half]
        shift = jnp.full((1, 2 * BLK), -jnp.inf, f32) if first else row_in_ref[half, 0:1, at(index, 2 * BLK)]
        old = shift

        def largest(n, shift):
            return jnp.maximum(shift, jnp.max(score(slot, index, 2 * n, query), axis=0, keepdims=True))

        shift = lax.fori_loop(0, count // 2, largest, shift)

        def add(n, total):
            return total + gather(slot, index, 2 * n, score(slot, index, 2 * n, query), shift)

        total = lax.fori_loop(0, count // 2, add, jnp.zeros((LANES + 16, 2 * BLK), f32))
        finish(half, index, shift, total, None if first else jnp.exp(old - shift))

    step = pl.program_id(0)
    steps = pl.num_programs(0)
    together = 2 if blocks % 2 == 0 else 1

    def attend_pair(half, following):
        def body(number, peak):
            for n in range(together):
                index = number * together + n
                if following is not None:
                    project(following, index, slots[1 - half])
                peak = jnp.maximum(peak, one(half, index))
            return peak

        return lax.fori_loop(0, blocks // together, body, jnp.zeros((1, 2 * BLK), f32))

    def repair(half, peak):
        @pl.when(jnp.logical_not(jnp.max(peak) <= TOTAL_CAP))
        def _():
            lax.fori_loop(0, blocks, lambda index, carry: (whole_row(half, index), carry)[1], 0)

    @pl.when(step == 0)
    def _():
        lax.fori_loop(0, blocks, lambda index, carry: (project(0, index, slots[0]), carry)[1], 0)

    repair(0, attend_pair(0, 2 * step + 1))

    @pl.when(step < steps - 1)
    def _():
        repair(1, attend_pair(1, 2 * step + 2))

    @pl.when(step == steps - 1)
    def _():
        repair(1, attend_pair(1, None))


def attend(name, table, query, weight, sources, state, last):
    f32, bf16 = jnp.float32, jnp.bfloat16
    rows = query.shape[1]
    blocks = rows // BLK
    count = table.shape[1]
    total_rows = sum(source.shape[0] for source in sources)
    whole = lambda array: pl.BlockSpec(array.shape, lambda g: (0, 0), pipeline_mode=pl.Buffered(1))
    columns = pl.BlockSpec((2 * LANES, rows), lambda g: (g, 0))
    per_row = pl.BlockSpec((2, 2, 2 * rows), lambda g: (g, 0, 0))
    in_specs = [pl.BlockSpec(memory_space=pltpu.SMEM), columns, whole(weight)]
    in_specs += [whole(source) for source in sources]
    if state:
        in_specs += [columns, per_row]
    if last:
        out_specs = pl.BlockSpec((rows, 2 * LANES), lambda g: (0, g))
        out_shape = jax.ShapeDtypeStruct((rows, D), bf16)
    else:
        out_specs = [columns, per_row]
        out_shape = [jax.ShapeDtypeStruct((D, rows), f32), jax.ShapeDtypeStruct((PAIRS, 2, 2 * rows), f32)]
    scores = rows * count * BLK * H
    return pl.pallas_call(
        functools.partial(attend_kernel, not state, last, blocks, count, len(sources)),
        grid=(PAIRS // 2,),
        in_specs=in_specs,
        out_specs=out_specs,
        out_shape=out_shape,
        scratch_shapes=[pltpu.VMEM((total_rows, LANES), bf16), pltpu.VMEM((LANES, total_rows), bf16)] * 2,
        compiler_params=pltpu.CompilerParams(vmem_limit_bytes=48 * 2**20),
        cost_estimate=pl.CostEstimate(
            flops=16 * scores * HD + 4 * total_rows * D * D,
            bytes_accessed=2 * (total_rows * D + weight.size + query.size) + 8 * rows * D,
            transcendentals=scores,
        ),
        name=name,
    )(table, query, weight, *sources, *state)


def on_device(tokens, proj_weight, out_weight, pattern):
    heads = lax.axis_size("head")
    strides = lax.axis_size("blk")
    place = lax.axis_index("head")
    stride = lax.axis_index("blk")
    own = tokens[0]
    blocks = own.shape[0] // BLK
    lower = place < heads // 2
    summary = SUMB * BLK
    share = summary // heads

    along = []
    for h in range(heads):
        for s in range(strides - 1):
            ends = (h * strides + s, h * strides + s + 1)
            along.append(ends if h < heads // 2 else ends[::-1])
    to_next = lambda rows: lax.ppermute(rows, ("head", "blk"), along)

    if heads == 2:
        swap = lambda rows: lax.ppermute(rows, "head", [(0, 1), (1, 0)])
        cut = own.shape[0] - summary
        other_mid = swap(own[cut : cut + share])
        piece = jnp.where(lower, other_mid, own[cut + share :])
        far_rows = lax.all_gather(piece, ("blk", "head"), axis=0, tiled=True)
        other_low = swap(own[:cut])
        other_high = jnp.concatenate([other_mid, swap(own[cut + share :])], axis=0)
        other = jnp.concatenate([other_low, other_high], axis=0)
        edge = jnp.concatenate([to_next(other_low), to_next(other_high)], axis=0)
        near_rows = [own, other, edge]
    else:
        stride_rows = lax.all_gather(own, "head", axis=0, tiled=True)
        piece = lax.dynamic_slice_in_dim(stride_rows[-summary:], place * share, share, 0)
        far_rows = lax.all_gather(piece, ("blk", "head"), axis=0, tiled=True)
        half = stride_rows.shape[0] // 2
        near_rows = [stride_rows, to_next(jnp.where(lower, stride_rows[half:], stride_rows[:half]))]

    query_weight, weight = split_weights(proj_weight)
    query = lax.dot_general(query_weight, own, (((1,), (1,)), ((), ())), preferred_element_type=jnp.float32)
    query = (query * HD**-0.5).astype(jnp.bfloat16)

    listed = lax.dynamic_slice_in_dim(pattern, place * blocks, blocks, 0)
    near = listed[:, :LSEL] - stride * SB
    swapped = jnp.logical_and(heads == 2, jnp.logical_and(jnp.logical_not(lower), near < SB))
    near = jnp.where(near < 0, near + SB + REACH, jnp.where(swapped, near ^ (SB // 2), near))
    far = listed[:, LSEL:]
    far = far // SB * SUMB + far % SB - (SB - SUMB)

    state = attend("attend_far", far, query, weight, [far_rows], [], False)
    mixed = attend("attend_near", near, query, weight, near_rows, state, True)
    out = jnp.dot(mixed, out_weight, preferred_element_type=jnp.float32).astype(jnp.bfloat16)
    return out.reshape(tokens.shape)


def solution(mesh):
    return jax.shard_map(
        on_device,
        mesh=mesh,
        in_specs=(P(("batch", "blk"), "head", None), P(), P(), P(("batch", "blk"), None)),
        out_specs=P(("batch", "blk"), "head", None),
        check_vma=False,
    )
```

```python
import functools

import jax
import jax.numpy as jnp
from jax import lax
from jax.experimental import pallas as pl
from jax.experimental.pallas import tpu as pltpu
from jax.sharding import PartitionSpec as P

D = 1024
H = 16
HD = 64
BLK = 128
REACH = 8
LSEL = 6
SUMB = 4
SB = 16
KSEL = 16
PAIRS = H // 2
LANES = 2 * HD
TOTAL_CAP = 2.0**100


def split_kernel(weight_ref, query_ref, key_ref, value_ref):
    both = weight_ref[...]
    first, second = both[:, : 3 * HD], both[:, 3 * HD :]

    def columns(which):
        lo = which * HD
        return jnp.concatenate([first[:, lo : lo + HD], second[:, lo : lo + HD]], axis=1)

    query_ref[...] = columns(0).T
    key_ref[...] = columns(1)
    value_ref[...] = columns(2).T


def split_weights(proj_weight):
    wide = jax.ShapeDtypeStruct((D, D), jnp.bfloat16)
    across = pl.BlockSpec((LANES, D), lambda p: (p, 0))
    down = pl.BlockSpec((D, LANES), lambda p: (0, p))
    return pl.pallas_call(
        split_kernel,
        grid=(PAIRS,),
        in_specs=[pl.BlockSpec((D, 3 * LANES), lambda p: (0, p))],
        out_specs=[across, down, across],
        out_shape=[wide, wide, wide],
        cost_estimate=pl.CostEstimate(flops=0, bytes_accessed=4 * D * 3 * D, transcendentals=0),
        name="split_weights",
    )(proj_weight)


def attend_kernel(first, last, blocks, count, together, long_sum, pieces, *refs):
    f32, bf16 = jnp.float32, jnp.bfloat16
    refs = list(refs)
    table_ref, query_ref = refs[:2]
    key_refs = refs[2 : 2 + pieces]
    value_refs = refs[2 + pieces : 2 + 2 * pieces]
    refs = refs[2 + 2 * pieces :]
    if not first:
        sum_in_ref, row_in_ref = refs[:2]
        refs = refs[2:]
    if last:
        out_ref = refs.pop(0)
    else:
        sum_out_ref, row_out_ref = refs[:2]
        refs = refs[2:]
    if pieces == 1:
        key_ref, value_ref = key_refs[0], value_refs[0]
    else:
        key_ref, value_ref = refs
        start = 0
        for key_piece, value_piece in zip(key_refs, value_refs):
            size = key_piece.shape[0]
            key_ref[start : start + size, :] = key_piece[...]
            value_ref[:, start : start + size] = value_piece[...]
            start += size

    row = lax.broadcasted_iota(jnp.int32, (LANES, BLK), 0)

    def at(index, size=BLK):
        return pl.ds(pl.multiple_of(index * size, size), size)

    def queries(index):
        own = query_ref[:, at(index)]
        zero = jnp.zeros_like(own)
        return jnp.concatenate([jnp.where(row < HD, own, zero), jnp.where(row < HD, zero, own)], axis=1)

    def places(index, which):
        return [pl.multiple_of(table_ref[index, which + n] * BLK, BLK) for n in range(2)]

    def score(index, which, query):
        keys = [key_ref[pl.ds(place, BLK), :] for place in places(index, which)]
        return jnp.dot(jnp.concatenate(keys, axis=0), query, preferred_element_type=f32)

    def values(index, which):
        return jnp.concatenate([value_ref[:, pl.ds(place, BLK)] for place in places(index, which)], axis=1)

    def gather(picked, raised):
        ones = jnp.ones((16, raised.shape[0]), bf16)
        return jnp.dot(jnp.concatenate([picked, ones], axis=0), raised, preferred_element_type=f32)

    def by_head(rows):
        return jnp.where(row < HD, rows[:, :BLK], rows[:, BLK:])

    def finish(index, shift, total, rescale=None):
        mine = jnp.concatenate([total[:HD, :BLK], total[HD:LANES, BLK:]], axis=0)
        count_all = total[LANES : LANES + 1]
        if not first:
            before = sum_in_ref[:, at(index)]
            count_before = row_in_ref[0, 1:2, at(index, 2 * BLK)]
            if rescale is not None:
                before = before * by_head(rescale)
                count_before = count_before * rescale
            mine = mine + before
            count_all = count_all + count_before
        if last:
            out_ref[at(index), :] = (mine * by_head(1.0 / count_all)).T.astype(bf16)
        else:
            sum_out_ref[:, at(index)] = mine
            row_out_ref[0, 0:1, at(index, 2 * BLK)] = shift
            row_out_ref[0, 1:2, at(index, 2 * BLK)] = count_all
        return count_all

    def one(index):
        query = queries(index)
        total = None
        picked, raised = [], []
        shift = None if first else row_in_ref[0, 0:1, at(index, 2 * BLK)]
        for which in range(0, count, 2):
            scores = score(index, which, query)
            if shift is None:
                shift = jnp.max(scores, axis=0, keepdims=True)
            picked.append(values(index, which))
            raised.append(jnp.exp(scores - shift).astype(bf16))
            if not long_sum:
                part = gather(picked[-1], raised[-1])
                total = part if total is None else total + part
        if long_sum:
            total = gather(jnp.concatenate(picked, axis=1), jnp.concatenate(raised, axis=0))
        return finish(index, shift, total)

    def whole_row(index):
        query = queries(index)
        shift = jnp.full((1, 2 * BLK), -jnp.inf, f32) if first else row_in_ref[0, 0:1, at(index, 2 * BLK)]
        old = shift

        def largest(n, shift):
            return jnp.maximum(shift, jnp.max(score(index, 2 * n, query), axis=0, keepdims=True))

        shift = lax.fori_loop(0, count // 2, largest, shift)

        def add(n, total):
            raised = jnp.exp(score(index, 2 * n, query) - shift).astype(bf16)
            return total + gather(values(index, 2 * n), raised)

        total = lax.fori_loop(0, count // 2, add, jnp.zeros((LANES + 16, 2 * BLK), f32))
        finish(index, shift, total, None if first else jnp.exp(old - shift))

    def body(number, peak):
        for n in range(together):
            peak = jnp.maximum(peak, one(number * together + n))
        return peak

    peak = lax.fori_loop(0, blocks // together, body, jnp.zeros((1, 2 * BLK), f32))

    @pl.when(jnp.logical_not(jnp.max(peak) <= TOTAL_CAP))
    def _():
        lax.fori_loop(0, blocks, lambda index, carry: (whole_row(index), carry)[1], 0)


def attend(name, table, query, keys, values, state, last, together, long_sum=False):
    f32, bf16 = jnp.float32, jnp.bfloat16
    rows = query.shape[1]
    blocks = rows // BLK
    count = table.shape[1]
    while blocks % together:
        together //= 2
    total_rows = sum(key.shape[0] for key in keys)
    across = lambda array: pl.BlockSpec((LANES, array.shape[1]), lambda p: (p, 0))
    down = lambda array: pl.BlockSpec((array.shape[0], LANES), lambda p: (0, p))
    per_row = pl.BlockSpec((1, 2, 2 * rows), lambda p: (p, 0, 0))
    in_specs = [pl.BlockSpec(memory_space=pltpu.SMEM), across(query)]
    in_specs += [down(key) for key in keys] + [across(value) for value in values]
    if state:
        in_specs += [across(query), per_row]
    if last:
        out_specs = pl.BlockSpec((rows, LANES), lambda p: (0, p))
        out_shape = jax.ShapeDtypeStruct((rows, D), bf16)
    else:
        out_specs = [across(query), per_row]
        out_shape = [jax.ShapeDtypeStruct((D, rows), f32), jax.ShapeDtypeStruct((PAIRS, 2, 2 * rows), f32)]
    scratch = [pltpu.VMEM((total_rows, LANES), bf16), pltpu.VMEM((LANES, total_rows), bf16)]
    scores = rows * count * BLK * H
    return pl.pallas_call(
        functools.partial(attend_kernel, not state, last, blocks, count, together, long_sum, len(keys)),
        grid=(PAIRS,),
        in_specs=in_specs,
        out_specs=out_specs,
        out_shape=out_shape,
        scratch_shapes=scratch if len(keys) > 1 else [],
        compiler_params=pltpu.CompilerParams(vmem_limit_bytes=48 * 2**20),
        cost_estimate=pl.CostEstimate(
            flops=24 * scores * HD, bytes_accessed=4 * total_rows * D + 10 * rows * D, transcendentals=scores
        ),
        name=name,
    )(table, query, *keys, *values, *state)


def project_rows(rows, weight):
    return jnp.dot(rows, weight, preferred_element_type=jnp.float32).astype(jnp.bfloat16)


def project_columns(weight, rows, scale=1.0):
    wide = lax.dot_general(weight, rows, (((1,), (1,)), ((), ())), preferred_element_type=jnp.float32)
    return (wide * scale).astype(jnp.bfloat16)


def on_device(tokens, proj_weight, out_weight, pattern):
    heads = lax.axis_size("head")
    strides = lax.axis_size("blk")
    place = lax.axis_index("head")
    stride = lax.axis_index("blk")
    own = tokens[0]
    blocks = own.shape[0] // BLK
    lower = place < heads // 2
    summary = SUMB * BLK
    share = summary // heads

    along = []
    for h in range(heads):
        for s in range(strides - 1):
            ends = (h * strides + s, h * strides + s + 1)
            along.append(ends if h < heads // 2 else ends[::-1])
    to_next = lambda rows: lax.ppermute(rows, ("head", "blk"), along)

    if heads == 2:
        swap = lambda rows: lax.ppermute(rows, "head", [(0, 1), (1, 0)])
        cut = own.shape[0] - summary
        piece = jnp.where(lower, swap(own[cut : cut + share]), own[cut + share :])
        far_rows = lax.all_gather(piece, ("blk", "head"), axis=0, tiled=True)
        later, far_rows = lax.optimization_barrier((own, far_rows))
        others = [swap(later[:cut]), swap(later[cut:])]
        near_rows = [own, *others, *[to_next(rows) for rows in others]]
    else:
        stride_rows = lax.all_gather(own, "head", axis=0, tiled=True)
        piece = lax.dynamic_slice_in_dim(stride_rows[-summary:], place * share, share, 0)
        far_rows = lax.all_gather(piece, ("blk", "head"), axis=0, tiled=True)
        half = stride_rows.shape[0] // 2
        near_rows = [stride_rows, to_next(jnp.where(lower, stride_rows[half:], stride_rows[:half]))]

    query_weight, key_weight, value_weight = split_weights(proj_weight)
    query = project_columns(query_weight, own, HD**-0.5)
    far_key = project_rows(far_rows, key_weight)
    far_value = project_columns(value_weight, far_rows)
    near_keys = [project_rows(rows, key_weight) for rows in near_rows]
    near_values = [project_columns(value_weight, rows) for rows in near_rows]

    listed = lax.dynamic_slice_in_dim(pattern, place * blocks, blocks, 0)
    near = listed[:, :LSEL] - stride * SB
    swapped = jnp.logical_and(heads == 2, jnp.logical_and(jnp.logical_not(lower), near < SB))
    near = jnp.where(near < 0, near + SB + REACH, jnp.where(swapped, near ^ (SB // 2), near))
    far = listed[:, LSEL:]
    far = far // SB * SUMB + far % SB - (SB - SUMB)

    state = attend("attend_far", far, query, [far_key], [far_value], [], False, 4)
    mixed = attend("attend_near", near, query, near_keys, near_values, state, True, 2, True)
    out = jnp.dot(mixed, out_weight, preferred_element_type=jnp.float32).astype(jnp.bfloat16)
    return out.reshape(tokens.shape)


def solution(mesh):
    return jax.shard_map(
        on_device,
        mesh=mesh,
        in_specs=(P(("batch", "blk"), "head", None), P(), P(), P(("batch", "blk"), None)),
        out_specs=P(("batch", "blk"), "head", None),
        check_vma=False,
    )
```

```python
import functools

import jax
import jax.numpy as jnp
from jax import lax
from jax.experimental import pallas as pl
from jax.experimental.pallas import tpu as pltpu
from jax.sharding import PartitionSpec as P

D = 1024
H = 16
HD = 64
BLK = 128
REACH = 8
LSEL = 6
SUMB = 4
SB = 16
KSEL = 16
PAIRS = H // 2
LANES = 2 * HD
TOTAL_CAP = 2.0**100


def split_kernel(weight_ref, query_ref, key_ref, value_ref):
    both = weight_ref[...]
    first, second = both[:, : 3 * HD], both[:, 3 * HD :]

    def columns(which):
        lo = which * HD
        return jnp.concatenate([first[:, lo : lo + HD], second[:, lo : lo + HD]], axis=1)

    query_ref[...] = columns(0).T
    key_ref[...] = columns(1)
    value_ref[...] = columns(2).T


def split_weights(proj_weight):
    wide = jax.ShapeDtypeStruct((D, D), jnp.bfloat16)
    across = pl.BlockSpec((LANES, D), lambda p: (p, 0))
    down = pl.BlockSpec((D, LANES), lambda p: (0, p))
    return pl.pallas_call(
        split_kernel,
        grid=(PAIRS,),
        in_specs=[pl.BlockSpec((D, 3 * LANES), lambda p: (0, p))],
        out_specs=[across, down, across],
        out_shape=[wide, wide, wide],
        cost_estimate=pl.CostEstimate(flops=0, bytes_accessed=4 * D * 3 * D, transcendentals=0),
        name="split_weights",
    )(proj_weight)


def attend_kernel(first, last, blocks, count, together, long_sum, pieces, *refs):
    f32, bf16 = jnp.float32, jnp.bfloat16
    refs = list(refs)
    table_ref, query_ref = refs[:2]
    key_refs = refs[2 : 2 + pieces]
    value_refs = refs[2 + pieces : 2 + 2 * pieces]
    refs = refs[2 + 2 * pieces :]
    if not first:
        sum_in_ref, row_in_ref = refs[:2]
        refs = refs[2:]
    if last:
        out_ref = refs.pop(0)
    else:
        sum_out_ref, row_out_ref = refs[:2]
        refs = refs[2:]
    if pieces == 1:
        key_ref, value_ref = key_refs[0], value_refs[0]
    else:
        key_ref, value_ref = refs
        start = 0
        for key_piece, value_piece in zip(key_refs, value_refs):
            size = key_piece.shape[0]
            key_ref[start : start + size, :] = key_piece[...]
            value_ref[:, start : start + size] = value_piece[...]
            start += size

    row = lax.broadcasted_iota(jnp.int32, (LANES, BLK), 0)

    def at(index, size=BLK):
        return pl.ds(pl.multiple_of(index * size, size), size)

    def queries(index):
        own = query_ref[:, at(index)]
        zero = jnp.zeros_like(own)
        return jnp.concatenate([jnp.where(row < HD, own, zero), jnp.where(row < HD, zero, own)], axis=1)

    def places(index, which):
        return [pl.multiple_of(table_ref[index, which + n] * BLK, BLK) for n in range(2)]

    def score(index, which, query):
        keys = [key_ref[pl.ds(place, BLK), :] for place in places(index, which)]
        return jnp.dot(jnp.concatenate(keys, axis=0), query, preferred_element_type=f32)

    def values(index, which):
        return jnp.concatenate([value_ref[:, pl.ds(place, BLK)] for place in places(index, which)], axis=1)

    def gather(picked, raised):
        ones = jnp.ones((16, raised.shape[0]), bf16)
        return jnp.dot(jnp.concatenate([picked, ones], axis=0), raised, preferred_element_type=f32)

    def by_head(rows):
        return jnp.where(row < HD, rows[:, :BLK], rows[:, BLK:])

    def finish(index, shift, total, rescale=None):
        mine = jnp.concatenate([total[:HD, :BLK], total[HD:LANES, BLK:]], axis=0)
        count_all = total[LANES : LANES + 1]
        if not first:
            before = sum_in_ref[:, at(index)]
            count_before = row_in_ref[0, 1:2, at(index, 2 * BLK)]
            if rescale is not None:
                before = before * by_head(rescale)
                count_before = count_before * rescale
            mine = mine + before
            count_all = count_all + count_before
        if last:
            out_ref[at(index), :] = (mine * by_head(1.0 / count_all)).T.astype(bf16)
        else:
            sum_out_ref[:, at(index)] = mine
            row_out_ref[0, 0:1, at(index, 2 * BLK)] = shift
            row_out_ref[0, 1:2, at(index, 2 * BLK)] = count_all
        return count_all

    def one(index):
        query = queries(index)
        total = None
        picked, raised = [], []
        shift = None if first else row_in_ref[0, 0:1, at(index, 2 * BLK)]
        for which in range(0, count, 2):
            scores = score(index, which, query)
            if shift is None:
                shift = jnp.max(scores, axis=0, keepdims=True)
            picked.append(values(index, which))
            raised.append(jnp.exp(scores - shift).astype(bf16))
            if not long_sum:
                part = gather(picked[-1], raised[-1])
                total = part if total is None else total + part
        if long_sum:
            total = gather(jnp.concatenate(picked, axis=1), jnp.concatenate(raised, axis=0))
        return finish(index, shift, total)

    def whole_row(index):
        query = queries(index)
        shift = jnp.full((1, 2 * BLK), -jnp.inf, f32) if first else row_in_ref[0, 0:1, at(index, 2 * BLK)]
        old = shift

        def largest(n, shift):
            return jnp.maximum(shift, jnp.max(score(index, 2 * n, query), axis=0, keepdims=True))

        shift = lax.fori_loop(0, count // 2, largest, shift)

        def add(n, total):
            raised = jnp.exp(score(index, 2 * n, query) - shift).astype(bf16)
            return total + gather(values(index, 2 * n), raised)

        total = lax.fori_loop(0, count // 2, add, jnp.zeros((LANES + 16, 2 * BLK), f32))
        finish(index, shift, total, None if first else jnp.exp(old - shift))

    def body(number, peak):
        for n in range(together):
            peak = jnp.maximum(peak, one(number * together + n))
        return peak

    peak = lax.fori_loop(0, blocks // together, body, jnp.zeros((1, 2 * BLK), f32))

    @pl.when(jnp.logical_not(jnp.max(peak) <= TOTAL_CAP))
    def _():
        lax.fori_loop(0, blocks, lambda index, carry: (whole_row(index), carry)[1], 0)


def attend(name, table, query, keys, values, state, last, together, long_sum=False):
    f32, bf16 = jnp.float32, jnp.bfloat16
    rows = query.shape[1]
    blocks = rows // BLK
    count = table.shape[1]
    while blocks % together:
        together //= 2
    total_rows = sum(key.shape[0] for key in keys)
    across = lambda array: pl.BlockSpec((LANES, array.shape[1]), lambda p: (p, 0))
    down = lambda array: pl.BlockSpec((array.shape[0], LANES), lambda p: (0, p))
    per_row = pl.BlockSpec((1, 2, 2 * rows), lambda p: (p, 0, 0))
    in_specs = [pl.BlockSpec(memory_space=pltpu.SMEM), across(query)]
    in_specs += [down(key) for key in keys] + [across(value) for value in values]
    if state:
        in_specs += [across(query), per_row]
    if last:
        out_specs = pl.BlockSpec((rows, LANES), lambda p: (0, p))
        out_shape = jax.ShapeDtypeStruct((rows, D), bf16)
    else:
        out_specs = [across(query), per_row]
        out_shape = [jax.ShapeDtypeStruct((D, rows), f32), jax.ShapeDtypeStruct((PAIRS, 2, 2 * rows), f32)]
    scratch = [pltpu.VMEM((total_rows, LANES), bf16), pltpu.VMEM((LANES, total_rows), bf16)]
    scores = rows * count * BLK * H
    return pl.pallas_call(
        functools.partial(attend_kernel, not state, last, blocks, count, together, long_sum, len(keys)),
        grid=(PAIRS,),
        in_specs=in_specs,
        out_specs=out_specs,
        out_shape=out_shape,
        scratch_shapes=scratch if len(keys) > 1 else [],
        compiler_params=pltpu.CompilerParams(vmem_limit_bytes=48 * 2**20),
        cost_estimate=pl.CostEstimate(
            flops=24 * scores * HD, bytes_accessed=4 * total_rows * D + 10 * rows * D, transcendentals=scores
        ),
        name=name,
    )(table, query, *keys, *values, *state)


def project_rows(rows, weight):
    return jnp.dot(rows, weight, preferred_element_type=jnp.float32).astype(jnp.bfloat16)


def project_columns(weight, rows, scale=1.0):
    wide = lax.dot_general(weight, rows, (((1,), (1,)), ((), ())), preferred_element_type=jnp.float32)
    return (wide * scale).astype(jnp.bfloat16)


def rows_by_axes(own, place, stride, strides):
    summary = SUMB * BLK
    half = summary // 2
    cut = own.shape[0] - summary
    chips = strides // 2
    low = place == 0
    swap = lambda rows: lax.ppermute(rows, "head", [(0, 1), (1, 0)])
    beside = lambda rows: lax.ppermute(rows, "blk", [(s, s ^ 1) for s in range(strides)])

    def along(rows, k):
        return lax.ppermute(rows, "blk", [(s, (s + 2 * k) % strides) for s in range(strides)])

    steps = []
    for s in range(strides - 1):
        steps += [(s, s + 1), (strides + s + 1, strides + s)]
    to_next = lambda rows: lax.ppermute(rows, ("head", "blk"), steps)

    other_mid = swap(own[cut : cut + half])
    carried = jnp.where(low, other_mid, own[cut + half :])
    slots = [along(carried, k) for k in range(1, chips)]
    other_low = swap(own[:cut])
    other_high = jnp.concatenate([other_mid, swap(own[cut + half :])], axis=0)
    edge_low = to_next(other_low)
    edge_high = to_next(other_high)
    slots = [jnp.concatenate([rows, swap(rows)], axis=0) for rows in slots]
    pieces = [own, other_low, other_high, edge_low, edge_high, beside(jnp.where(low, other_high, own[cut:]))]
    for rows in slots:
        pieces += [rows, beside(rows)]

    def position(block):
        of, inside = block // SB, block % SB
        rel = block - stride * SB
        mine = inside % 8 + jnp.where(inside // 8 == place, 0, 8)
        edge = jnp.where(rel < 0, rel + SB + 8, rel)
        order = inside - (SB - SUMB)
        k = (stride // 2 - of // 2) % chips
        turned = (order // 2 ^ place) * 2 + order % 2
        far = 28 + (k - 1) * 8 + jnp.where(of % 2 == stride % 2, 0, 4) + turned
        far = jnp.where(k == 0, 24 + order, far)
        return jnp.where(of == stride, mine, edge), jnp.where(of == stride, mine, far)

    return pieces, position


def rows_by_gather(own, place, stride, strides, heads):
    summary = SUMB * BLK
    share = summary // heads
    lower = place < heads // 2
    stride_rows = lax.all_gather(own, "head", axis=0, tiled=True)
    piece = lax.dynamic_slice_in_dim(stride_rows[-summary:], place * share, share, 0)
    far_rows = lax.all_gather(piece, ("blk", "head"), axis=0, tiled=True)
    half = stride_rows.shape[0] // 2
    steps = []
    for h in range(heads):
        for s in range(strides - 1):
            ends = (h * strides + s, h * strides + s + 1)
            steps.append(ends if h < heads // 2 else ends[::-1])
    edge = lax.ppermute(jnp.where(lower, stride_rows[half:], stride_rows[:half]), ("head", "blk"), steps)

    def position(block):
        rel = block - stride * SB
        near = jnp.where(rel < 0, rel + SB + REACH, rel)
        return near, SB + REACH + block // SB * SUMB + block % SB - (SB - SUMB)

    return [stride_rows, edge, far_rows], position


def on_device(tokens, proj_weight, out_weight, pattern):
    heads = lax.axis_size("head")
    strides = lax.axis_size("blk")
    place = lax.axis_index("head")
    stride = lax.axis_index("blk")
    own = tokens[0]
    blocks = own.shape[0] // BLK

    if heads == 2:
        pieces, position = rows_by_axes(own, place, stride, strides)
    else:
        pieces, position = rows_by_gather(own, place, stride, strides, heads)
    listed = lax.dynamic_slice_in_dim(pattern, place * blocks, blocks, 0)
    near, far = position(listed)
    column = lax.broadcasted_iota(jnp.int32, listed.shape, 1)
    table = jnp.where(column < LSEL, near, far)

    query_weight, key_weight, value_weight = split_weights(proj_weight)
    query = project_columns(query_weight, own, HD**-0.5)
    keys = [project_rows(rows, key_weight) for rows in pieces]
    values = [project_columns(value_weight, rows) for rows in pieces]
    mixed = attend("attend", table, query, keys, values, [], True, 2)
    out = jnp.dot(mixed, out_weight, preferred_element_type=jnp.float32).astype(jnp.bfloat16)
    return out.reshape(tokens.shape)


def solution(mesh):
    return jax.shard_map(
        on_device,
        mesh=mesh,
        in_specs=(P(("batch", "blk"), "head", None), P(), P(), P(("batch", "blk"), None)),
        out_specs=P(("batch", "blk"), "head", None),
        check_vma=False,
    )
```

```python
import functools

import jax
import jax.numpy as jnp
from jax import lax
from jax.experimental import pallas as pl
from jax.experimental.pallas import tpu as pltpu
from jax.sharding import PartitionSpec as P

D = 1024
H = 16
HD = 64
BLK = 128
REACH = 8
LSEL = 6
SUMB = 4
SB = 16
KSEL = 16
PAIRS = H // 2
LANES = 2 * HD
TOTAL_CAP = 2.0**100


def split_kernel(weight_ref, query_ref, key_ref, value_ref):
    both = weight_ref[...]
    first, second = both[:, : 3 * HD], both[:, 3 * HD :]

    def columns(which):
        lo = which * HD
        return jnp.concatenate([first[:, lo : lo + HD], second[:, lo : lo + HD]], axis=1)

    query_ref[...] = columns(0).T
    key_ref[...] = columns(1)
    value_ref[...] = columns(2).T


def split_weights(proj_weight):
    wide = jax.ShapeDtypeStruct((D, D), jnp.bfloat16)
    across = pl.BlockSpec((LANES, D), lambda p: (p, 0))
    down = pl.BlockSpec((D, LANES), lambda p: (0, p))
    return pl.pallas_call(
        split_kernel,
        grid=(PAIRS,),
        in_specs=[pl.BlockSpec((D, 3 * LANES), lambda p: (0, p))],
        out_specs=[across, down, across],
        out_shape=[wide, wide, wide],
        cost_estimate=pl.CostEstimate(flops=0, bytes_accessed=4 * D * 3 * D, transcendentals=0),
        name="split_weights",
    )(proj_weight)


def attend_kernel(first, last, blocks, count, together, long_sum, pieces, *refs):
    f32, bf16 = jnp.float32, jnp.bfloat16
    refs = list(refs)
    table_ref, query_ref = refs[:2]
    key_refs = refs[2 : 2 + pieces]
    value_refs = refs[2 + pieces : 2 + 2 * pieces]
    refs = refs[2 + 2 * pieces :]
    if not first:
        sum_in_ref, row_in_ref = refs[:2]
        refs = refs[2:]
    if last:
        out_ref = refs.pop(0)
    else:
        sum_out_ref, row_out_ref = refs[:2]
        refs = refs[2:]
    if pieces == 1:
        key_ref, value_ref = key_refs[0], value_refs[0]
    else:
        key_ref, value_ref = refs
        start = 0
        for key_piece, value_piece in zip(key_refs, value_refs):
            size = key_piece.shape[0]
            key_ref[start : start + size, :] = key_piece[...]
            value_ref[:, start : start + size] = value_piece[...]
            start += size

    row = lax.broadcasted_iota(jnp.int32, (LANES, BLK), 0)

    def at(index, size=BLK):
        return pl.ds(pl.multiple_of(index * size, size), size)

    def queries(index):
        own = query_ref[:, at(index)]
        zero = jnp.zeros_like(own)
        return jnp.concatenate([jnp.where(row < HD, own, zero), jnp.where(row < HD, zero, own)], axis=1)

    def places(index, which):
        return [pl.multiple_of(table_ref[index, which + n] * BLK, BLK) for n in range(2)]

    def score(index, which, query):
        keys = [key_ref[pl.ds(place, BLK), :] for place in places(index, which)]
        return jnp.dot(jnp.concatenate(keys, axis=0), query, preferred_element_type=f32)

    def values(index, which):
        return jnp.concatenate([value_ref[:, pl.ds(place, BLK)] for place in places(index, which)], axis=1)

    def gather(picked, raised):
        ones = jnp.ones((16, raised.shape[0]), bf16)
        parts = []
        for n in range(2):
            rows = jnp.concatenate([picked[n * HD : (n + 1) * HD], ones], axis=0)
            parts.append(jnp.dot(rows, raised[:, n * BLK : (n + 1) * BLK], preferred_element_type=f32))
        return parts

    def by_head(rows):
        return jnp.where(row < HD, rows[:, :BLK], rows[:, BLK:])

    def finish(index, shift, total, rescale=None):
        mine = jnp.concatenate([part[:HD] for part in total], axis=0)
        count_all = jnp.concatenate([part[HD : HD + 1] for part in total], axis=1)
        if not first:
            before = sum_in_ref[:, at(index)]
            count_before = row_in_ref[0, 1:2, at(index, 2 * BLK)]
            if rescale is not None:
                before = before * by_head(rescale)
                count_before = count_before * rescale
            mine = mine + before
            count_all = count_all + count_before
        if last:
            out_ref[at(index), :] = (mine * by_head(1.0 / count_all)).T.astype(bf16)
        else:
            sum_out_ref[:, at(index)] = mine
            row_out_ref[0, 0:1, at(index, 2 * BLK)] = shift
            row_out_ref[0, 1:2, at(index, 2 * BLK)] = count_all
        return count_all

    def one(index):
        query = queries(index)
        total = None
        picked, raised = [], []
        shift = None if first else row_in_ref[0, 0:1, at(index, 2 * BLK)]
        for which in range(0, count, 2):
            scores = score(index, which, query)
            if shift is None:
                shift = jnp.max(scores, axis=0, keepdims=True)
            picked.append(values(index, which))
            raised.append(jnp.exp(scores - shift).astype(bf16))
            if not long_sum:
                part = gather(picked[-1], raised[-1])
                total = part if total is None else [old + new for old, new in zip(total, part)]
        if long_sum:
            total = gather(jnp.concatenate(picked, axis=1), jnp.concatenate(raised, axis=0))
        return finish(index, shift, total)

    def whole_row(index):
        query = queries(index)
        shift = jnp.full((1, 2 * BLK), -jnp.inf, f32) if first else row_in_ref[0, 0:1, at(index, 2 * BLK)]
        old = shift

        def largest(n, shift):
            return jnp.maximum(shift, jnp.max(score(index, 2 * n, query), axis=0, keepdims=True))

        shift = lax.fori_loop(0, count // 2, largest, shift)

        def add(n, total):
            raised = jnp.exp(score(index, 2 * n, query) - shift).astype(bf16)
            return [old + new for old, new in zip(total, gather(values(index, 2 * n), raised))]

        total = lax.fori_loop(0, count // 2, add, [jnp.zeros((HD + 16, BLK), f32)] * 2)
        finish(index, shift, total, None if first else jnp.exp(old - shift))

    def body(number, peak):
        for n in range(together):
            peak = jnp.maximum(peak, one(number * together + n))
        return peak

    peak = lax.fori_loop(0, blocks // together, body, jnp.zeros((1, 2 * BLK), f32))

    @pl.when(jnp.logical_not(jnp.max(peak) <= TOTAL_CAP))
    def _():
        lax.fori_loop(0, blocks, lambda index, carry: (whole_row(index), carry)[1], 0)


def attend(name, table, query, keys, values, state, last, together, long_sum=False):
    f32, bf16 = jnp.float32, jnp.bfloat16
    rows = query.shape[1]
    blocks = rows // BLK
    count = table.shape[1]
    while blocks % together:
        together //= 2
    total_rows = sum(key.shape[0] for key in keys)
    across = lambda array: pl.BlockSpec((LANES, array.shape[1]), lambda p: (p, 0))
    down = lambda array: pl.BlockSpec((array.shape[0], LANES), lambda p: (0, p))
    per_row = pl.BlockSpec((1, 2, 2 * rows), lambda p: (p, 0, 0))
    in_specs = [pl.BlockSpec(memory_space=pltpu.SMEM), across(query)]
    in_specs += [down(key) for key in keys] + [across(value) for value in values]
    if state:
        in_specs += [across(query), per_row]
    if last:
        out_specs = pl.BlockSpec((rows, LANES), lambda p: (0, p))
        out_shape = jax.ShapeDtypeStruct((rows, D), bf16)
    else:
        out_specs = [across(query), per_row]
        out_shape = [jax.ShapeDtypeStruct((D, rows), f32), jax.ShapeDtypeStruct((PAIRS, 2, 2 * rows), f32)]
    scratch = [pltpu.VMEM((total_rows, LANES), bf16), pltpu.VMEM((LANES, total_rows), bf16)]
    scores = rows * count * BLK * H
    return pl.pallas_call(
        functools.partial(attend_kernel, not state, last, blocks, count, together, long_sum, len(keys)),
        grid=(PAIRS,),
        in_specs=in_specs,
        out_specs=out_specs,
        out_shape=out_shape,
        scratch_shapes=scratch if len(keys) > 1 else [],
        compiler_params=pltpu.CompilerParams(vmem_limit_bytes=18 * 2**20),
        cost_estimate=pl.CostEstimate(
            flops=24 * scores * HD, bytes_accessed=4 * total_rows * D + 10 * rows * D, transcendentals=scores
        ),
        name=name,
    )(table, query, *keys, *values, *state)


def project_rows(rows, weight):
    return jnp.dot(rows, weight, preferred_element_type=jnp.float32).astype(jnp.bfloat16)


def project_columns(weight, rows, scale=1.0):
    wide = lax.dot_general(weight, rows, (((1,), (1,)), ((), ())), preferred_element_type=jnp.float32)
    return (wide * scale).astype(jnp.bfloat16)


def rows_by_axes(own, weights, place, stride, strides):
    summary = SUMB * BLK
    half = summary // 2
    cut = own.shape[0] - summary
    chips = strides // 2
    low = place == 0
    swap = lambda rows: lax.ppermute(rows, "head", [(0, 1), (1, 0)])
    beside = lambda rows: lax.ppermute(rows, "blk", [(s, s ^ 1) for s in range(strides)])

    def along(rows, k):
        return lax.ppermute(rows, "blk", [(s, (s + 2 * k) % strides) for s in range(strides)])

    steps = []
    for s in range(strides - 1):
        steps += [(s, s + 1), (strides + s + 1, strides + s)]
    to_next = lambda rows: lax.ppermute(rows, ("head", "blk"), steps)

    other_mid = swap(own[cut : cut + half])
    other_mid, own, weights = lax.optimization_barrier((other_mid, own, weights))
    carried = jnp.where(low, other_mid, own[cut + half :])
    other_low, other_top = swap(own[:cut]), swap(own[cut + half :])
    slots = [None] * (chips - 1)
    for k in sorted(range(1, chips), key=lambda k: min(k, chips - k)):
        slot = along(carried, k)
        slot, carried = lax.optimization_barrier((slot, carried))
        slots[k - 1] = jnp.concatenate([slot, swap(slot)], axis=0)
    other_high = jnp.concatenate([other_mid, other_top], axis=0)
    edge_low = to_next(other_low)
    edge_high = to_next(other_high)
    pieces = [own, other_low, other_high, edge_low, edge_high, beside(jnp.where(low, other_high, own[cut:]))]
    for rows in slots:
        pieces += [rows, beside(rows)]

    def position(block):
        of, inside = block // SB, block % SB
        rel = block - stride * SB
        mine = inside % 8 + jnp.where(inside // 8 == place, 0, 8)
        edge = jnp.where(rel < 0, rel + SB + 8, rel)
        order = inside - (SB - SUMB)
        k = (stride // 2 - of // 2) % chips
        turned = (order // 2 ^ place) * 2 + order % 2
        far = 28 + (k - 1) * 8 + jnp.where(of % 2 == stride % 2, 0, 4) + turned
        far = jnp.where(k == 0, 24 + order, far)
        return jnp.where(of == stride, mine, edge), jnp.where(of == stride, mine, far)

    return pieces, weights, position


def rows_by_gather(own, place, stride, strides, heads):
    summary = SUMB * BLK
    share = summary // heads
    lower = place < heads // 2
    stride_rows = lax.all_gather(own, "head", axis=0, tiled=True)
    piece = lax.dynamic_slice_in_dim(stride_rows[-summary:], place * share, share, 0)
    far_rows = lax.all_gather(piece, ("blk", "head"), axis=0, tiled=True)
    half = stride_rows.shape[0] // 2
    steps = []
    for h in range(heads):
        for s in range(strides - 1):
            ends = (h * strides + s, h * strides + s + 1)
            steps.append(ends if h < heads // 2 else ends[::-1])
    edge = lax.ppermute(jnp.where(lower, stride_rows[half:], stride_rows[:half]), ("head", "blk"), steps)

    def position(block):
        rel = block - stride * SB
        near = jnp.where(rel < 0, rel + SB + REACH, rel)
        return near, SB + REACH + block // SB * SUMB + block % SB - (SB - SUMB)

    return [stride_rows, edge, far_rows], position


def on_device(tokens, proj_weight, out_weight, pattern):
    heads = lax.axis_size("head")
    strides = lax.axis_size("blk")
    place = lax.axis_index("head")
    stride = lax.axis_index("blk")
    own = tokens[0]
    blocks = own.shape[0] // BLK
    weights = split_weights(proj_weight)

    if heads == 2:
        pieces, weights, position = rows_by_axes(own, weights, place, stride, strides)
        own = pieces[0]
    else:
        pieces, position = rows_by_gather(own, place, stride, strides, heads)
    listed = lax.dynamic_slice_in_dim(pattern, place * blocks, blocks, 0)
    near, far = position(listed)
    column = lax.broadcasted_iota(jnp.int32, listed.shape, 1)
    table = jnp.where(column < LSEL, near, far)

    query_weight, key_weight, value_weight = weights
    query = project_columns(query_weight, own, HD**-0.5)
    keys = [project_rows(rows, key_weight) for rows in pieces]
    values = [project_columns(value_weight, rows) for rows in pieces]
    mixed = attend("attend", table, query, keys, values, [], True, 2)
    out = jnp.dot(mixed, out_weight, preferred_element_type=jnp.float32).astype(jnp.bfloat16)
    return out.reshape(tokens.shape)


def solution(mesh):
    return jax.shard_map(
        on_device,
        mesh=mesh,
        in_specs=(P(("batch", "blk"), "head", None), P(), P(), P(("batch", "blk"), None)),
        out_specs=P(("batch", "blk"), "head", None),
        check_vma=False,
    )
```

```python
import functools

import jax
import jax.numpy as jnp
from jax import lax
from jax.experimental import pallas as pl
from jax.experimental.pallas import tpu as pltpu
from jax.sharding import PartitionSpec as P

D = 1024
H = 16
HD = 64
BLK = 128
REACH = 8
LSEL = 6
SUMB = 4
SB = 16
KSEL = 16
PAIRS = H // 2
LANES = 2 * HD
TOTAL_CAP = 2.0**100


def split_kernel(weight_ref, query_ref, key_ref, value_ref):
    both = weight_ref[...]
    first, second = both[:, : 3 * HD], both[:, 3 * HD :]

    def columns(which):
        lo = which * HD
        return jnp.concatenate([first[:, lo : lo + HD], second[:, lo : lo + HD]], axis=1)

    query_ref[...] = columns(0).T
    key_ref[...] = columns(1)
    value_ref[...] = columns(2).T


def split_weights(proj_weight):
    wide = jax.ShapeDtypeStruct((D, D), jnp.bfloat16)
    across = pl.BlockSpec((LANES, D), lambda p: (p, 0))
    down = pl.BlockSpec((D, LANES), lambda p: (0, p))
    return pl.pallas_call(
        split_kernel,
        grid=(PAIRS,),
        in_specs=[pl.BlockSpec((D, 3 * LANES), lambda p: (0, p))],
        out_specs=[across, down, across],
        out_shape=[wide, wide, wide],
        cost_estimate=pl.CostEstimate(flops=0, bytes_accessed=4 * D * 3 * D, transcendentals=0),
        name="split_weights",
    )(proj_weight)


def attend_kernel(first, last, blocks, count, together, chunk, pieces, *refs):
    f32, bf16 = jnp.float32, jnp.bfloat16
    refs = list(refs)
    table_ref, query_ref = refs[:2]
    key_refs = refs[2 : 2 + pieces]
    value_refs = refs[2 + pieces : 2 + 2 * pieces]
    refs = refs[2 + 2 * pieces :]
    if not first:
        sum_in_ref, row_in_ref = refs[:2]
        refs = refs[2:]
    if last:
        out_ref = refs.pop(0)
    else:
        sum_out_ref, row_out_ref = refs[:2]
        refs = refs[2:]
    if pieces == 1:
        key_ref, value_ref = key_refs[0], value_refs[0]
    else:
        key_ref, value_ref = refs
        start = 0
        for key_piece, value_piece in zip(key_refs, value_refs):
            size = key_piece.shape[0]
            key_ref[start : start + size, :] = key_piece[...]
            value_ref[:, start : start + size] = value_piece[...]
            start += size

    row = lax.broadcasted_iota(jnp.int32, (LANES, BLK), 0)

    def at(index, size=BLK):
        return pl.ds(pl.multiple_of(index * size, size), size)

    def queries(index):
        own = query_ref[:, at(index)]
        zero = jnp.zeros_like(own)
        return jnp.concatenate([jnp.where(row < HD, own, zero), jnp.where(row < HD, zero, own)], axis=1)

    def places(index, which):
        return [pl.multiple_of(table_ref[index, which + n] * BLK, BLK) for n in range(chunk)]

    def score(index, which, query):
        keys = [key_ref[pl.ds(place, BLK), :] for place in places(index, which)]
        return jnp.dot(jnp.concatenate(keys, axis=0), query, preferred_element_type=f32)

    def values(index, which):
        return jnp.concatenate([value_ref[:, pl.ds(place, BLK)] for place in places(index, which)], axis=1)

    def gather(picked, raised):
        ones = jnp.ones((16, raised.shape[0]), bf16)
        return jnp.dot(jnp.concatenate([picked, ones], axis=0), raised, preferred_element_type=f32)

    def by_head(rows):
        return jnp.where(row < HD, rows[:, :BLK], rows[:, BLK:])

    def finish(index, shift, total, rescale=None):
        mine = jnp.concatenate([total[:HD, :BLK], total[HD:LANES, BLK:]], axis=0)
        count_all = total[LANES : LANES + 1]
        if not first:
            before = sum_in_ref[:, at(index)]
            count_before = row_in_ref[0, 1:2, at(index, 2 * BLK)]
            if rescale is not None:
                before = before * by_head(rescale)
                count_before = count_before * rescale
            mine = mine + before
            count_all = count_all + count_before
        if last:
            out_ref[at(index), :] = (mine * by_head(1.0 / count_all)).T.astype(bf16)
        else:
            sum_out_ref[:, at(index)] = mine
            row_out_ref[0, 0:1, at(index, 2 * BLK)] = shift
            row_out_ref[0, 1:2, at(index, 2 * BLK)] = count_all
        return count_all

    def one(index):
        query = queries(index)
        total = None
        shift = None if first else row_in_ref[0, 0:1, at(index, 2 * BLK)]
        for which in range(0, count, chunk):
            scores = score(index, which, query)
            if shift is None:
                shift = jnp.max(scores, axis=0, keepdims=True)
            part = gather(values(index, which), jnp.exp(scores - shift).astype(bf16))
            total = part if total is None else total + part
        return finish(index, shift, total)

    def whole_row(index):
        query = queries(index)
        shift = jnp.full((1, 2 * BLK), -jnp.inf, f32) if first else row_in_ref[0, 0:1, at(index, 2 * BLK)]
        old = shift

        def largest(n, shift):
            return jnp.maximum(shift, jnp.max(score(index, chunk * n, query), axis=0, keepdims=True))

        shift = lax.fori_loop(0, count // chunk, largest, shift)

        def add(n, total):
            raised = jnp.exp(score(index, chunk * n, query) - shift).astype(bf16)
            return total + gather(values(index, chunk * n), raised)

        total = lax.fori_loop(0, count // chunk, add, jnp.zeros((LANES + 16, 2 * BLK), f32))
        finish(index, shift, total, None if first else jnp.exp(old - shift))

    def body(number, peak):
        for n in range(together):
            peak = jnp.maximum(peak, one(number * together + n))
        return peak

    peak = lax.fori_loop(0, blocks // together, body, jnp.zeros((1, 2 * BLK), f32))

    @pl.when(jnp.logical_not(jnp.max(peak) <= TOTAL_CAP))
    def _():
        lax.fori_loop(0, blocks, lambda index, carry: (whole_row(index), carry)[1], 0)


def attend(name, table, query, keys, values, state, last, together, chunk):
    f32, bf16 = jnp.float32, jnp.bfloat16
    rows = query.shape[1]
    blocks = rows // BLK
    count = table.shape[1]
    while blocks % together:
        together //= 2
    total_rows = sum(key.shape[0] for key in keys)
    across = lambda array: pl.BlockSpec((LANES, array.shape[1]), lambda p: (p, 0))
    down = lambda array: pl.BlockSpec((array.shape[0], LANES), lambda p: (0, p))
    per_row = pl.BlockSpec((1, 2, 2 * rows), lambda p: (p, 0, 0))
    in_specs = [pl.BlockSpec(memory_space=pltpu.SMEM), across(query)]
    in_specs += [down(key) for key in keys] + [across(value) for value in values]
    if state:
        in_specs += [across(query), per_row]
    if last:
        out_specs = pl.BlockSpec((rows, LANES), lambda p: (0, p))
        out_shape = jax.ShapeDtypeStruct((rows, D), bf16)
    else:
        out_specs = [across(query), per_row]
        out_shape = [jax.ShapeDtypeStruct((D, rows), f32), jax.ShapeDtypeStruct((PAIRS, 2, 2 * rows), f32)]
    scratch = [pltpu.VMEM((total_rows, LANES), bf16), pltpu.VMEM((LANES, total_rows), bf16)]
    scores = rows * count * BLK * H
    return pl.pallas_call(
        functools.partial(attend_kernel, not state, last, blocks, count, together, chunk, len(keys)),
        grid=(PAIRS,),
        in_specs=in_specs,
        out_specs=out_specs,
        out_shape=out_shape,
        scratch_shapes=scratch if len(keys) > 1 else [],
        compiler_params=pltpu.CompilerParams(vmem_limit_bytes=18 * 2**20),
        cost_estimate=pl.CostEstimate(
            flops=24 * scores * HD, bytes_accessed=4 * total_rows * D + 10 * rows * D, transcendentals=scores
        ),
        name=name,
    )(table, query, *keys, *values, *state)


def project_rows(rows, weight):
    return jnp.dot(rows, weight, preferred_element_type=jnp.float32).astype(jnp.bfloat16)


def project_columns(weight, rows, scale=1.0):
    wide = lax.dot_general(weight, rows, (((1,), (1,)), ((), ())), preferred_element_type=jnp.float32)
    return (wide * scale).astype(jnp.bfloat16)


def rows_by_axes(own, weights, place, stride, strides):
    summary = SUMB * BLK
    half = summary // 2
    cut = own.shape[0] - summary
    chips = strides // 2
    low = place == 0
    swap = lambda rows: lax.ppermute(rows, "head", [(0, 1), (1, 0)])
    beside = lambda rows: lax.ppermute(rows, "blk", [(s, s ^ 1) for s in range(strides)])

    def along(rows, k):
        return lax.ppermute(rows, "blk", [(s, (s + 2 * k) % strides) for s in range(strides)])

    steps = []
    for s in range(strides - 1):
        steps += [(s, s + 1), (strides + s + 1, strides + s)]
    to_next = lambda rows: lax.ppermute(rows, ("head", "blk"), steps)

    other_mid = swap(own[cut : cut + half])
    other_mid, own, weights = lax.optimization_barrier((other_mid, own, weights))
    carried = jnp.where(low, other_mid, own[cut + half :])
    other_low, other_top = swap(own[:cut]), swap(own[cut + half :])
    slots = [None] * chips
    slots[2:-1] = [along(carried, k) for k in range(2, chips - 1)]
    slots[1] = along(carried, 1)
    slots[1], carried = lax.optimization_barrier((slots[1], carried))
    slots[-1] = along(carried, chips - 1)
    slots = [jnp.concatenate([rows, swap(rows)], axis=0) for rows in slots[1:]]
    other_high = jnp.concatenate([other_mid, other_top], axis=0)
    edge_low = to_next(other_low)
    edge_high = to_next(other_high)
    pieces = [own, other_low, other_high, edge_low, edge_high, beside(jnp.where(low, other_high, own[cut:]))]
    for rows in slots:
        pieces += [rows, beside(rows)]

    def position(block):
        of, inside = block // SB, block % SB
        rel = block - stride * SB
        mine = inside % 8 + jnp.where(inside // 8 == place, 0, 8)
        edge = jnp.where(rel < 0, rel + SB + 8, rel)
        order = inside - (SB - SUMB)
        k = (stride // 2 - of // 2) % chips
        turned = (order // 2 ^ place) * 2 + order % 2
        far = 28 + (k - 1) * 8 + jnp.where(of % 2 == stride % 2, 0, 4) + turned
        far = jnp.where(k == 0, 24 + order, far)
        return jnp.where(of == stride, mine, edge), jnp.where(of == stride, mine, far)

    return pieces, weights, position


def rows_by_gather(own, place, stride, strides, heads):
    summary = SUMB * BLK
    share = summary // heads
    lower = place < heads // 2
    stride_rows = lax.all_gather(own, "head", axis=0, tiled=True)
    piece = lax.dynamic_slice_in_dim(stride_rows[-summary:], place * share, share, 0)
    far_rows = lax.all_gather(piece, ("blk", "head"), axis=0, tiled=True)
    half = stride_rows.shape[0] // 2
    steps = []
    for h in range(heads):
        for s in range(strides - 1):
            ends = (h * strides + s, h * strides + s + 1)
            steps.append(ends if h < heads // 2 else ends[::-1])
    edge = lax.ppermute(jnp.where(lower, stride_rows[half:], stride_rows[:half]), ("head", "blk"), steps)

    def position(block):
        rel = block - stride * SB
        near = jnp.where(rel < 0, rel + SB + REACH, rel)
        return near, SB + REACH + block // SB * SUMB + block % SB - (SB - SUMB)

    return [stride_rows, edge, far_rows], position


def on_device(tokens, proj_weight, out_weight, pattern):
    heads = lax.axis_size("head")
    strides = lax.axis_size("blk")
    place = lax.axis_index("head")
    stride = lax.axis_index("blk")
    own = tokens[0]
    blocks = own.shape[0] // BLK
    weights = split_weights(proj_weight)

    if heads == 2:
        pieces, weights, position = rows_by_axes(own, weights, place, stride, strides)
        own = pieces[0]
    else:
        pieces, position = rows_by_gather(own, place, stride, strides, heads)
    listed = lax.dynamic_slice_in_dim(pattern, place * blocks, blocks, 0)
    near, far = position(listed)
    column = lax.broadcasted_iota(jnp.int32, listed.shape, 1)
    table = jnp.where(column < LSEL, near, far)

    query_weight, key_weight, value_weight = weights
    query = project_columns(query_weight, own, HD**-0.5)
    keys = [project_rows(rows, key_weight) for rows in pieces]
    values = [project_columns(value_weight, rows) for rows in pieces]
    mixed = attend("attend", table, query, keys, values, [], True, 2, 4)
    out = jnp.dot(mixed, out_weight, preferred_element_type=jnp.float32).astype(jnp.bfloat16)
    return out.reshape(tokens.shape)


def solution(mesh):
    return jax.shard_map(
        on_device,
        mesh=mesh,
        in_specs=(P(("batch", "blk"), "head", None), P(), P(), P(("batch", "blk"), None)),
        out_specs=P(("batch", "blk"), "head", None),
        check_vma=False,
    )
```

```python
import functools

import jax
import jax.numpy as jnp
from jax import lax
from jax.experimental import pallas as pl
from jax.experimental.pallas import tpu as pltpu
from jax.sharding import PartitionSpec as P

D = 1024
H = 16
HD = 64
BLK = 128
REACH = 8
LSEL = 6
SUMB = 4
SB = 16
KSEL = 16
PAIRS = H // 2
LANES = 2 * HD
TOTAL_CAP = 2.0**100


def split_kernel(weight_ref, query_ref, key_ref, value_ref):
    both = weight_ref[...]
    first, second = both[:, : 3 * HD], both[:, 3 * HD :]

    def columns(which):
        lo = which * HD
        return jnp.concatenate([first[:, lo : lo + HD], second[:, lo : lo + HD]], axis=1)

    query_ref[...] = columns(0).T
    key_ref[...] = columns(1)
    value_ref[...] = columns(2).T


def split_weights(proj_weight):
    wide = jax.ShapeDtypeStruct((D, D), jnp.bfloat16)
    across = pl.BlockSpec((LANES, D), lambda p: (p, 0))
    down = pl.BlockSpec((D, LANES), lambda p: (0, p))
    return pl.pallas_call(
        split_kernel,
        grid=(PAIRS,),
        in_specs=[pl.BlockSpec((D, 3 * LANES), lambda p: (0, p))],
        out_specs=[across, down, across],
        out_shape=[wide, wide, wide],
        cost_estimate=pl.CostEstimate(flops=0, bytes_accessed=4 * D * 3 * D, transcendentals=0),
        name="split_weights",
    )(proj_weight)


def attend_kernel(first, last, blocks, count, together, chunk, pieces, *refs):
    f32, bf16 = jnp.float32, jnp.bfloat16
    refs = list(refs)
    table_ref, query_ref = refs[:2]
    key_refs = refs[2 : 2 + pieces]
    value_refs = refs[2 + pieces : 2 + 2 * pieces]
    refs = refs[2 + 2 * pieces :]
    if not first:
        sum_in_ref, row_in_ref = refs[:2]
        refs = refs[2:]
    if last:
        out_ref = refs.pop(0)
    else:
        sum_out_ref, row_out_ref = refs[:2]
        refs = refs[2:]
    if pieces == 1:
        key_ref, value_ref = key_refs[0], value_refs[0]
    else:
        key_ref, value_ref = refs
        start = 0
        for key_piece, value_piece in zip(key_refs, value_refs):
            size = key_piece.shape[0]
            key_ref[start : start + size, :] = key_piece[...]
            value_ref[:, start : start + size] = value_piece[...]
            start += size

    row = lax.broadcasted_iota(jnp.int32, (LANES, BLK), 0)

    def at(index, size=BLK):
        return pl.ds(pl.multiple_of(index * size, size), size)

    def queries(index):
        own = query_ref[:, at(index)]
        zero = jnp.zeros_like(own)
        return jnp.concatenate([jnp.where(row < HD, own, zero), jnp.where(row < HD, zero, own)], axis=1)

    def places(index, which):
        return [pl.multiple_of(table_ref[index, which + n] * BLK, BLK) for n in range(chunk)]

    def score(index, which, query):
        keys = [key_ref[pl.ds(place, BLK), :] for place in places(index, which)]
        return jnp.dot(jnp.concatenate(keys, axis=0), query, preferred_element_type=f32)

    def values(index, which):
        return jnp.concatenate([value_ref[:, pl.ds(place, BLK)] for place in places(index, which)], axis=1)

    def gather(picked, raised):
        ones = jnp.ones((16, raised.shape[0]), bf16)
        return jnp.dot(jnp.concatenate([picked, ones], axis=0), raised, preferred_element_type=f32)

    def by_head(rows):
        return jnp.where(row < HD, rows[:, :BLK], rows[:, BLK:])

    def finish(index, shift, total, rescale=None):
        mine = jnp.concatenate([total[:HD, :BLK], total[HD:LANES, BLK:]], axis=0)
        count_all = total[LANES : LANES + 1]
        if not first:
            before = sum_in_ref[:, at(index)]
            count_before = row_in_ref[0, 1:2, at(index, 2 * BLK)]
            if rescale is not None:
                before = before * by_head(rescale)
                count_before = count_before * rescale
            mine = mine + before
            count_all = count_all + count_before
        if last:
            out_ref[at(index), :] = (mine * by_head(1.0 / count_all)).T.astype(bf16)
        else:
            sum_out_ref[:, at(index)] = mine
            row_out_ref[0, 0:1, at(index, 2 * BLK)] = shift
            row_out_ref[0, 1:2, at(index, 2 * BLK)] = count_all
        return count_all

    def one(index):
        query = queries(index)
        total = None
        shift = None if first else row_in_ref[0, 0:1, at(index, 2 * BLK)]
        for which in range(0, count, chunk):
            scores = score(index, which, query)
            if shift is None:
                shift = jnp.max(scores, axis=0, keepdims=True)
            part = gather(values(index, which), jnp.exp(scores - shift).astype(bf16))
            total = part if total is None else total + part
        return finish(index, shift, total)

    def whole_row(index):
        query = queries(index)
        shift = jnp.full((1, 2 * BLK), -jnp.inf, f32) if first else row_in_ref[0, 0:1, at(index, 2 * BLK)]
        old = shift

        def largest(n, shift):
            return jnp.maximum(shift, jnp.max(score(index, chunk * n, query), axis=0, keepdims=True))

        shift = lax.fori_loop(0, count // chunk, largest, shift)

        def add(n, total):
            raised = jnp.exp(score(index, chunk * n, query) - shift).astype(bf16)
            return total + gather(values(index, chunk * n), raised)

        total = lax.fori_loop(0, count // chunk, add, jnp.zeros((LANES + 16, 2 * BLK), f32))
        finish(index, shift, total, None if first else jnp.exp(old - shift))

    def body(number, peak):
        for n in range(together):
            peak = jnp.maximum(peak, one(number * together + n))
        return peak

    peak = lax.fori_loop(0, blocks // together, body, jnp.zeros((1, 2 * BLK), f32))

    @pl.when(jnp.logical_not(jnp.max(peak) <= TOTAL_CAP))
    def _():
        lax.fori_loop(0, blocks, lambda index, carry: (whole_row(index), carry)[1], 0)


def attend(name, table, query, keys, values, state, last, together, chunk):
    f32, bf16 = jnp.float32, jnp.bfloat16
    rows = query.shape[1]
    blocks = rows // BLK
    count = table.shape[1]
    while blocks % together:
        together //= 2
    total_rows = sum(key.shape[0] for key in keys)
    across = lambda array: pl.BlockSpec((LANES, array.shape[1]), lambda p: (p, 0))
    down = lambda array: pl.BlockSpec((array.shape[0], LANES), lambda p: (0, p))
    per_row = pl.BlockSpec((1, 2, 2 * rows), lambda p: (p, 0, 0))
    in_specs = [pl.BlockSpec(memory_space=pltpu.SMEM), across(query)]
    in_specs += [down(key) for key in keys] + [across(value) for value in values]
    if state:
        in_specs += [across(query), per_row]
    if last:
        out_specs = pl.BlockSpec((rows, LANES), lambda p: (0, p))
        out_shape = jax.ShapeDtypeStruct((rows, D), bf16)
    else:
        out_specs = [across(query), per_row]
        out_shape = [jax.ShapeDtypeStruct((D, rows), f32), jax.ShapeDtypeStruct((PAIRS, 2, 2 * rows), f32)]
    scratch = [pltpu.VMEM((total_rows, LANES), bf16), pltpu.VMEM((LANES, total_rows), bf16)]
    scores = rows * count * BLK * H
    return pl.pallas_call(
        functools.partial(attend_kernel, not state, last, blocks, count, together, chunk, len(keys)),
        grid=(PAIRS,),
        in_specs=in_specs,
        out_specs=out_specs,
        out_shape=out_shape,
        scratch_shapes=scratch if len(keys) > 1 else [],
        compiler_params=pltpu.CompilerParams(vmem_limit_bytes=18 * 2**20),
        cost_estimate=pl.CostEstimate(
            flops=24 * scores * HD, bytes_accessed=4 * total_rows * D + 10 * rows * D, transcendentals=scores
        ),
        name=name,
    )(table, query, *keys, *values, *state)


def project_rows(rows, weight):
    return jnp.dot(rows, weight, preferred_element_type=jnp.float32).astype(jnp.bfloat16)


def project_columns(weight, rows, scale=1.0):
    wide = lax.dot_general(weight, rows, (((1,), (1,)), ((), ())), preferred_element_type=jnp.float32)
    return (wide * scale).astype(jnp.bfloat16)


def rows_by_axes(own, weights, place, stride, strides):
    summary = SUMB * BLK
    half = summary // 2
    cut = own.shape[0] - summary
    chips = strides // 2
    low = place == 0
    swap = lambda rows: lax.ppermute(rows, "head", [(0, 1), (1, 0)])
    beside = lambda rows: lax.ppermute(rows, "blk", [(s, s ^ 1) for s in range(strides)])

    def along(rows, k):
        return lax.ppermute(rows, "blk", [(s, (s + 2 * k) % strides) for s in range(strides)])

    steps = []
    for s in range(strides - 1):
        steps += [(s, s + 1), (strides + s + 1, strides + s)]
    to_next = lambda rows: lax.ppermute(rows, ("head", "blk"), steps)

    other_end = swap(own[-half:])
    other_end, own, weights = lax.optimization_barrier((other_end, own, weights))
    carried = jnp.where(low, other_end, own[cut : cut + half])
    other = swap(own[:-half])
    slots = [None] * chips
    slots[2:-1] = [along(carried, k) for k in range(2, chips - 1)]
    slots[1] = along(carried, 1)
    slots[1], after = lax.optimization_barrier((slots[1], carried))
    slots[-1] = along(after, chips - 1)
    slots[0] = jnp.concatenate([carried, jnp.where(low, other[-half:], own[-half:])], axis=0)
    slots[1:] = [jnp.concatenate([rows, swap(rows)], axis=0) for rows in slots[1:]]
    pieces = [own, other, other_end, to_next(other), to_next(other_end), beside(slots[0])]
    for rows in slots[1:]:
        pieces += [rows, beside(rows)]

    def position(block):
        of, inside = block // SB, block % SB
        rel = block - stride * SB
        mine = inside % 8 + jnp.where(inside // 8 == place, 0, 8)
        edge = jnp.where(rel < 0, rel + SB + 8, rel)
        order = inside - (SB - SUMB)
        k = (stride // 2 - of // 2) % chips
        turned = (order // 2 ^ (1 - place)) * 2 + order % 2
        far = jnp.where(k == 0, 24, 28 + (k - 1) * 8 + jnp.where(of % 2 == stride % 2, 0, 4)) + turned
        return jnp.where(of == stride, mine, edge), jnp.where(of == stride, mine, far)

    return pieces, weights, position


def rows_by_gather(own, place, stride, strides, heads):
    summary = SUMB * BLK
    share = summary // heads
    lower = place < heads // 2
    stride_rows = lax.all_gather(own, "head", axis=0, tiled=True)
    piece = lax.dynamic_slice_in_dim(stride_rows[-summary:], place * share, share, 0)
    far_rows = lax.all_gather(piece, ("blk", "head"), axis=0, tiled=True)
    half = stride_rows.shape[0] // 2
    steps = []
    for h in range(heads):
        for s in range(strides - 1):
            ends = (h * strides + s, h * strides + s + 1)
            steps.append(ends if h < heads // 2 else ends[::-1])
    edge = lax.ppermute(jnp.where(lower, stride_rows[half:], stride_rows[:half]), ("head", "blk"), steps)

    def position(block):
        rel = block - stride * SB
        near = jnp.where(rel < 0, rel + SB + REACH, rel)
        return near, SB + REACH + block // SB * SUMB + block % SB - (SB - SUMB)

    return [stride_rows, edge, far_rows], position


def on_device(tokens, proj_weight, out_weight, pattern):
    heads = lax.axis_size("head")
    strides = lax.axis_size("blk")
    place = lax.axis_index("head")
    stride = lax.axis_index("blk")
    own = tokens[0]
    blocks = own.shape[0] // BLK
    weights = split_weights(proj_weight)

    if heads == 2:
        pieces, weights, position = rows_by_axes(own, weights, place, stride, strides)
        own = pieces[0]
    else:
        pieces, position = rows_by_gather(own, place, stride, strides, heads)
    listed = lax.dynamic_slice_in_dim(pattern, place * blocks, blocks, 0)
    near, far = position(listed)
    column = lax.broadcasted_iota(jnp.int32, listed.shape, 1)
    table = jnp.where(column < LSEL, near, far)

    query_weight, key_weight, value_weight = weights
    query = project_columns(query_weight, own, HD**-0.5)
    keys = [project_rows(rows, key_weight) for rows in pieces]
    values = [project_columns(value_weight, rows) for rows in pieces]
    mixed = attend("attend", table, query, keys, values, [], True, 2, 8)
    out = jnp.dot(mixed, out_weight, preferred_element_type=jnp.float32).astype(jnp.bfloat16)
    return out.reshape(tokens.shape)


def solution(mesh):
    return jax.shard_map(
        on_device,
        mesh=mesh,
        in_specs=(P(("batch", "blk"), "head", None), P(), P(), P(("batch", "blk"), None)),
        out_specs=P(("batch", "blk"), "head", None),
        check_vma=False,
    )
```

```python
import functools

import jax
import jax.numpy as jnp
from jax import lax
from jax.experimental import pallas as pl
from jax.experimental.pallas import tpu as pltpu
from jax.sharding import PartitionSpec as P

D = 1024
H = 16
HD = 64
BLK = 128
REACH = 8
LSEL = 6
SUMB = 4
SB = 16
KSEL = 16
PAIRS = H // 2
LANES = 2 * HD
TOTAL_CAP = 2.0**100


def split_kernel(weight_ref, query_ref, key_ref, value_ref):
    both = weight_ref[...]
    first, second = both[:, : 3 * HD], both[:, 3 * HD :]

    def columns(which):
        lo = which * HD
        return jnp.concatenate([first[:, lo : lo + HD], second[:, lo : lo + HD]], axis=1)

    query_ref[...] = columns(0).T
    key_ref[...] = columns(1)
    value_ref[...] = columns(2).T


def split_weights(proj_weight):
    wide = jax.ShapeDtypeStruct((D, D), jnp.bfloat16)
    across = pl.BlockSpec((LANES, D), lambda p: (p, 0))
    down = pl.BlockSpec((D, LANES), lambda p: (0, p))
    return pl.pallas_call(
        split_kernel,
        grid=(PAIRS,),
        in_specs=[pl.BlockSpec((D, 3 * LANES), lambda p: (0, p))],
        out_specs=[across, down, across],
        out_shape=[wide, wide, wide],
        cost_estimate=pl.CostEstimate(flops=0, bytes_accessed=4 * D * 3 * D, transcendentals=0),
        name="split_weights",
    )(proj_weight)


def attend_kernel(first, last, blocks, count, together, chunk, pieces, *refs):
    f32, bf16 = jnp.float32, jnp.bfloat16
    refs = list(refs)
    table_ref, query_ref = refs[:2]
    key_refs = refs[2 : 2 + pieces]
    value_refs = refs[2 + pieces : 2 + 2 * pieces]
    refs = refs[2 + 2 * pieces :]
    if not first:
        sum_in_ref, row_in_ref = refs[:2]
        refs = refs[2:]
    if last:
        out_ref = refs.pop(0)
    else:
        sum_out_ref, row_out_ref = refs[:2]
        refs = refs[2:]
    if pieces == 1:
        key_ref, value_ref = key_refs[0], value_refs[0]
    else:
        key_ref, value_ref = refs
        start = 0
        for key_piece, value_piece in zip(key_refs, value_refs):
            size = key_piece.shape[0]
            key_ref[start : start + size, :] = key_piece[...]
            value_ref[:, start : start + size] = value_piece[...]
            start += size

    row = lax.broadcasted_iota(jnp.int32, (LANES, BLK), 0)

    def at(index, size=BLK):
        return pl.ds(pl.multiple_of(index * size, size), size)

    def queries(index):
        own = query_ref[:, at(index)]
        zero = jnp.zeros_like(own)
        return jnp.concatenate([jnp.where(row < HD, own, zero), jnp.where(row < HD, zero, own)], axis=1)

    def places(index, which):
        return [pl.multiple_of(table_ref[index, which + n] * BLK, BLK) for n in range(chunk)]

    def score(index, which, query):
        keys = [key_ref[pl.ds(place, BLK), :] for place in places(index, which)]
        return jnp.dot(jnp.concatenate(keys, axis=0), query, preferred_element_type=f32)

    def values(index, which):
        return jnp.concatenate([value_ref[:, pl.ds(place, BLK)] for place in places(index, which)], axis=1)

    def gather(picked, raised):
        ones = jnp.ones((16, raised.shape[0]), bf16)
        return jnp.dot(jnp.concatenate([picked, ones], axis=0), raised, preferred_element_type=f32)

    def by_head(rows):
        return jnp.where(row < HD, rows[:, :BLK], rows[:, BLK:])

    def finish(index, shift, total, rescale=None):
        mine = jnp.concatenate([total[:HD, :BLK], total[HD:LANES, BLK:]], axis=0)
        count_all = total[LANES : LANES + 1]
        if not first:
            before = sum_in_ref[:, at(index)]
            count_before = row_in_ref[0, 1:2, at(index, 2 * BLK)]
            if rescale is not None:
                before = before * by_head(rescale)
                count_before = count_before * rescale
            mine = mine + before
            count_all = count_all + count_before
        if last:
            out_ref[at(index), :] = (mine * by_head(1.0 / count_all)).T.astype(bf16)
        else:
            sum_out_ref[:, at(index)] = mine
            row_out_ref[0, 0:1, at(index, 2 * BLK)] = shift
            row_out_ref[0, 1:2, at(index, 2 * BLK)] = count_all
        return count_all

    def whole_row(index):
        query = queries(index)
        shift = jnp.full((1, 2 * BLK), -jnp.inf, f32) if first else row_in_ref[0, 0:1, at(index, 2 * BLK)]
        old = shift

        def largest(n, shift):
            return jnp.maximum(shift, jnp.max(score(index, chunk * n, query), axis=0, keepdims=True))

        shift = lax.fori_loop(0, count // chunk, largest, shift)

        def add(n, total):
            raised = jnp.exp(score(index, chunk * n, query) - shift).astype(bf16)
            return total + gather(values(index, chunk * n), raised)

        total = lax.fori_loop(0, count // chunk, add, jnp.zeros((LANES + 16, 2 * BLK), f32))
        finish(index, shift, total, None if first else jnp.exp(old - shift))

    def body(number, peak):
        steps = [(number * together + n, which) for n in range(together) for which in range(0, count, chunk)]
        asked = {}

        def ask(index, which):
            if which == 0:
                asked["query"] = queries(index)
            return score(index, which, asked["query"])

        following = ask(*steps[0])
        for number, (index, which) in enumerate(steps):
            scores = following
            if number + 1 < len(steps):
                following = ask(*steps[number + 1])
            if which == 0:
                total = None
                shift = jnp.max(scores, axis=0, keepdims=True) if first else row_in_ref[0, 0:1, at(index, 2 * BLK)]
            part = gather(values(index, which), jnp.exp(scores - shift).astype(bf16))
            total = part if total is None else total + part
            if which + chunk == count:
                peak = jnp.maximum(peak, finish(index, shift, total))
        return peak

    peak = lax.fori_loop(0, blocks // together, body, jnp.zeros((1, 2 * BLK), f32))

    @pl.when(jnp.logical_not(jnp.max(peak) <= TOTAL_CAP))
    def _():
        lax.fori_loop(0, blocks, lambda index, carry: (whole_row(index), carry)[1], 0)


def attend(name, table, query, keys, values, state, last, together, chunk):
    f32, bf16 = jnp.float32, jnp.bfloat16
    rows = query.shape[1]
    blocks = rows // BLK
    count = table.shape[1]
    while blocks % together:
        together //= 2
    total_rows = sum(key.shape[0] for key in keys)
    across = lambda array: pl.BlockSpec((LANES, array.shape[1]), lambda p: (p, 0))
    down = lambda array: pl.BlockSpec((array.shape[0], LANES), lambda p: (0, p))
    per_row = pl.BlockSpec((1, 2, 2 * rows), lambda p: (p, 0, 0))
    in_specs = [pl.BlockSpec(memory_space=pltpu.SMEM), across(query)]
    in_specs += [down(key) for key in keys] + [across(value) for value in values]
    if state:
        in_specs += [across(query), per_row]
    if last:
        out_specs = pl.BlockSpec((rows, LANES), lambda p: (0, p))
        out_shape = jax.ShapeDtypeStruct((rows, D), bf16)
    else:
        out_specs = [across(query), per_row]
        out_shape = [jax.ShapeDtypeStruct((D, rows), f32), jax.ShapeDtypeStruct((PAIRS, 2, 2 * rows), f32)]
    scratch = [pltpu.VMEM((total_rows, LANES), bf16), pltpu.VMEM((LANES, total_rows), bf16)]
    scores = rows * count * BLK * H
    return pl.pallas_call(
        functools.partial(attend_kernel, not state, last, blocks, count, together, chunk, len(keys)),
        grid=(PAIRS,),
        in_specs=in_specs,
        out_specs=out_specs,
        out_shape=out_shape,
        scratch_shapes=scratch if len(keys) > 1 else [],
        compiler_params=pltpu.CompilerParams(vmem_limit_bytes=18 * 2**20),
        cost_estimate=pl.CostEstimate(
            flops=24 * scores * HD, bytes_accessed=4 * total_rows * D + 10 * rows * D, transcendentals=scores
        ),
        name=name,
    )(table, query, *keys, *values, *state)


def project_rows(rows, weight):
    return jnp.dot(rows, weight, preferred_element_type=jnp.float32).astype(jnp.bfloat16)


def project_columns(weight, rows, scale=1.0):
    wide = lax.dot_general(weight, rows, (((1,), (1,)), ((), ())), preferred_element_type=jnp.float32)
    return (wide * scale).astype(jnp.bfloat16)


def rows_by_axes(own, weights, place, stride, strides):
    summary = SUMB * BLK
    half = summary // 2
    cut = own.shape[0] - summary
    chips = strides // 2
    low = place == 0
    swap = lambda rows: lax.ppermute(rows, "head", [(0, 1), (1, 0)])
    beside = lambda rows: lax.ppermute(rows, "blk", [(s, s ^ 1) for s in range(strides)])

    def along(rows, k):
        return lax.ppermute(rows, "blk", [(s, (s + 2 * k) % strides) for s in range(strides)])

    steps = []
    for s in range(strides - 1):
        steps += [(s, s + 1), (strides + s + 1, strides + s)]
    to_next = lambda rows: lax.ppermute(rows, ("head", "blk"), steps)

    other_end = swap(own[-half:])
    other_end, own, weights = lax.optimization_barrier((other_end, own, weights))
    carried = lax.optimization_barrier(jnp.where(low, other_end, own[cut : cut + half]))
    other = swap(own[:-half])
    slots = [None] * chips
    slots[2:-1] = [along(carried, k) for k in range(2, chips - 1)]
    slots[1] = along(carried, 1)
    slots[1], other, after = lax.optimization_barrier((slots[1], other, carried))
    slots[-1] = along(after, chips - 1)
    slots[0] = jnp.where(low, jnp.concatenate([other_end, other[-half:]], axis=0), own[cut:])
    slots[1:] = [jnp.concatenate([rows, swap(rows)], axis=0) for rows in slots[1:]]
    pieces = [own, other, other_end, to_next(other), to_next(other_end), beside(slots[0])]
    for rows in slots[1:]:
        pieces += [rows, beside(rows)]

    def position(block):
        of, inside = block // SB, block % SB
        rel = block - stride * SB
        mine = inside % 8 + jnp.where(inside // 8 == place, 0, 8)
        edge = jnp.where(rel < 0, rel + SB + 8, rel)
        order = inside - (SB - SUMB)
        k = (stride // 2 - of // 2) % chips
        turned = (order // 2 ^ (1 - place)) * 2 + order % 2
        far = jnp.where(k == 0, 24, 28 + (k - 1) * 8 + jnp.where(of % 2 == stride % 2, 0, 4)) + turned
        return jnp.where(of == stride, mine, edge), jnp.where(of == stride, mine, far)

    return pieces, weights, position


def rows_by_gather(own, place, stride, strides, heads):
    summary = SUMB * BLK
    share = summary // heads
    lower = place < heads // 2
    stride_rows = lax.all_gather(own, "head", axis=0, tiled=True)
    piece = lax.dynamic_slice_in_dim(stride_rows[-summary:], place * share, share, 0)
    far_rows = lax.all_gather(piece, ("blk", "head"), axis=0, tiled=True)
    half = stride_rows.shape[0] // 2
    steps = []
    for h in range(heads):
        for s in range(strides - 1):
            ends = (h * strides + s, h * strides + s + 1)
            steps.append(ends if h < heads // 2 else ends[::-1])
    edge = lax.ppermute(jnp.where(lower, stride_rows[half:], stride_rows[:half]), ("head", "blk"), steps)

    def position(block):
        rel = block - stride * SB
        near = jnp.where(rel < 0, rel + SB + REACH, rel)
        return near, SB + REACH + block // SB * SUMB + block % SB - (SB - SUMB)

    return [stride_rows, edge, far_rows], position


def on_device(tokens, proj_weight, out_weight, pattern):
    heads = lax.axis_size("head")
    strides = lax.axis_size("blk")
    place = lax.axis_index("head")
    stride = lax.axis_index("blk")
    own = tokens[0]
    blocks = own.shape[0] // BLK
    weights = split_weights(proj_weight)

    if heads == 2:
        pieces, weights, position = rows_by_axes(own, weights, place, stride, strides)
        own = pieces[0]
    else:
        pieces, position = rows_by_gather(own, place, stride, strides, heads)
    listed = lax.dynamic_slice_in_dim(pattern, place * blocks, blocks, 0)
    near, far = position(listed)
    column = lax.broadcasted_iota(jnp.int32, listed.shape, 1)
    table = jnp.where(column < LSEL, near, far)

    query_weight, key_weight, value_weight = weights
    query = project_columns(query_weight, own, HD**-0.5)
    keys = [project_rows(rows, key_weight) for rows in pieces]
    values = [project_columns(value_weight, rows) for rows in pieces]
    mixed = attend("attend", table, query, keys, values, [], True, 2, 4)
    out = jnp.dot(mixed, out_weight, preferred_element_type=jnp.float32).astype(jnp.bfloat16)
    return out.reshape(tokens.shape)


def solution(mesh):
    return jax.shard_map(
        on_device,
        mesh=mesh,
        in_specs=(P(("batch", "blk"), "head", None), P(), P(), P(("batch", "blk"), None)),
        out_specs=P(("batch", "blk"), "head", None),
        check_vma=False,
    )
```

```python
import functools

import jax
import jax.numpy as jnp
from jax import lax
from jax.experimental import pallas as pl
from jax.experimental.pallas import tpu as pltpu
from jax.sharding import PartitionSpec as P

D = 1024
H = 16
HD = 64
BLK = 128
REACH = 8
LSEL = 6
SUMB = 4
SB = 16
KSEL = 16
PAIRS = H // 2
LANES = 2 * HD
TOTAL_CAP = 2.0**100


def split_kernel(weight_ref, query_ref, key_ref, value_ref):
    both = weight_ref[...]
    first, second = both[:, : 3 * HD], both[:, 3 * HD :]

    def columns(which):
        lo = which * HD
        return jnp.concatenate([first[:, lo : lo + HD], second[:, lo : lo + HD]], axis=1)

    query_ref[...] = columns(0).T
    key_ref[...] = columns(1)
    value_ref[...] = columns(2).T


def split_weights(proj_weight):
    wide = jax.ShapeDtypeStruct((D, D), jnp.bfloat16)
    across = pl.BlockSpec((LANES, D), lambda p: (p, 0))
    down = pl.BlockSpec((D, LANES), lambda p: (0, p))
    return pl.pallas_call(
        split_kernel,
        grid=(PAIRS,),
        in_specs=[pl.BlockSpec((D, 3 * LANES), lambda p: (0, p))],
        out_specs=[across, down, across],
        out_shape=[wide, wide, wide],
        cost_estimate=pl.CostEstimate(flops=0, bytes_accessed=4 * D * 3 * D, transcendentals=0),
        name="split_weights",
    )(proj_weight)


def attend_kernel(first, last, blocks, count, together, chunk, pieces, *refs):
    f32, bf16 = jnp.float32, jnp.bfloat16
    refs = list(refs)
    table_ref, query_ref = refs[:2]
    key_refs = refs[2 : 2 + pieces]
    value_refs = refs[2 + pieces : 2 + 2 * pieces]
    refs = refs[2 + 2 * pieces :]
    if not first:
        sum_in_ref, row_in_ref = refs[:2]
        refs = refs[2:]
    if last:
        out_ref = refs.pop(0)
    else:
        sum_out_ref, row_out_ref = refs[:2]
        refs = refs[2:]
    if pieces == 1:
        key_ref, value_ref = key_refs[0], value_refs[0]
    else:
        key_ref, value_ref = refs
        start = 0
        for key_piece, value_piece in zip(key_refs, value_refs):
            size = key_piece.shape[0]
            key_ref[start : start + size, :] = key_piece[...]
            value_ref[:, start : start + size] = value_piece[...]
            start += size

    row = lax.broadcasted_iota(jnp.int32, (LANES, BLK), 0)

    def at(index, size=BLK):
        return pl.ds(pl.multiple_of(index * size, size), size)

    def queries(index):
        own = query_ref[:, at(index)]
        zero = jnp.zeros_like(own)
        return jnp.concatenate([jnp.where(row < HD, own, zero), jnp.where(row < HD, zero, own)], axis=1)

    def places(index, which):
        return [pl.multiple_of(table_ref[index, which + n] * BLK, BLK) for n in range(chunk)]

    def score(index, which, query):
        keys = [key_ref[pl.ds(place, BLK), :] for place in places(index, which)]
        return jnp.dot(jnp.concatenate(keys, axis=0), query, preferred_element_type=f32)

    def values(index, which):
        return jnp.concatenate([value_ref[:, pl.ds(place, BLK)] for place in places(index, which)], axis=1)

    def gather(picked, raised):
        ones = jnp.ones((16, raised.shape[0]), bf16)
        return jnp.dot(jnp.concatenate([picked, ones], axis=0), raised, preferred_element_type=f32)

    def by_head(rows):
        return jnp.where(row < HD, rows[:, :BLK], rows[:, BLK:])

    def finish(index, shift, total, rescale=None):
        mine = jnp.concatenate([total[:HD, :BLK], total[HD:LANES, BLK:]], axis=0)
        count_all = total[LANES : LANES + 1]
        if not first:
            before = sum_in_ref[:, at(index)]
            count_before = row_in_ref[0, 1:2, at(index, 2 * BLK)]
            if rescale is not None:
                before = before * by_head(rescale)
                count_before = count_before * rescale
            mine = mine + before
            count_all = count_all + count_before
        if last:
            out_ref[at(index), :] = (mine * by_head(1.0 / count_all)).T.astype(bf16)
        else:
            sum_out_ref[:, at(index)] = mine
            row_out_ref[0, 0:1, at(index, 2 * BLK)] = shift
            row_out_ref[0, 1:2, at(index, 2 * BLK)] = count_all
        return count_all

    def whole_row(index):
        query = queries(index)
        shift = jnp.full((1, 2 * BLK), -jnp.inf, f32) if first else row_in_ref[0, 0:1, at(index, 2 * BLK)]
        old = shift

        def largest(n, shift):
            return jnp.maximum(shift, jnp.max(score(index, chunk * n, query), axis=0, keepdims=True))

        shift = lax.fori_loop(0, count // chunk, largest, shift)

        def add(n, total):
            raised = jnp.exp(score(index, chunk * n, query) - shift).astype(bf16)
            return total + gather(values(index, chunk * n), raised)

        total = lax.fori_loop(0, count // chunk, add, jnp.zeros((LANES + 16, 2 * BLK), f32))
        finish(index, shift, total, None if first else jnp.exp(old - shift))

    def one(index):
        query = queries(index)
        total = None
        shift = None if first else row_in_ref[0, 0:1, at(index, 2 * BLK)]
        for which in range(0, count, chunk):
            scores = score(index, which, query)
            if shift is None:
                shift = jnp.max(scores, axis=0, keepdims=True)
            part = gather(values(index, which), jnp.exp(scores - shift).astype(bf16))
            total = part if total is None else total + part
        return finish(index, shift, total)

    def body(number, peak):
        for n in range(together):
            peak = jnp.maximum(peak, one(number * together + n))
        return peak

    peak = lax.fori_loop(0, blocks // together, body, jnp.zeros((1, 2 * BLK), f32))

    @pl.when(jnp.logical_not(jnp.max(peak) <= TOTAL_CAP))
    def _():
        lax.fori_loop(0, blocks, lambda index, carry: (whole_row(index), carry)[1], 0)


def attend(name, table, query, keys, values, state, last, together, chunk):
    f32, bf16 = jnp.float32, jnp.bfloat16
    rows = query.shape[1]
    blocks = rows // BLK
    count = table.shape[1]
    while blocks % together:
        together //= 2
    total_rows = sum(key.shape[0] for key in keys)
    across = lambda array: pl.BlockSpec((LANES, array.shape[1]), lambda p: (p, 0))
    down = lambda array: pl.BlockSpec((array.shape[0], LANES), lambda p: (0, p))
    per_row = pl.BlockSpec((1, 2, 2 * rows), lambda p: (p, 0, 0))
    in_specs = [pl.BlockSpec(memory_space=pltpu.SMEM), across(query)]
    in_specs += [down(key) for key in keys] + [across(value) for value in values]
    if state:
        in_specs += [across(query), per_row]
    if last:
        out_specs = pl.BlockSpec((rows, LANES), lambda p: (0, p))
        out_shape = jax.ShapeDtypeStruct((rows, D), bf16)
    else:
        out_specs = [across(query), per_row]
        out_shape = [jax.ShapeDtypeStruct((D, rows), f32), jax.ShapeDtypeStruct((PAIRS, 2, 2 * rows), f32)]
    scratch = [pltpu.VMEM((total_rows, LANES), bf16), pltpu.VMEM((LANES, total_rows), bf16)]
    scores = rows * count * BLK * H
    return pl.pallas_call(
        functools.partial(attend_kernel, not state, last, blocks, count, together, chunk, len(keys)),
        grid=(PAIRS,),
        in_specs=in_specs,
        out_specs=out_specs,
        out_shape=out_shape,
        scratch_shapes=scratch if len(keys) > 1 else [],
        compiler_params=pltpu.CompilerParams(vmem_limit_bytes=18 * 2**20),
        cost_estimate=pl.CostEstimate(
            flops=24 * scores * HD, bytes_accessed=4 * total_rows * D + 10 * rows * D, transcendentals=scores
        ),
        name=name,
    )(table, query, *keys, *values, *state)


def project_rows(rows, weight):
    return jnp.dot(rows, weight, preferred_element_type=jnp.float32).astype(jnp.bfloat16)


def project_columns(weight, rows, scale=1.0):
    wide = lax.dot_general(weight, rows, (((1,), (1,)), ((), ())), preferred_element_type=jnp.float32)
    return (wide * scale).astype(jnp.bfloat16)


def rows_by_axes(own, weights, place, stride, strides):
    summary = SUMB * BLK
    half = summary // 2
    cut = own.shape[0] - summary
    chips = strides // 2
    low = place == 0
    swap = lambda rows: lax.ppermute(rows, "head", [(0, 1), (1, 0)])
    beside = lambda rows: lax.ppermute(rows, "blk", [(s, s ^ 1) for s in range(strides)])

    steps = []
    for s in range(strides - 1):
        steps += [(s, s + 1), (strides + s + 1, strides + s)]
    to_next = lambda rows: lax.ppermute(rows, ("head", "blk"), steps)

    other_end = swap(own[-half:])
    other_end, own, weights = lax.optimization_barrier((other_end, own, weights))
    carried = jnp.where(low, other_end, own[cut : cut + half])
    other = swap(own[:-half])
    parities = [[s for s in range(strides) if s % 2 == core] for core in range(2)]
    column = lax.all_gather(carried, "blk", axis=0, tiled=True, axis_index_groups=parities)
    turned_column = jnp.concatenate([column, column], axis=0)
    foreign = lax.dynamic_slice_in_dim(turned_column, (stride // 2 + 1) * half, column.shape[0] - half, 0)
    across = swap(foreign)
    nearby = jnp.where(low, jnp.concatenate([other_end, other[-half:]], axis=0), own[cut:])
    pieces = [own, other, other_end, to_next(other), to_next(other_end), beside(nearby)]
    pieces += [foreign, across, beside(foreign), beside(across)]
    base = 28
    span = 2 * (chips - 1)

    def position(block):
        of, inside = block // SB, block % SB
        rel = block - stride * SB
        mine = inside % 8 + jnp.where(inside // 8 == place, 0, 8)
        edge = jnp.where(rel < 0, rel + SB + 8, rel)
        order = inside - (SB - SUMB)
        k = (of // 2 - stride // 2) % chips
        turned = (order // 2 ^ (1 - place)) * 2 + order % 2
        part = jnp.where(of % 2 == stride % 2, 0, 2) + jnp.where(order // 2 == 1 - place, 0, 1)
        far = jnp.where(k == 0, 24 + turned, base + part * span + (k - 1) * 2 + order % 2)
        return jnp.where(of == stride, mine, edge), jnp.where(of == stride, mine, far)

    return pieces, weights, position


def rows_by_gather(own, place, stride, strides, heads):
    summary = SUMB * BLK
    share = summary // heads
    lower = place < heads // 2
    stride_rows = lax.all_gather(own, "head", axis=0, tiled=True)
    piece = lax.dynamic_slice_in_dim(stride_rows[-summary:], place * share, share, 0)
    far_rows = lax.all_gather(piece, ("blk", "head"), axis=0, tiled=True)
    half = stride_rows.shape[0] // 2
    steps = []
    for h in range(heads):
        for s in range(strides - 1):
            ends = (h * strides + s, h * strides + s + 1)
            steps.append(ends if h < heads // 2 else ends[::-1])
    edge = lax.ppermute(jnp.where(lower, stride_rows[half:], stride_rows[:half]), ("head", "blk"), steps)

    def position(block):
        rel = block - stride * SB
        near = jnp.where(rel < 0, rel + SB + REACH, rel)
        return near, SB + REACH + block // SB * SUMB + block % SB - (SB - SUMB)

    return [stride_rows, edge, far_rows], position


def on_device(tokens, proj_weight, out_weight, pattern):
    heads = lax.axis_size("head")
    strides = lax.axis_size("blk")
    place = lax.axis_index("head")
    stride = lax.axis_index("blk")
    own = tokens[0]
    blocks = own.shape[0] // BLK
    weights = split_weights(proj_weight)

    if heads == 2:
        pieces, weights, position = rows_by_axes(own, weights, place, stride, strides)
        own = pieces[0]
    else:
        pieces, position = rows_by_gather(own, place, stride, strides, heads)
    listed = lax.dynamic_slice_in_dim(pattern, place * blocks, blocks, 0)
    near, far = position(listed)
    column = lax.broadcasted_iota(jnp.int32, listed.shape, 1)
    table = jnp.where(column < LSEL, near, far)

    query_weight, key_weight, value_weight = weights
    query = project_columns(query_weight, own, HD**-0.5)
    keys = [project_rows(rows, key_weight) for rows in pieces]
    values = [project_columns(value_weight, rows) for rows in pieces]
    mixed = attend("attend", table, query, keys, values, [], True, 2, 4)
    out = jnp.dot(mixed, out_weight, preferred_element_type=jnp.float32).astype(jnp.bfloat16)
    return out.reshape(tokens.shape)


def solution(mesh):
    return jax.shard_map(
        on_device,
        mesh=mesh,
        in_specs=(P(("batch", "blk"), "head", None), P(), P(), P(("batch", "blk"), None)),
        out_specs=P(("batch", "blk"), "head", None),
        check_vma=False,
    )
```

```python
import functools

import jax
import jax.numpy as jnp
from jax import lax
from jax.experimental import pallas as pl
from jax.experimental.pallas import tpu as pltpu
from jax.sharding import PartitionSpec as P

D = 1024
H = 16
HD = 64
BLK = 128
REACH = 8
LSEL = 6
SUMB = 4
SB = 16
KSEL = 16
PAIRS = H // 2
LANES = 2 * HD
TOTAL_CAP = 2.0**100


def split_kernel(weight_ref, query_ref, key_ref, value_ref):
    both = weight_ref[...]
    first, second = both[:, : 3 * HD], both[:, 3 * HD :]

    def columns(which):
        lo = which * HD
        return jnp.concatenate([first[:, lo : lo + HD], second[:, lo : lo + HD]], axis=1)

    query_ref[...] = columns(0).T
    key_ref[...] = columns(1)
    value_ref[...] = columns(2).T


def split_weights(proj_weight):
    wide = jax.ShapeDtypeStruct((D, D), jnp.bfloat16)
    across = pl.BlockSpec((LANES, D), lambda p: (p, 0))
    down = pl.BlockSpec((D, LANES), lambda p: (0, p))
    return pl.pallas_call(
        split_kernel,
        grid=(PAIRS,),
        in_specs=[pl.BlockSpec((D, 3 * LANES), lambda p: (0, p))],
        out_specs=[across, down, across],
        out_shape=[wide, wide, wide],
        cost_estimate=pl.CostEstimate(flops=0, bytes_accessed=4 * D * 3 * D, transcendentals=0),
        name="split_weights",
    )(proj_weight)


def attend_kernel(first, last, blocks, count, together, chunk, pieces, *refs):
    f32, bf16 = jnp.float32, jnp.bfloat16
    refs = list(refs)
    table_ref, query_ref = refs[:2]
    key_refs = refs[2 : 2 + pieces]
    value_refs = refs[2 + pieces : 2 + 2 * pieces]
    refs = refs[2 + 2 * pieces :]
    if not first:
        sum_in_ref, row_in_ref = refs[:2]
        refs = refs[2:]
    if last:
        out_ref = refs.pop(0)
    else:
        sum_out_ref, row_out_ref = refs[:2]
        refs = refs[2:]
    if pieces == 1:
        key_ref, value_ref = key_refs[0], value_refs[0]
    else:
        key_ref, value_ref = refs
        start = 0
        for key_piece, value_piece in zip(key_refs, value_refs):
            size = key_piece.shape[0]
            key_ref[start : start + size, :] = key_piece[...]
            value_ref[:, start : start + size] = value_piece[...]
            start += size

    row = lax.broadcasted_iota(jnp.int32, (LANES, BLK), 0)

    def at(index, size=BLK):
        return pl.ds(pl.multiple_of(index * size, size), size)

    def queries(index):
        own = query_ref[:, at(index)]
        zero = jnp.zeros_like(own)
        return jnp.concatenate([jnp.where(row < HD, own, zero), jnp.where(row < HD, zero, own)], axis=1)

    def places(index, which, size):
        return [pl.multiple_of(table_ref[index, which + n] * BLK, BLK) for n in range(size)]

    def score(index, which, size, query):
        keys = [key_ref[pl.ds(place, BLK), :] for place in places(index, which, size)]
        return jnp.dot(jnp.concatenate(keys, axis=0), query, preferred_element_type=f32)

    def values(index, which, size):
        return jnp.concatenate([value_ref[:, pl.ds(place, BLK)] for place in places(index, which, size)], axis=1)

    def gather(picked, raised):
        ones = jnp.ones((16, raised.shape[0]), bf16)
        return jnp.dot(jnp.concatenate([picked, ones], axis=0), raised, preferred_element_type=f32)

    def by_head(rows):
        return jnp.where(row < HD, rows[:, :BLK], rows[:, BLK:])

    def finish(index, shift, total, rescale=None):
        mine = jnp.concatenate([total[:HD, :BLK], total[HD:LANES, BLK:]], axis=0)
        count_all = total[LANES : LANES + 1]
        if not first:
            before = sum_in_ref[:, at(index)]
            count_before = row_in_ref[0, 1:2, at(index, 2 * BLK)]
            if rescale is not None:
                before = before * by_head(rescale)
                count_before = count_before * rescale
            mine = mine + before
            count_all = count_all + count_before
        if last:
            out_ref[at(index), :] = (mine * by_head(1.0 / count_all)).T.astype(bf16)
        else:
            sum_out_ref[:, at(index)] = mine
            row_out_ref[0, 0:1, at(index, 2 * BLK)] = shift
            row_out_ref[0, 1:2, at(index, 2 * BLK)] = count_all
        return count_all

    def whole_row(index):
        query = queries(index)
        shift = jnp.full((1, 2 * BLK), -jnp.inf, f32) if first else row_in_ref[0, 0:1, at(index, 2 * BLK)]
        old = shift

        def largest(n, shift):
            return jnp.maximum(shift, jnp.max(score(index, 2 * n, 2, query), axis=0, keepdims=True))

        shift = lax.fori_loop(0, count // 2, largest, shift)

        def add(n, total):
            raised = jnp.exp(score(index, 2 * n, 2, query) - shift).astype(bf16)
            return total + gather(values(index, 2 * n, 2), raised)

        total = lax.fori_loop(0, count // 2, add, jnp.zeros((LANES + 16, 2 * BLK), f32))
        finish(index, shift, total, None if first else jnp.exp(old - shift))

    def one(index):
        query = queries(index)
        total = None
        shift = None if first else row_in_ref[0, 0:1, at(index, 2 * BLK)]
        for which in range(0, count, chunk):
            size = min(chunk, count - which)
            scores = score(index, which, size, query)
            if shift is None:
                shift = jnp.max(scores, axis=0, keepdims=True)
            part = gather(values(index, which, size), jnp.exp(scores - shift).astype(bf16))
            total = part if total is None else total + part
        return finish(index, shift, total)

    def body(number, peak):
        for n in range(together):
            peak = jnp.maximum(peak, one(number * together + n))
        return peak

    peak = lax.fori_loop(0, blocks // together, body, jnp.zeros((1, 2 * BLK), f32))

    @pl.when(jnp.logical_not(jnp.max(peak) <= TOTAL_CAP))
    def _():
        lax.fori_loop(0, blocks, lambda index, carry: (whole_row(index), carry)[1], 0)


def attend(name, table, query, keys, values, state, last, together, chunk):
    f32, bf16 = jnp.float32, jnp.bfloat16
    rows = query.shape[1]
    blocks = rows // BLK
    count = table.shape[1]
    while blocks % together:
        together //= 2
    total_rows = sum(key.shape[0] for key in keys)
    across = lambda array: pl.BlockSpec((LANES, array.shape[1]), lambda p: (p, 0))
    down = lambda array: pl.BlockSpec((array.shape[0], LANES), lambda p: (0, p))
    per_row = pl.BlockSpec((1, 2, 2 * rows), lambda p: (p, 0, 0))
    in_specs = [pl.BlockSpec(memory_space=pltpu.SMEM), across(query)]
    in_specs += [down(key) for key in keys] + [across(value) for value in values]
    if state:
        in_specs += [across(query), per_row]
    if last:
        out_specs = pl.BlockSpec((rows, LANES), lambda p: (0, p))
        out_shape = jax.ShapeDtypeStruct((rows, D), bf16)
    else:
        out_specs = [across(query), per_row]
        out_shape = [jax.ShapeDtypeStruct((D, rows), f32), jax.ShapeDtypeStruct((PAIRS, 2, 2 * rows), f32)]
    scratch = [pltpu.VMEM((total_rows, LANES), bf16), pltpu.VMEM((LANES, total_rows), bf16)]
    scores = rows * count * BLK * H
    return pl.pallas_call(
        functools.partial(attend_kernel, not state, last, blocks, count, together, chunk, len(keys)),
        grid=(PAIRS,),
        in_specs=in_specs,
        out_specs=out_specs,
        out_shape=out_shape,
        scratch_shapes=scratch if len(keys) > 1 else [],
        compiler_params=pltpu.CompilerParams(vmem_limit_bytes=18 * 2**20),
        cost_estimate=pl.CostEstimate(
            flops=24 * scores * HD, bytes_accessed=4 * total_rows * D + 10 * rows * D, transcendentals=scores
        ),
        name=name,
    )(table, query, *keys, *values, *state)


def project_rows(rows, weight):
    return jnp.dot(rows, weight, preferred_element_type=jnp.float32).astype(jnp.bfloat16)


def project_columns(weight, rows, scale=1.0):
    wide = lax.dot_general(weight, rows, (((1,), (1,)), ((), ())), preferred_element_type=jnp.float32)
    return (wide * scale).astype(jnp.bfloat16)


def rows_by_axes(own, weights, place, stride, strides):
    summary = SUMB * BLK
    half = summary // 2
    cut = own.shape[0] - summary
    chips = strides // 2
    low = place == 0
    swap = lambda rows: lax.ppermute(rows, "head", [(0, 1), (1, 0)])
    beside = lambda rows: lax.ppermute(rows, "blk", [(s, s ^ 1) for s in range(strides)])

    def along(rows, k):
        return lax.ppermute(rows, "blk", [(s, (s + 2 * k) % strides) for s in range(strides)])

    steps = []
    for s in range(strides - 1):
        steps += [(s, s + 1), (strides + s + 1, strides + s)]
    to_next = lambda rows: lax.ppermute(rows, ("head", "blk"), steps)

    other_end = swap(own[-half:])
    other_end, own, weights = lax.optimization_barrier((other_end, own, weights))
    carried = jnp.where(low, other_end, own[cut : cut + half])
    other = swap(own[:-half])
    slots = [along(carried, k) for k in range(1, chips)]
    across = [swap(rows) for rows in slots]
    foreign = jnp.concatenate(slots, axis=0)
    nearby = jnp.where(low, jnp.concatenate([other_end, other[-half:]], axis=0), own[cut:])
    near_rows = [own, other, other_end, to_next(other), to_next(other_end)]
    far_rows = [nearby, beside(nearby), foreign, beside(foreign)]
    span = 2 * (chips - 1)

    def late_rows(state):
        state, arrived = lax.optimization_barrier((state, across))
        arrived = jnp.concatenate(arrived, axis=0)
        return state, [arrived, beside(arrived)]

    def position(block):
        of, inside = block // SB, block % SB
        rel = block - stride * SB
        mine = inside % 8 + jnp.where(inside // 8 == place, 0, 8)
        edge = jnp.where(rel < 0, rel + SB + 8, rel)
        order = inside - (SB - SUMB)
        k = (stride // 2 - of // 2) % chips
        turned = (order // 2 ^ (1 - place)) * 2 + order % 2
        beside_me = jnp.where(of % 2 == stride % 2, 0, 1)
        part = beside_me + jnp.where(order // 2 == 1 - place, 0, 2)
        far = jnp.where(k == 0, 4 * beside_me + turned, 8 + part * span + (k - 1) * 2 + order % 2)
        return jnp.where(of == stride, mine, edge), far

    return near_rows, far_rows, late_rows, weights, position


def rows_by_gather(own, place, stride, strides, heads):
    summary = SUMB * BLK
    share = summary // heads
    lower = place < heads // 2
    stride_rows = lax.all_gather(own, "head", axis=0, tiled=True)
    piece = lax.dynamic_slice_in_dim(stride_rows[-summary:], place * share, share, 0)
    far_rows = lax.all_gather(piece, ("blk", "head"), axis=0, tiled=True)
    half = stride_rows.shape[0] // 2
    steps = []
    for h in range(heads):
        for s in range(strides - 1):
            ends = (h * strides + s, h * strides + s + 1)
            steps.append(ends if h < heads // 2 else ends[::-1])
    edge = lax.ppermute(jnp.where(lower, stride_rows[half:], stride_rows[:half]), ("head", "blk"), steps)

    def position(block):
        rel = block - stride * SB
        near = jnp.where(rel < 0, rel + SB + REACH, rel)
        return near, block // SB * SUMB + block % SB - (SB - SUMB)

    return [stride_rows, edge], [far_rows], lambda state: (state, []), position


def on_device(tokens, proj_weight, out_weight, pattern):
    heads = lax.axis_size("head")
    strides = lax.axis_size("blk")
    place = lax.axis_index("head")
    stride = lax.axis_index("blk")
    own = tokens[0]
    blocks = own.shape[0] // BLK
    weights = split_weights(proj_weight)

    if heads == 2:
        near_rows, far_rows, late_rows, weights, position = rows_by_axes(own, weights, place, stride, strides)
        own = near_rows[0]
    else:
        near_rows, far_rows, late_rows, position = rows_by_gather(own, place, stride, strides, heads)
    listed = lax.dynamic_slice_in_dim(pattern, place * blocks, blocks, 0)
    near = position(listed[:, :LSEL])[0]
    far = position(listed[:, LSEL:])[1]

    query_weight, key_weight, value_weight = weights
    query = project_columns(query_weight, own, HD**-0.5)
    both = lambda pieces: (
        [project_rows(rows, key_weight) for rows in pieces],
        [project_columns(value_weight, rows) for rows in pieces],
    )
    near_keys, near_values = both(near_rows)
    far_keys, far_values = both(far_rows)
    state = attend("attend_near", near, query, near_keys, near_values, [], False, 2, 4)
    state, late = late_rows(state)
    late_keys, late_values = both(late)
    mixed = attend("attend_far", far, query, far_keys + late_keys, far_values + late_values, state, True, 2, 4)
    out = jnp.dot(mixed, out_weight, preferred_element_type=jnp.float32).astype(jnp.bfloat16)
    return out.reshape(tokens.shape)


def solution(mesh):
    return jax.shard_map(
        on_device,
        mesh=mesh,
        in_specs=(P(("batch", "blk"), "head", None), P(), P(), P(("batch", "blk"), None)),
        out_specs=P(("batch", "blk"), "head", None),
        check_vma=False,
    )
```

```python
import functools

import jax
import jax.numpy as jnp
from jax import lax
from jax.experimental import pallas as pl
from jax.experimental.pallas import tpu as pltpu
from jax.sharding import PartitionSpec as P

D = 1024
H = 16
HD = 64
BLK = 128
REACH = 8
LSEL = 6
SUMB = 4
SB = 16
KSEL = 16
PAIRS = H // 2
LANES = 2 * HD
TOTAL_CAP = 2.0**100


def split_kernel(weight_ref, query_ref, key_ref, value_ref):
    both = weight_ref[...]
    first, second = both[:, : 3 * HD], both[:, 3 * HD :]

    def columns(which):
        lo = which * HD
        return jnp.concatenate([first[:, lo : lo + HD], second[:, lo : lo + HD]], axis=1)

    query_ref[...] = columns(0).T
    key_ref[...] = columns(1)
    value_ref[...] = columns(2).T


def split_weights(proj_weight):
    wide = jax.ShapeDtypeStruct((D, D), jnp.bfloat16)
    across = pl.BlockSpec((LANES, D), lambda p: (p, 0))
    down = pl.BlockSpec((D, LANES), lambda p: (0, p))
    return pl.pallas_call(
        split_kernel,
        grid=(PAIRS,),
        in_specs=[pl.BlockSpec((D, 3 * LANES), lambda p: (0, p))],
        out_specs=[across, down, across],
        out_shape=[wide, wide, wide],
        cost_estimate=pl.CostEstimate(flops=0, bytes_accessed=4 * D * 3 * D, transcendentals=0),
        name="split_weights",
    )(proj_weight)


def attend_kernel(first, last, blocks, count, together, chunk, pieces, *refs):
    f32, bf16 = jnp.float32, jnp.bfloat16
    refs = list(refs)
    table_ref, query_ref = refs[:2]
    key_refs = refs[2 : 2 + pieces]
    value_refs = refs[2 + pieces : 2 + 2 * pieces]
    refs = refs[2 + 2 * pieces :]
    if not first:
        sum_in_ref, row_in_ref = refs[:2]
        refs = refs[2:]
    if last:
        out_ref = refs.pop(0)
    else:
        sum_out_ref, row_out_ref = refs[:2]
        refs = refs[2:]
    if first:
        shift_ref = refs.pop()
    if pieces == 1:
        key_ref, value_ref = key_refs[0], value_refs[0]
    else:
        key_ref, value_ref = refs
        start = 0
        for key_piece, value_piece in zip(key_refs, value_refs):
            size = key_piece.shape[0]
            key_ref[start : start + size, :] = key_piece[...]
            value_ref[:, start : start + size] = value_piece[...]
            start += size

    row = lax.broadcasted_iota(jnp.int32, (LANES, BLK), 0)

    def at(index, size=BLK):
        return pl.ds(pl.multiple_of(index * size, size), size)

    def queries(index):
        own = query_ref[:, at(index)]
        zero = jnp.zeros_like(own)
        return jnp.concatenate([jnp.where(row < HD, own, zero), jnp.where(row < HD, zero, own)], axis=1)

    def places(index, which, size):
        return [pl.multiple_of(table_ref[index, which + n] * BLK, BLK) for n in range(size)]

    def score(index, which, size, query):
        keys = [key_ref[pl.ds(place, BLK), :] for place in places(index, which, size)]
        return jnp.dot(jnp.concatenate(keys, axis=0), query, preferred_element_type=f32)

    def values(index, which, size):
        return jnp.concatenate([value_ref[:, pl.ds(place, BLK)] for place in places(index, which, size)], axis=1)

    def gather(picked, raised):
        ones = jnp.ones((16, raised.shape[0]), bf16)
        return jnp.dot(jnp.concatenate([picked, ones], axis=0), raised, preferred_element_type=f32)

    def by_head(rows):
        return jnp.where(row < HD, rows[:, :BLK], rows[:, BLK:])

    def finish(index, shift, total, rescale=None):
        mine = jnp.concatenate([total[:HD, :BLK], total[HD:LANES, BLK:]], axis=0)
        count_all = total[LANES : LANES + 1]
        if not first:
            before = sum_in_ref[:, at(index)]
            count_before = row_in_ref[0, 1:2, at(index, 2 * BLK)]
            if rescale is not None:
                before = before * by_head(rescale)
                count_before = count_before * rescale
            mine = mine + before
            count_all = count_all + count_before
        if last:
            out_ref[at(index), :] = (mine * by_head(1.0 / count_all)).T.astype(bf16)
        else:
            sum_out_ref[:, at(index)] = mine
            row_out_ref[0, 0:1, at(index, 2 * BLK)] = shift
            row_out_ref[0, 1:2, at(index, 2 * BLK)] = count_all
        return count_all

    def whole_row(index):
        query = queries(index)
        shift = jnp.full((1, 2 * BLK), -jnp.inf, f32) if first else row_in_ref[0, 0:1, at(index, 2 * BLK)]
        old = shift

        def largest(n, shift):
            return jnp.maximum(shift, jnp.max(score(index, 2 * n, 2, query), axis=0, keepdims=True))

        shift = lax.fori_loop(0, count // 2, largest, shift)

        def add(n, total):
            raised = jnp.exp(score(index, 2 * n, 2, query) - shift).astype(bf16)
            return total + gather(values(index, 2 * n, 2), raised)

        total = lax.fori_loop(0, count // 2, add, jnp.zeros((LANES + 16, 2 * BLK), f32))
        finish(index, shift, total, None if first else jnp.exp(old - shift))

    def one(index):
        query = queries(index)
        total = None
        shift = shift_ref[pl.ds(index, 1), :] if first else row_in_ref[0, 0:1, at(index, 2 * BLK)]
        for which in range(0, count, chunk):
            size = min(chunk, count - which)
            scores = score(index, which, size, query)
            part = gather(values(index, which, size), jnp.exp(scores - shift).astype(bf16))
            total = part if total is None else total + part
        return finish(index, shift, total)

    if first:
        for index in range(blocks):
            shift_ref[index : index + 1, :] = jnp.max(score(index, 0, 1, queries(index)), axis=0, keepdims=True)

    def body(number, peak):
        for n in range(together):
            peak = jnp.maximum(peak, one(number * together + n))
        return peak

    peak = lax.fori_loop(0, blocks // together, body, jnp.zeros((1, 2 * BLK), f32))

    @pl.when(jnp.logical_not(jnp.max(peak) <= TOTAL_CAP))
    def _():
        lax.fori_loop(0, blocks, lambda index, carry: (whole_row(index), carry)[1], 0)


def attend(name, table, query, keys, values, state, last, together, chunk):
    f32, bf16 = jnp.float32, jnp.bfloat16
    rows = query.shape[1]
    blocks = rows // BLK
    count = table.shape[1]
    while blocks % together:
        together //= 2
    total_rows = sum(key.shape[0] for key in keys)
    across = lambda array: pl.BlockSpec((LANES, array.shape[1]), lambda p: (p, 0))
    down = lambda array: pl.BlockSpec((array.shape[0], LANES), lambda p: (0, p))
    per_row = pl.BlockSpec((1, 2, 2 * rows), lambda p: (p, 0, 0))
    in_specs = [pl.BlockSpec(memory_space=pltpu.SMEM), across(query)]
    in_specs += [down(key) for key in keys] + [across(value) for value in values]
    if state:
        in_specs += [across(query), per_row]
    if last:
        out_specs = pl.BlockSpec((rows, LANES), lambda p: (0, p))
        out_shape = jax.ShapeDtypeStruct((rows, D), bf16)
    else:
        out_specs = [across(query), per_row]
        out_shape = [jax.ShapeDtypeStruct((D, rows), f32), jax.ShapeDtypeStruct((PAIRS, 2, 2 * rows), f32)]
    scratch = [pltpu.VMEM((total_rows, LANES), bf16), pltpu.VMEM((LANES, total_rows), bf16)]
    scratch = scratch if len(keys) > 1 else []
    if not state:
        scratch.append(pltpu.VMEM((blocks, 2 * BLK), f32))
    scores = rows * count * BLK * H
    return pl.pallas_call(
        functools.partial(attend_kernel, not state, last, blocks, count, together, chunk, len(keys)),
        grid=(PAIRS,),
        in_specs=in_specs,
        out_specs=out_specs,
        out_shape=out_shape,
        scratch_shapes=scratch,
        compiler_params=pltpu.CompilerParams(vmem_limit_bytes=18 * 2**20),
        cost_estimate=pl.CostEstimate(
            flops=24 * scores * HD, bytes_accessed=4 * total_rows * D + 10 * rows * D, transcendentals=scores
        ),
        name=name,
    )(table, query, *keys, *values, *state)


def project_rows(rows, weight):
    return jnp.dot(rows, weight, preferred_element_type=jnp.float32).astype(jnp.bfloat16)


def project_columns(weight, rows, scale=1.0):
    wide = lax.dot_general(weight, rows, (((1,), (1,)), ((), ())), preferred_element_type=jnp.float32)
    return (wide * scale).astype(jnp.bfloat16)


def rows_by_axes(own, weights, place, stride, strides):
    summary = SUMB * BLK
    half = summary // 2
    cut = own.shape[0] - summary
    chips = strides // 2
    low = place == 0
    swap = lambda rows: lax.ppermute(rows, "head", [(0, 1), (1, 0)])
    beside = lambda rows: lax.ppermute(rows, "blk", [(s, s ^ 1) for s in range(strides)])

    def along(rows, k):
        return lax.ppermute(rows, "blk", [(s, (s + 2 * k) % strides) for s in range(strides)])

    steps = []
    for s in range(strides - 1):
        steps += [(s, s + 1), (strides + s + 1, strides + s)]
    to_next = lambda rows: lax.ppermute(rows, ("head", "blk"), steps)

    other_end = swap(own[-half:])
    other_end, own, weights = lax.optimization_barrier((other_end, own, weights))
    carried = jnp.where(low, other_end, own[cut : cut + half])
    other = swap(own[:-half])
    slots = [along(carried, k) for k in range(1, chips)]
    edge_end = to_next(other_end)
    own, other, other_end = lax.optimization_barrier((own, other, other_end))
    query = project_columns(weights[0], own, HD**-0.5)
    query, *slots = lax.optimization_barrier((query, *slots))
    across = [swap(rows) for rows in slots]
    foreign = jnp.concatenate(slots, axis=0)
    nearby = jnp.where(low, jnp.concatenate([other_end, other[-half:]], axis=0), own[cut:])
    near_rows = [own, other, other_end, to_next(other), edge_end]
    far_rows = [nearby, beside(nearby), foreign, beside(foreign)]
    span = 2 * (chips - 1)

    def late_rows(state):
        state, arrived = lax.optimization_barrier((state, across))
        arrived = jnp.concatenate(arrived, axis=0)
        return state, [arrived, beside(arrived)]

    def position(block):
        of, inside = block // SB, block % SB
        rel = block - stride * SB
        mine = inside % 8 + jnp.where(inside // 8 == place, 0, 8)
        edge = jnp.where(rel < 0, rel + SB + 8, rel)
        order = inside - (SB - SUMB)
        k = (stride // 2 - of // 2) % chips
        turned = (order // 2 ^ (1 - place)) * 2 + order % 2
        beside_me = jnp.where(of % 2 == stride % 2, 0, 1)
        part = beside_me + jnp.where(order // 2 == 1 - place, 0, 2)
        far = jnp.where(k == 0, 4 * beside_me + turned, 8 + part * span + (k - 1) * 2 + order % 2)
        return jnp.where(of == stride, mine, edge), far

    return near_rows, far_rows, late_rows, weights, query, position


def rows_by_gather(own, place, stride, strides, heads):
    summary = SUMB * BLK
    share = summary // heads
    lower = place < heads // 2
    stride_rows = lax.all_gather(own, "head", axis=0, tiled=True)
    piece = lax.dynamic_slice_in_dim(stride_rows[-summary:], place * share, share, 0)
    far_rows = lax.all_gather(piece, ("blk", "head"), axis=0, tiled=True)
    half = stride_rows.shape[0] // 2
    steps = []
    for h in range(heads):
        for s in range(strides - 1):
            ends = (h * strides + s, h * strides + s + 1)
            steps.append(ends if h < heads // 2 else ends[::-1])
    edge = lax.ppermute(jnp.where(lower, stride_rows[half:], stride_rows[:half]), ("head", "blk"), steps)

    def position(block):
        rel = block - stride * SB
        near = jnp.where(rel < 0, rel + SB + REACH, rel)
        return near, block // SB * SUMB + block % SB - (SB - SUMB)

    return [stride_rows, edge], [far_rows], lambda state: (state, []), position


def on_device(tokens, proj_weight, out_weight, pattern):
    heads = lax.axis_size("head")
    strides = lax.axis_size("blk")
    place = lax.axis_index("head")
    stride = lax.axis_index("blk")
    own = tokens[0]
    blocks = own.shape[0] // BLK
    weights = split_weights(proj_weight)

    if heads == 2:
        near_rows, far_rows, late_rows, weights, query, position = rows_by_axes(
            own, weights, place, stride, strides
        )
    else:
        near_rows, far_rows, late_rows, position = rows_by_gather(own, place, stride, strides, heads)
        query = project_columns(weights[0], own, HD**-0.5)
    listed = lax.dynamic_slice_in_dim(pattern, place * blocks, blocks, 0)
    near = position(listed[:, :LSEL])[0]
    far = position(listed[:, LSEL:])[1]

    _, key_weight, value_weight = weights
    both = lambda pieces: (
        [project_rows(rows, key_weight) for rows in pieces],
        [project_columns(value_weight, rows) for rows in pieces],
    )
    near_keys, near_values = both(near_rows)
    far_keys, far_values = both(far_rows)
    state = attend("attend_near", near, query, near_keys, near_values, [], False, 2, 4)
    state, late = late_rows(state)
    late_keys, late_values = both(late)
    mixed = attend("attend_far", far, query, far_keys + late_keys, far_values + late_values, state, True, 2, 4)
    out = jnp.dot(mixed, out_weight, preferred_element_type=jnp.float32).astype(jnp.bfloat16)
    return out.reshape(tokens.shape)


def solution(mesh):
    return jax.shard_map(
        on_device,
        mesh=mesh,
        in_specs=(P(("batch", "blk"), "head", None), P(), P(), P(("batch", "blk"), None)),
        out_specs=P(("batch", "blk"), "head", None),
        check_vma=False,
    )
```

```python
import functools

import jax
import jax.numpy as jnp
from jax import lax
from jax.experimental import pallas as pl
from jax.experimental.pallas import tpu as pltpu
from jax.sharding import PartitionSpec as P

D = 1024
H = 16
HD = 64
BLK = 128
REACH = 8
LSEL = 6
SUMB = 4
SB = 16
KSEL = 16
PAIRS = H // 2
LANES = 2 * HD
TOTAL_CAP = 2.0**100


def split_kernel(weight_ref, query_ref, key_ref, value_ref):
    both = weight_ref[...]
    first, second = both[:, : 3 * HD], both[:, 3 * HD :]

    def columns(which):
        lo = which * HD
        return jnp.concatenate([first[:, lo : lo + HD], second[:, lo : lo + HD]], axis=1)

    query_ref[...] = columns(0).T
    key_ref[...] = columns(1)
    value_ref[...] = columns(2).T


def split_weights(proj_weight):
    wide = jax.ShapeDtypeStruct((D, D), jnp.bfloat16)
    across = pl.BlockSpec((LANES, D), lambda p: (p, 0))
    down = pl.BlockSpec((D, LANES), lambda p: (0, p))
    return pl.pallas_call(
        split_kernel,
        grid=(PAIRS,),
        in_specs=[pl.BlockSpec((D, 3 * LANES), lambda p: (0, p))],
        out_specs=[across, down, across],
        out_shape=[wide, wide, wide],
        cost_estimate=pl.CostEstimate(flops=0, bytes_accessed=4 * D * 3 * D, transcendentals=0),
        name="split_weights",
    )(proj_weight)


def attend_kernel(first, last, blocks, count, together, chunk, pieces, *refs):
    f32, bf16 = jnp.float32, jnp.bfloat16
    refs = list(refs)
    table_ref, query_ref = refs[:2]
    key_refs = refs[2 : 2 + pieces]
    value_refs = refs[2 + pieces : 2 + 2 * pieces]
    refs = refs[2 + 2 * pieces :]
    if not first:
        sum_in_ref, row_in_ref = refs[:2]
        refs = refs[2:]
    if last:
        out_ref = refs.pop(0)
    else:
        sum_out_ref, row_out_ref = refs[:2]
        refs = refs[2:]
    if first:
        shift_ref = refs.pop()
    if pieces == 1:
        key_ref, value_ref = key_refs[0], value_refs[0]
    else:
        key_ref, value_ref = refs
        start = 0
        for key_piece, value_piece in zip(key_refs, value_refs):
            size = key_piece.shape[0]
            key_ref[start : start + size, :] = key_piece[...]
            value_ref[:, start : start + size] = value_piece[...]
            start += size

    row = lax.broadcasted_iota(jnp.int32, (LANES, BLK), 0)

    def at(index, size=BLK):
        return pl.ds(pl.multiple_of(index * size, size), size)

    def queries(index):
        own = query_ref[:, at(index)]
        zero = jnp.zeros_like(own)
        return jnp.concatenate([jnp.where(row < HD, own, zero), jnp.where(row < HD, zero, own)], axis=1)

    def places(index, which, size):
        return [pl.multiple_of(table_ref[index, which + n] * BLK, BLK) for n in range(size)]

    def score(index, which, size, query):
        keys = [key_ref[pl.ds(place, BLK), :] for place in places(index, which, size)]
        return jnp.dot(jnp.concatenate(keys, axis=0), query, preferred_element_type=f32)

    def values(index, which, size):
        return jnp.concatenate([value_ref[:, pl.ds(place, BLK)] for place in places(index, which, size)], axis=1)

    def gather(picked, raised):
        ones = jnp.ones((16, raised.shape[0]), bf16)
        return jnp.dot(jnp.concatenate([picked, ones], axis=0), raised, preferred_element_type=f32)

    def by_head(rows):
        return jnp.where(row < HD, rows[:, :BLK], rows[:, BLK:])

    def finish(index, shift, total, rescale=None):
        mine = jnp.concatenate([total[:HD, :BLK], total[HD:LANES, BLK:]], axis=0)
        count_all = total[LANES : LANES + 1]
        if not first:
            before = sum_in_ref[:, at(index)]
            count_before = row_in_ref[0, 1:2, at(index, 2 * BLK)]
            if rescale is not None:
                before = before * by_head(rescale)
                count_before = count_before * rescale
            mine = mine + before
            count_all = count_all + count_before
        if last:
            out_ref[at(index), :] = (mine * by_head(1.0 / count_all)).T.astype(bf16)
        else:
            sum_out_ref[:, at(index)] = mine
            row_out_ref[0, 0:1, at(index, 2 * BLK)] = shift
            row_out_ref[0, 1:2, at(index, 2 * BLK)] = count_all
        return count_all

    def whole_row(index):
        query = queries(index)
        shift = jnp.full((1, 2 * BLK), -jnp.inf, f32) if first else row_in_ref[0, 0:1, at(index, 2 * BLK)]
        old = shift

        def largest(n, shift):
            return jnp.maximum(shift, jnp.max(score(index, 2 * n, 2, query), axis=0, keepdims=True))

        shift = lax.fori_loop(0, count // 2, largest, shift)

        def add(n, total):
            raised = jnp.exp(score(index, 2 * n, 2, query) - shift).astype(bf16)
            return total + gather(values(index, 2 * n, 2), raised)

        total = lax.fori_loop(0, count // 2, add, jnp.zeros((LANES + 16, 2 * BLK), f32))
        finish(index, shift, total, None if first else jnp.exp(old - shift))

    def one(index):
        query = queries(index)
        total = None
        shift = shift_ref[pl.ds(index, 1), :] if first else row_in_ref[0, 0:1, at(index, 2 * BLK)]
        for which in range(0, count, chunk):
            size = min(chunk, count - which)
            scores = score(index, which, size, query)
            part = gather(values(index, which, size), jnp.exp(scores - shift).astype(bf16))
            total = part if total is None else total + part
        return finish(index, shift, total)

    if first:
        for index in range(blocks):
            shift_ref[index : index + 1, :] = jnp.max(score(index, 0, 1, queries(index)), axis=0, keepdims=True)

    def body(number, peak):
        for n in range(together):
            peak = jnp.maximum(peak, one(number * together + n))
        return peak

    peak = lax.fori_loop(0, blocks // together, body, jnp.zeros((1, 2 * BLK), f32))

    @pl.when(jnp.logical_not(jnp.max(peak) <= TOTAL_CAP))
    def _():
        lax.fori_loop(0, blocks, lambda index, carry: (whole_row(index), carry)[1], 0)


def attend(name, table, query, keys, values, state, last, together, chunk):
    f32, bf16 = jnp.float32, jnp.bfloat16
    rows = query.shape[1]
    blocks = rows // BLK
    count = table.shape[1]
    while blocks % together:
        together //= 2
    total_rows = sum(key.shape[0] for key in keys)
    across = lambda array: pl.BlockSpec((LANES, array.shape[1]), lambda p: (p, 0))
    down = lambda array: pl.BlockSpec((array.shape[0], LANES), lambda p: (0, p))
    per_row = pl.BlockSpec((1, 2, 2 * rows), lambda p: (p, 0, 0))
    in_specs = [pl.BlockSpec(memory_space=pltpu.SMEM), across(query)]
    in_specs += [down(key) for key in keys] + [across(value) for value in values]
    if state:
        in_specs += [across(query), per_row]
    if last:
        out_specs = pl.BlockSpec((rows, LANES), lambda p: (0, p))
        out_shape = jax.ShapeDtypeStruct((rows, D), bf16)
    else:
        out_specs = [across(query), per_row]
        out_shape = [jax.ShapeDtypeStruct((D, rows), f32), jax.ShapeDtypeStruct((PAIRS, 2, 2 * rows), f32)]
    scratch = [pltpu.VMEM((total_rows, LANES), bf16), pltpu.VMEM((LANES, total_rows), bf16)]
    scratch = scratch if len(keys) > 1 else []
    if not state:
        scratch.append(pltpu.VMEM((blocks, 2 * BLK), f32))
    scores = rows * count * BLK * H
    return pl.pallas_call(
        functools.partial(attend_kernel, not state, last, blocks, count, together, chunk, len(keys)),
        grid=(PAIRS,),
        in_specs=in_specs,
        out_specs=out_specs,
        out_shape=out_shape,
        scratch_shapes=scratch,
        compiler_params=pltpu.CompilerParams(vmem_limit_bytes=18 * 2**20),
        cost_estimate=pl.CostEstimate(
            flops=24 * scores * HD, bytes_accessed=4 * total_rows * D + 10 * rows * D, transcendentals=scores
        ),
        name=name,
    )(table, query, *keys, *values, *state)


def project_rows(rows, weight):
    return jnp.dot(rows, weight, preferred_element_type=jnp.float32).astype(jnp.bfloat16)


def project_columns(weight, rows, scale=1.0):
    wide = lax.dot_general(weight, rows, (((1,), (1,)), ((), ())), preferred_element_type=jnp.float32)
    return (wide * scale).astype(jnp.bfloat16)


def rows_by_axes(own, weights, place, stride, strides):
    summary = SUMB * BLK
    half = summary // 2
    cut = own.shape[0] - summary
    chips = strides // 2
    low = place == 0
    swap = lambda rows: lax.ppermute(rows, "head", [(0, 1), (1, 0)])
    beside = lambda rows: lax.ppermute(rows, "blk", [(s, s ^ 1) for s in range(strides)])

    def along(rows, k):
        return lax.ppermute(rows, "blk", [(s, (s + 2 * k) % strides) for s in range(strides)])

    steps = []
    for s in range(strides - 1):
        steps += [(s, s + 1), (strides + s + 1, strides + s)]
    to_next = lambda rows: lax.ppermute(rows, ("head", "blk"), steps)

    other_end = swap(own[-half:])
    other_end, own, weights = lax.optimization_barrier((other_end, own, weights))
    carried = jnp.where(low, other_end, own[cut : cut + half])
    other = swap(own[:-half])
    edge_end = to_next(other_end)
    ends = {1, chips - 1}
    slots = {k: along(carried, k) for k in ends}
    slots, after, own, other_end = lax.optimization_barrier((slots, carried, own, other_end))
    middle = {k: along(after, k) for k in range(2, chips - 1)}
    query = project_columns(weights[0], own, HD**-0.5)
    across = {k: swap(slots[k]) for k in ends}
    middle, other = lax.optimization_barrier((middle, other))
    edge = to_next(other)
    last, edge = lax.optimization_barrier(({k: swap(rows) for k, rows in middle.items()}, edge))
    slots.update(middle)
    across.update(last)
    across = [across[k] for k in range(1, chips)]
    slots = [slots[k] for k in range(1, chips)]
    foreign = jnp.concatenate(slots, axis=0)
    nearby = jnp.where(low, jnp.concatenate([other_end, other[-half:]], axis=0), own[cut:])
    pieces = [own, other, other_end, edge, edge_end, beside(nearby), foreign, beside(foreign)]
    pieces += across + [beside(rows) for rows in across]
    span = 2 * (chips - 1)

    def position(block):
        of, inside = block // SB, block % SB
        rel = block - stride * SB
        mine = inside % 8 + jnp.where(inside // 8 == place, 0, 8)
        edge = jnp.where(rel < 0, rel + SB + 8, rel)
        order = inside - (SB - SUMB)
        k = (stride // 2 - of // 2) % chips
        turned = (order // 2 ^ (1 - place)) * 2 + order % 2
        part = jnp.where(of % 2 == stride % 2, 0, 1) + jnp.where(order // 2 == 1 - place, 0, 2)
        far = jnp.where(k == 0, 24 + turned, 28 + part * span + (k - 1) * 2 + order % 2)
        return jnp.where(of == stride, mine, edge), jnp.where(of == stride, mine, far)

    return pieces, weights, query, position


def rows_by_gather(own, place, stride, strides, heads):
    summary = SUMB * BLK
    share = summary // heads
    lower = place < heads // 2
    stride_rows = lax.all_gather(own, "head", axis=0, tiled=True)
    piece = lax.dynamic_slice_in_dim(stride_rows[-summary:], place * share, share, 0)
    far_rows = lax.all_gather(piece, ("blk", "head"), axis=0, tiled=True)
    half = stride_rows.shape[0] // 2
    steps = []
    for h in range(heads):
        for s in range(strides - 1):
            ends = (h * strides + s, h * strides + s + 1)
            steps.append(ends if h < heads // 2 else ends[::-1])
    edge = lax.ppermute(jnp.where(lower, stride_rows[half:], stride_rows[:half]), ("head", "blk"), steps)

    def position(block):
        rel = block - stride * SB
        near = jnp.where(rel < 0, rel + SB + REACH, rel)
        return near, SB + REACH + block // SB * SUMB + block % SB - (SB - SUMB)

    return [stride_rows, edge, far_rows], position


def on_device(tokens, proj_weight, out_weight, pattern):
    heads = lax.axis_size("head")
    strides = lax.axis_size("blk")
    place = lax.axis_index("head")
    stride = lax.axis_index("blk")
    own = tokens[0]
    blocks = own.shape[0] // BLK
    weights = split_weights(proj_weight)

    if heads == 2:
        pieces, weights, query, position = rows_by_axes(own, weights, place, stride, strides)
    else:
        pieces, position = rows_by_gather(own, place, stride, strides, heads)
        query = project_columns(weights[0], own, HD**-0.5)
    listed = lax.dynamic_slice_in_dim(pattern, place * blocks, blocks, 0)
    near, far = position(listed)
    table = jnp.where(lax.broadcasted_iota(jnp.int32, listed.shape, 1) < LSEL, near, far)

    _, key_weight, value_weight = weights
    keys = [project_rows(rows, key_weight) for rows in pieces]
    values = [project_columns(value_weight, rows) for rows in pieces]
    mixed = attend("attend", table, query, keys, values, [], True, 2, 4)
    out = jnp.dot(mixed, out_weight, preferred_element_type=jnp.float32).astype(jnp.bfloat16)
    return out.reshape(tokens.shape)


def solution(mesh):
    return jax.shard_map(
        on_device,
        mesh=mesh,
        in_specs=(P(("batch", "blk"), "head", None), P(), P(), P(("batch", "blk"), None)),
        out_specs=P(("batch", "blk"), "head", None),
        check_vma=False,
    )
```

```python
import functools

import jax
import jax.numpy as jnp
from jax import lax
from jax.experimental import pallas as pl
from jax.experimental.pallas import tpu as pltpu
from jax.sharding import PartitionSpec as P

D = 1024
H = 16
HD = 64
BLK = 128
REACH = 8
LSEL = 6
SUMB = 4
SB = 16
KSEL = 16
PAIRS = H // 2
LANES = 2 * HD
TOTAL_CAP = 2.0**100


def split_kernel(weight_ref, query_ref, key_ref, value_ref):
    both = weight_ref[...]
    first, second = both[:, : 3 * HD], both[:, 3 * HD :]

    def columns(which):
        lo = which * HD
        return jnp.concatenate([first[:, lo : lo + HD], second[:, lo : lo + HD]], axis=1)

    query_ref[...] = columns(0).T
    key_ref[...] = columns(1)
    value_ref[...] = columns(2).T


def split_weights(proj_weight):
    wide = jax.ShapeDtypeStruct((D, D), jnp.bfloat16)
    across = pl.BlockSpec((LANES, D), lambda p: (p, 0))
    down = pl.BlockSpec((D, LANES), lambda p: (0, p))
    return pl.pallas_call(
        split_kernel,
        grid=(PAIRS,),
        in_specs=[pl.BlockSpec((D, 3 * LANES), lambda p: (0, p))],
        out_specs=[across, down, across],
        out_shape=[wide, wide, wide],
        cost_estimate=pl.CostEstimate(flops=0, bytes_accessed=4 * D * 3 * D, transcendentals=0),
        name="split_weights",
    )(proj_weight)


def attend_kernel(first, last, blocks, count, together, chunk, pieces, *refs):
    f32, bf16 = jnp.float32, jnp.bfloat16
    refs = list(refs)
    table_ref, query_ref = refs[:2]
    key_refs = refs[2 : 2 + pieces]
    value_refs = refs[2 + pieces : 2 + 2 * pieces]
    refs = refs[2 + 2 * pieces :]
    if not first:
        sum_in_ref, row_in_ref = refs[:2]
        refs = refs[2:]
    if last:
        out_ref = refs.pop(0)
    else:
        sum_out_ref, row_out_ref = refs[:2]
        refs = refs[2:]
    if first:
        shift_ref = refs.pop()
    if pieces == 1:
        key_ref, value_ref = key_refs[0], value_refs[0]
    else:
        key_ref, value_ref = refs
        start = 0
        for key_piece, value_piece in zip(key_refs, value_refs):
            size = key_piece.shape[0]
            key_ref[start : start + size, :] = key_piece[...]
            value_ref[:, start : start + size] = value_piece[...]
            start += size

    row = lax.broadcasted_iota(jnp.int32, (LANES, BLK), 0)

    def at(index, size=BLK):
        return pl.ds(pl.multiple_of(index * size, size), size)

    def queries(index):
        own = query_ref[:, at(index)]
        zero = jnp.zeros_like(own)
        return jnp.concatenate([jnp.where(row < HD, own, zero), jnp.where(row < HD, zero, own)], axis=1)

    def places(index, which, size):
        return [pl.multiple_of(table_ref[index, which + n] * BLK, BLK) for n in range(size)]

    def score(index, which, size, query):
        keys = [key_ref[pl.ds(place, BLK), :] for place in places(index, which, size)]
        return jnp.dot(jnp.concatenate(keys, axis=0), query, preferred_element_type=f32)

    def values(index, which, size):
        return jnp.concatenate([value_ref[:, pl.ds(place, BLK)] for place in places(index, which, size)], axis=1)

    def gather(picked, raised):
        ones = jnp.ones((16, raised.shape[0]), bf16)
        return jnp.dot(jnp.concatenate([picked, ones], axis=0), raised, preferred_element_type=f32)

    def by_head(rows):
        return jnp.where(row < HD, rows[:, :BLK], rows[:, BLK:])

    def finish(index, shift, total, rescale=None):
        mine = jnp.concatenate([total[:HD, :BLK], total[HD:LANES, BLK:]], axis=0)
        count_all = total[LANES : LANES + 1]
        if not first:
            before = sum_in_ref[:, at(index)]
            count_before = row_in_ref[0, 1:2, at(index, 2 * BLK)]
            if rescale is not None:
                before = before * by_head(rescale)
                count_before = count_before * rescale
            mine = mine + before
            count_all = count_all + count_before
        if last:
            out_ref[at(index), :] = (mine * by_head(1.0 / count_all)).T.astype(bf16)
        else:
            sum_out_ref[:, at(index)] = mine
            row_out_ref[0, 0:1, at(index, 2 * BLK)] = shift
            row_out_ref[0, 1:2, at(index, 2 * BLK)] = count_all
        return count_all

    def whole_row(index):
        query = queries(index)
        shift = jnp.full((1, 2 * BLK), -jnp.inf, f32) if first else row_in_ref[0, 0:1, at(index, 2 * BLK)]
        old = shift

        def largest(n, shift):
            return jnp.maximum(shift, jnp.max(score(index, 2 * n, 2, query), axis=0, keepdims=True))

        shift = lax.fori_loop(0, count // 2, largest, shift)

        def add(n, total):
            raised = jnp.exp(score(index, 2 * n, 2, query) - shift).astype(bf16)
            return total + gather(values(index, 2 * n, 2), raised)

        total = lax.fori_loop(0, count // 2, add, jnp.zeros((LANES + 16, 2 * BLK), f32))
        finish(index, shift, total, None if first else jnp.exp(old - shift))

    def one(index):
        query = queries(index)
        total = None
        shift = shift_ref[pl.ds(index, 1), :] if first else row_in_ref[0, 0:1, at(index, 2 * BLK)]
        for which in range(0, count, chunk):
            size = min(chunk, count - which)
            scores = score(index, which, size, query)
            part = gather(values(index, which, size), jnp.exp(scores - shift).astype(bf16))
            total = part if total is None else total + part
        return finish(index, shift, total)

    if first:
        for index in range(blocks):
            shift_ref[index : index + 1, :] = jnp.max(score(index, 0, 1, queries(index)), axis=0, keepdims=True)

    def body(number, peak):
        for n in range(together):
            peak = jnp.maximum(peak, one(number * together + n))
        return peak

    peak = lax.fori_loop(0, blocks // together, body, jnp.zeros((1, 2 * BLK), f32))

    @pl.when(jnp.logical_not(jnp.max(peak) <= TOTAL_CAP))
    def _():
        lax.fori_loop(0, blocks, lambda index, carry: (whole_row(index), carry)[1], 0)


def attend(name, table, query, keys, values, state, last, together, chunk):
    f32, bf16 = jnp.float32, jnp.bfloat16
    rows = query.shape[1]
    blocks = rows // BLK
    count = table.shape[1]
    while blocks % together:
        together //= 2
    total_rows = sum(key.shape[0] for key in keys)
    across = lambda array: pl.BlockSpec((LANES, array.shape[1]), lambda p: (p, 0))
    down = lambda array: pl.BlockSpec((array.shape[0], LANES), lambda p: (0, p))
    per_row = pl.BlockSpec((1, 2, 2 * rows), lambda p: (p, 0, 0))
    in_specs = [pl.BlockSpec(memory_space=pltpu.SMEM), across(query)]
    in_specs += [down(key) for key in keys] + [across(value) for value in values]
    if state:
        in_specs += [across(query), per_row]
    if last:
        out_specs = pl.BlockSpec((rows, LANES), lambda p: (0, p))
        out_shape = jax.ShapeDtypeStruct((rows, D), bf16)
    else:
        out_specs = [across(query), per_row]
        out_shape = [jax.ShapeDtypeStruct((D, rows), f32), jax.ShapeDtypeStruct((PAIRS, 2, 2 * rows), f32)]
    scratch = [pltpu.VMEM((total_rows, LANES), bf16), pltpu.VMEM((LANES, total_rows), bf16)]
    scratch = scratch if len(keys) > 1 else []
    if not state:
        scratch.append(pltpu.VMEM((blocks, 2 * BLK), f32))
    scores = rows * count * BLK * H
    return pl.pallas_call(
        functools.partial(attend_kernel, not state, last, blocks, count, together, chunk, len(keys)),
        grid=(PAIRS,),
        in_specs=in_specs,
        out_specs=out_specs,
        out_shape=out_shape,
        scratch_shapes=scratch,
        compiler_params=pltpu.CompilerParams(vmem_limit_bytes=18 * 2**20),
        cost_estimate=pl.CostEstimate(
            flops=24 * scores * HD, bytes_accessed=4 * total_rows * D + 10 * rows * D, transcendentals=scores
        ),
        name=name,
    )(table, query, *keys, *values, *state)


def project_rows(rows, weight):
    return jnp.dot(rows, weight, preferred_element_type=jnp.float32).astype(jnp.bfloat16)


def project_columns(weight, rows, scale=1.0):
    wide = lax.dot_general(weight, rows, (((1,), (1,)), ((), ())), preferred_element_type=jnp.float32)
    return (wide * scale).astype(jnp.bfloat16)


def rows_by_axes(own, weights, place, stride, strides):
    summary = SUMB * BLK
    half = summary // 2
    cut = own.shape[0] - summary
    chips = strides // 2
    low = place == 0
    swap = lambda rows: lax.ppermute(rows, "head", [(0, 1), (1, 0)])
    beside = lambda rows: lax.ppermute(rows, "blk", [(s, s ^ 1) for s in range(strides)])

    def along(rows, k):
        return lax.ppermute(rows, "blk", [(s, (s + 2 * k) % strides) for s in range(strides)])

    steps = []
    for s in range(strides - 1):
        steps += [(s, s + 1), (strides + s + 1, strides + s)]
    to_next = lambda rows: lax.ppermute(rows, ("head", "blk"), steps)

    other_end = swap(own[-half:])
    other_end, own, weights = lax.optimization_barrier((other_end, own, weights))
    carried = jnp.where(low, other_end, own[cut : cut + half])
    other = swap(own[:-half])
    edge_end = to_next(other_end)
    slots = [along(carried, k) for k in range(1, chips)]
    own, other, other_end = lax.optimization_barrier((own, other, other_end))
    query = project_columns(weights[0], own, HD**-0.5)
    edge = to_next(other)
    query, *slots = lax.optimization_barrier((query, *slots))
    across, edge = lax.optimization_barrier(([swap(rows) for rows in slots], edge))
    foreign = jnp.concatenate(slots, axis=0)
    nearby = jnp.where(low, jnp.concatenate([other_end, other[-half:]], axis=0), own[cut:])
    pieces = [own, other, other_end, edge, edge_end, beside(nearby), foreign, beside(foreign)]
    pieces += across + [beside(rows) for rows in across]
    span = 2 * (chips - 1)

    def position(block):
        of, inside = block // SB, block % SB
        rel = block - stride * SB
        mine = inside % 8 + jnp.where(inside // 8 == place, 0, 8)
        edge = jnp.where(rel < 0, rel + SB + 8, rel)
        order = inside - (SB - SUMB)
        k = (stride // 2 - of // 2) % chips
        turned = (order // 2 ^ (1 - place)) * 2 + order % 2
        part = jnp.where(of % 2 == stride % 2, 0, 1) + jnp.where(order // 2 == 1 - place, 0, 2)
        far = jnp.where(k == 0, 24 + turned, 28 + part * span + (k - 1) * 2 + order % 2)
        return jnp.where(of == stride, mine, edge), jnp.where(of == stride, mine, far)

    return pieces, weights, query, position


def rows_by_gather(own, place, stride, strides, heads):
    summary = SUMB * BLK
    share = summary // heads
    lower = place < heads // 2
    stride_rows = lax.all_gather(own, "head", axis=0, tiled=True)
    piece = lax.dynamic_slice_in_dim(stride_rows[-summary:], place * share, share, 0)
    far_rows = lax.all_gather(piece, ("blk", "head"), axis=0, tiled=True)
    half = stride_rows.shape[0] // 2
    steps = []
    for h in range(heads):
        for s in range(strides - 1):
            ends = (h * strides + s, h * strides + s + 1)
            steps.append(ends if h < heads // 2 else ends[::-1])
    edge = lax.ppermute(jnp.where(lower, stride_rows[half:], stride_rows[:half]), ("head", "blk"), steps)

    def position(block):
        rel = block - stride * SB
        near = jnp.where(rel < 0, rel + SB + REACH, rel)
        return near, SB + REACH + block // SB * SUMB + block % SB - (SB - SUMB)

    return [stride_rows, edge, far_rows], position


def on_device(tokens, proj_weight, out_weight, pattern):
    heads = lax.axis_size("head")
    strides = lax.axis_size("blk")
    place = lax.axis_index("head")
    stride = lax.axis_index("blk")
    own = tokens[0]
    blocks = own.shape[0] // BLK
    weights = split_weights(proj_weight)

    if heads == 2:
        pieces, weights, query, position = rows_by_axes(own, weights, place, stride, strides)
    else:
        pieces, position = rows_by_gather(own, place, stride, strides, heads)
        query = project_columns(weights[0], own, HD**-0.5)
    listed = lax.dynamic_slice_in_dim(pattern, place * blocks, blocks, 0)
    near, far = position(listed)
    table = jnp.where(lax.broadcasted_iota(jnp.int32, listed.shape, 1) < LSEL, near, far)

    _, key_weight, value_weight = weights
    keys = [project_rows(rows, key_weight) for rows in pieces]
    values = [project_columns(value_weight, rows) for rows in pieces]
    mixed = attend("attend", table, query, keys, values, [], True, 2, 8)
    out = jnp.dot(mixed, out_weight, preferred_element_type=jnp.float32).astype(jnp.bfloat16)
    return out.reshape(tokens.shape)


def solution(mesh):
    return jax.shard_map(
        on_device,
        mesh=mesh,
        in_specs=(P(("batch", "blk"), "head", None), P(), P(), P(("batch", "blk"), None)),
        out_specs=P(("batch", "blk"), "head", None),
        check_vma=False,
    )
```

```python
import functools

import jax
import jax.numpy as jnp
from jax import lax
from jax.experimental import pallas as pl
from jax.experimental.pallas import tpu as pltpu
from jax.sharding import PartitionSpec as P

D = 1024
H = 16
HD = 64
BLK = 128
REACH = 8
LSEL = 6
SUMB = 4
SB = 16
KSEL = 16
PAIRS = H // 2
LANES = 2 * HD
QUAD = 4
WIDE = QUAD * HD
TOTAL_CAP = 2.0**100


def split_kernel(weight_ref, query_ref, key_ref, value_ref):
    both = weight_ref[...]
    first, second = both[:, : 3 * HD], both[:, 3 * HD :]

    def columns(which):
        lo = which * HD
        return jnp.concatenate([first[:, lo : lo + HD], second[:, lo : lo + HD]], axis=1)

    query_ref[...] = columns(0)
    key_ref[...] = columns(1).T
    value_ref[...] = columns(2)


def split_weights(proj_weight):
    wide = jax.ShapeDtypeStruct((D, D), jnp.bfloat16)
    across = pl.BlockSpec((LANES, D), lambda p: (p, 0))
    down = pl.BlockSpec((D, LANES), lambda p: (0, p))
    return pl.pallas_call(
        split_kernel,
        grid=(PAIRS,),
        in_specs=[pl.BlockSpec((D, 3 * LANES), lambda p: (0, p))],
        out_specs=[down, across, down],
        out_shape=[wide, wide, wide],
        cost_estimate=pl.CostEstimate(flops=0, bytes_accessed=4 * D * 3 * D, transcendentals=0),
        name="split_weights",
    )(proj_weight)


def attend_kernel(blocks, count, chunk, pieces, table_ref, query_ref, *refs):
    f32, bf16 = jnp.float32, jnp.bfloat16
    key_pieces, value_pieces = refs[:pieces], refs[pieces : 2 * pieces]
    out_ref, key_ref, value_ref, arrived = refs[2 * pieces :]
    step, steps = pl.program_id(0), pl.num_programs(0)
    slot = lax.rem(step, 2)

    def copies(quad, slot):
        lanes = pl.ds(pl.multiple_of(quad * WIDE, WIDE), WIDE)
        found, start = [], 0
        for n, (key_piece, value_piece) in enumerate(zip(key_pieces, value_pieces)):
            span = pl.ds(start, value_piece.shape[0])
            found.append(
                pltpu.make_async_copy(key_piece.at[lanes, :], key_ref.at[slot, :, span], arrived.at[slot, 2 * n])
            )
            found.append(
                pltpu.make_async_copy(
                    value_piece.at[:, lanes], value_ref.at[slot, span, :], arrived.at[slot, 2 * n + 1]
                )
            )
            start += value_piece.shape[0]
        return found

    @pl.when(step == 0)
    def _():
        for copy in copies(0, 0):
            copy.start()

    @pl.when(step + 1 < steps)
    def _():
        for copy in copies(step + 1, 1 - slot):
            copy.start()

    for copy in copies(step, slot):
        copy.wait()

    head = lax.broadcasted_iota(jnp.int32, (BLK, WIDE), 1) // HD
    first_half = lax.broadcasted_iota(jnp.int32, (BLK, LANES), 1) < HD

    def at(index):
        return pl.ds(pl.multiple_of(index * BLK, BLK), BLK)

    def queries(index):
        own = query_ref[at(index), :]
        return jnp.concatenate([jnp.where(head == h, own, jnp.zeros_like(own)) for h in range(QUAD)], axis=0)

    def places(index, which, size):
        return [at(table_ref[index, which + n]) for n in range(size)]

    def score(index, which, size, query):
        keys = [key_ref[slot, :, place] for place in places(index, which, size)]
        return jnp.dot(query, jnp.concatenate(keys, axis=1), preferred_element_type=f32)

    def gather(index, which, size, raised):
        picked = jnp.concatenate([value_ref[slot, place, :] for place in places(index, which, size)], axis=0)
        row = raised[:, :BLK]
        for n in range(1, size):
            row = row + raised[:, n * BLK : (n + 1) * BLK]
        return row, jnp.dot(raised.astype(bf16), picked, preferred_element_type=f32)

    def finish(index, row, total):
        count_all = jnp.sum(row, axis=1, keepdims=True)
        scaled = total / count_all
        tiles = []
        for n in range(QUAD // 2):
            span = slice(n * LANES, (n + 1) * LANES)
            one, two = scaled[2 * n * BLK : (2 * n + 1) * BLK, span], scaled[(2 * n + 1) * BLK : (2 * n + 2) * BLK, span]
            tiles.append(jnp.where(first_half, one, two))
        out_ref[at(index), :] = jnp.concatenate(tiles, axis=1).astype(bf16)
        return jnp.max(count_all, axis=0, keepdims=True)

    def body(index, peak):
        query = queries(index)
        row = total = shift = None
        for which in range(0, count, chunk):
            scores = score(index, which, chunk, query)
            if shift is None:
                shift = jnp.max(scores[:, :BLK], axis=1, keepdims=True)
            new_row, new_total = gather(index, which, chunk, jnp.exp(scores - shift))
            row = new_row if row is None else row + new_row
            total = new_total if total is None else total + new_total
        return jnp.maximum(peak, finish(index, row, total))

    peak = lax.fori_loop(0, blocks, body, jnp.zeros((1, 1), f32))

    @pl.when(jnp.logical_not(jnp.max(peak) <= TOTAL_CAP))
    def _():
        def whole_row(index, carry):
            query = queries(index)

            def largest(n, shift):
                return jnp.maximum(shift, jnp.max(score(index, 2 * n, 2, query), axis=1, keepdims=True))

            shift = lax.fori_loop(0, count // 2, largest, jnp.full((QUAD * BLK, 1), -jnp.inf, f32))

            def add(n, sums):
                new = gather(index, 2 * n, 2, jnp.exp(score(index, 2 * n, 2, query) - shift))
                return sums[0] + new[0], sums[1] + new[1]

            empty = jnp.zeros((QUAD * BLK, BLK), f32), jnp.zeros((QUAD * BLK, WIDE), f32)
            finish(index, *lax.fori_loop(0, count // 2, add, empty))
            return carry

        lax.fori_loop(0, blocks, whole_row, 0)


def attend(table, query, keys, values, chunk):
    rows = query.shape[0]
    blocks = rows // BLK
    count = table.shape[1]
    total_rows = sum(value.shape[0] for value in values)
    own = pl.BlockSpec((rows, WIDE), lambda g: (0, g))
    scores = rows * count * BLK * H
    scratch = 8 * total_rows * WIDE
    return pl.pallas_call(
        functools.partial(attend_kernel, blocks, count, chunk, len(keys)),
        grid=(H // QUAD,),
        in_specs=[pl.BlockSpec(memory_space=pltpu.SMEM), own]
        + [pl.BlockSpec(memory_space=pl.ANY)] * (2 * len(keys)),
        out_specs=own,
        out_shape=jax.ShapeDtypeStruct((rows, D), jnp.bfloat16),
        scratch_shapes=[
            pltpu.VMEM((2, WIDE, total_rows), jnp.bfloat16),
            pltpu.VMEM((2, total_rows, WIDE), jnp.bfloat16),
            pltpu.SemaphoreType.DMA((2, 2 * len(keys))),
        ],
        compiler_params=pltpu.CompilerParams(vmem_limit_bytes=scratch + 10 * 2**20),
        cost_estimate=pl.CostEstimate(
            flops=24 * scores * HD, bytes_accessed=4 * total_rows * D + 4 * rows * D, transcendentals=scores
        ),
        name="attend",
    )(table, query, *keys, *values)


def project_rows(rows, weight, scale=1.0):
    return (jnp.dot(rows, weight, preferred_element_type=jnp.float32) * scale).astype(jnp.bfloat16)


def project_columns(weight, rows):
    wide = lax.dot_general(weight, rows, (((1,), (1,)), ((), ())), preferred_element_type=jnp.float32)
    return wide.astype(jnp.bfloat16)


def rows_by_axes(own, weights, place, stride, strides):
    summary = SUMB * BLK
    half = summary // 2
    cut = own.shape[0] - summary
    chips = strides // 2
    low = place == 0
    swap = lambda rows: lax.ppermute(rows, "head", [(0, 1), (1, 0)])
    beside = lambda rows: lax.ppermute(rows, "blk", [(s, s ^ 1) for s in range(strides)])

    def along(rows, k):
        return lax.ppermute(rows, "blk", [(s, (s + 2 * k) % strides) for s in range(strides)])

    steps = []
    for s in range(strides - 1):
        steps += [(s, s + 1), (strides + s + 1, strides + s)]
    to_next = lambda rows: lax.ppermute(rows, ("head", "blk"), steps)

    other_end = swap(own[-half:])
    other_end, own, weights = lax.optimization_barrier((other_end, own, weights))
    carried = jnp.where(low, other_end, own[cut : cut + half])
    other = swap(own[:-half])
    edge_end = to_next(other_end)
    ends = {1, chips - 1}
    slots = {k: along(carried, k) for k in ends}
    slots, after, own, other_end = lax.optimization_barrier((slots, carried, own, other_end))
    middle = {k: along(after, k) for k in range(2, chips - 1)}
    query = project_rows(own, weights[0], HD**-0.5)
    across = {k: swap(slots[k]) for k in ends}
    middle, other = lax.optimization_barrier((middle, other))
    edge = to_next(other)
    last, edge = lax.optimization_barrier(({k: swap(rows) for k, rows in middle.items()}, edge))
    slots.update(middle)
    across.update(last)
    across = [across[k] for k in range(1, chips)]
    slots = [slots[k] for k in range(1, chips)]
    foreign = jnp.concatenate(slots, axis=0)
    nearby = jnp.where(low, jnp.concatenate([other_end, other[-half:]], axis=0), own[cut:])
    pieces = [own, other, other_end, edge, edge_end, beside(nearby), foreign, beside(foreign)]
    pieces += across + [beside(rows) for rows in across]
    span = 2 * (chips - 1)

    def position(block):
        of, inside = block // SB, block % SB
        rel = block - stride * SB
        mine = inside % 8 + jnp.where(inside // 8 == place, 0, 8)
        edge = jnp.where(rel < 0, rel + SB + 8, rel)
        order = inside - (SB - SUMB)
        k = (stride // 2 - of // 2) % chips
        turned = (order // 2 ^ (1 - place)) * 2 + order % 2
        part = jnp.where(of % 2 == stride % 2, 0, 1) + jnp.where(order // 2 == 1 - place, 0, 2)
        far = jnp.where(k == 0, 24 + turned, 28 + part * span + (k - 1) * 2 + order % 2)
        return jnp.where(of == stride, mine, edge), jnp.where(of == stride, mine, far)

    return pieces, weights, query, position


def rows_by_gather(own, place, stride, strides, heads):
    summary = SUMB * BLK
    share = summary // heads
    lower = place < heads // 2
    stride_rows = lax.all_gather(own, "head", axis=0, tiled=True)
    piece = lax.dynamic_slice_in_dim(stride_rows[-summary:], place * share, share, 0)
    far_rows = lax.all_gather(piece, ("blk", "head"), axis=0, tiled=True)
    half = stride_rows.shape[0] // 2
    steps = []
    for h in range(heads):
        for s in range(strides - 1):
            ends = (h * strides + s, h * strides + s + 1)
            steps.append(ends if h < heads // 2 else ends[::-1])
    edge = lax.ppermute(jnp.where(lower, stride_rows[half:], stride_rows[:half]), ("head", "blk"), steps)

    def position(block):
        rel = block - stride * SB
        near = jnp.where(rel < 0, rel + SB + REACH, rel)
        return near, SB + REACH + block // SB * SUMB + block % SB - (SB - SUMB)

    return [stride_rows, edge, far_rows], position


def on_device(tokens, proj_weight, out_weight, pattern):
    heads = lax.axis_size("head")
    strides = lax.axis_size("blk")
    place = lax.axis_index("head")
    stride = lax.axis_index("blk")
    own = tokens[0]
    blocks = own.shape[0] // BLK
    weights = split_weights(proj_weight)

    if heads == 2:
        pieces, weights, query, position = rows_by_axes(own, weights, place, stride, strides)
    else:
        pieces, position = rows_by_gather(own, place, stride, strides, heads)
        query = project_rows(own, weights[0], HD**-0.5)
    listed = lax.dynamic_slice_in_dim(pattern, place * blocks, blocks, 0)
    near, far = position(listed)
    table = jnp.where(lax.broadcasted_iota(jnp.int32, listed.shape, 1) < LSEL, near, far)

    _, key_weight, value_weight = weights
    keys = [project_columns(key_weight, rows) for rows in pieces]
    values = [project_rows(rows, value_weight) for rows in pieces]
    mixed = attend(table, query, keys, values, 8)
    out = jnp.dot(mixed, out_weight, preferred_element_type=jnp.float32).astype(jnp.bfloat16)
    return out.reshape(tokens.shape)


def solution(mesh):
    return jax.shard_map(
        on_device,
        mesh=mesh,
        in_specs=(P(("batch", "blk"), "head", None), P(), P(), P(("batch", "blk"), None)),
        out_specs=P(("batch", "blk"), "head", None),
        check_vma=False,
    )
```

```python
import functools

import jax
import jax.numpy as jnp
from jax import lax
from jax.experimental import pallas as pl
from jax.experimental.pallas import tpu as pltpu
from jax.sharding import PartitionSpec as P

D = 1024
H = 16
HD = 64
BLK = 128
REACH = 8
LSEL = 6
SUMB = 4
SB = 16
KSEL = 16
PAIRS = H // 2
LANES = 2 * HD
TOTAL_CAP = 2.0**100


def split_kernel(weight_ref, query_ref, key_ref, value_ref):
    both = weight_ref[...]
    first, second = both[:, : 3 * HD], both[:, 3 * HD :]

    def columns(which):
        lo = which * HD
        return jnp.concatenate([first[:, lo : lo + HD], second[:, lo : lo + HD]], axis=1)

    query_ref[...] = columns(0).T
    key_ref[...] = columns(1)
    value_ref[...] = columns(2).T


def split_weights(proj_weight):
    wide = jax.ShapeDtypeStruct((D, D), jnp.bfloat16)
    across = pl.BlockSpec((LANES, D), lambda p: (p, 0))
    down = pl.BlockSpec((D, LANES), lambda p: (0, p))
    return pl.pallas_call(
        split_kernel,
        grid=(PAIRS,),
        in_specs=[pl.BlockSpec((D, 3 * LANES), lambda p: (0, p))],
        out_specs=[across, down, across],
        out_shape=[wide, wide, wide],
        cost_estimate=pl.CostEstimate(flops=0, bytes_accessed=4 * D * 3 * D, transcendentals=0),
        name="split_weights",
    )(proj_weight)


def attend_kernel(blocks, count, chunk, together, pieces, table_ref, query_ref, *refs):
    f32, bf16 = jnp.float32, jnp.bfloat16
    key_pieces, value_pieces = refs[:pieces], refs[pieces : 2 * pieces]
    out_ref, key_ref, value_ref, shift_ref, arrived = refs[2 * pieces :]
    step, steps = pl.program_id(0), pl.num_programs(0)
    slot = lax.rem(step, 2)

    def copies(pair, slot):
        lanes = pl.ds(pl.multiple_of(pair * LANES, LANES), LANES)
        found, start = [], 0
        for n, (key_piece, value_piece) in enumerate(zip(key_pieces, value_pieces)):
            span = pl.ds(start, key_piece.shape[0])
            found += [
                pltpu.make_async_copy(key_piece.at[:, lanes], key_ref.at[slot, span, :], arrived.at[slot, 2 * n]),
                pltpu.make_async_copy(
                    value_piece.at[lanes, :], value_ref.at[slot, :, span], arrived.at[slot, 2 * n + 1]
                ),
            ]
            start += key_piece.shape[0]
        return found

    @pl.when(step == 0)
    def _():
        for copy in copies(0, 0):
            copy.start()

    @pl.when(step + 1 < steps)
    def _():
        for copy in copies(step + 1, 1 - slot):
            copy.start()

    for copy in copies(step, slot):
        copy.wait()

    row = lax.broadcasted_iota(jnp.int32, (LANES, BLK), 0)

    def at(index):
        return pl.ds(pl.multiple_of(index * BLK, BLK), BLK)

    def queries(index):
        own = query_ref[:, at(index)]
        zero = jnp.zeros_like(own)
        return jnp.concatenate([jnp.where(row < HD, own, zero), jnp.where(row < HD, zero, own)], axis=1)

    def places(index, which, size):
        return [at(table_ref[index, which + n]) for n in range(size)]

    def score(index, which, size, query):
        keys = [key_ref[slot, place, :] for place in places(index, which, size)]
        return jnp.dot(jnp.concatenate(keys, axis=0), query, preferred_element_type=f32)

    def gather(index, which, size, raised):
        picked = jnp.concatenate([value_ref[slot, :, place] for place in places(index, which, size)], axis=1)
        ones = jnp.ones((16, raised.shape[0]), bf16)
        return jnp.dot(jnp.concatenate([picked, ones], axis=0), raised, preferred_element_type=f32)

    def finish(index, total):
        count_all = total[LANES : LANES + 1]
        scale = 1.0 / count_all
        mine = jnp.concatenate([total[:HD, :BLK] * scale[:, :BLK], total[HD:LANES, BLK:] * scale[:, BLK:]], axis=0)
        out_ref[at(index), :] = mine.T.astype(bf16)
        return count_all

    for index in range(blocks):
        shift_ref[index : index + 1, :] = jnp.max(score(index, 0, 1, queries(index)), axis=0, keepdims=True)

    def one(index):
        query = queries(index)
        total = None
        shift = shift_ref[pl.ds(index, 1), :]
        for which in range(0, count, chunk):
            raised = jnp.exp(score(index, which, chunk, query) - shift).astype(bf16)
            part = gather(index, which, chunk, raised)
            total = part if total is None else total + part
        return finish(index, total)

    def body(number, peak):
        for n in range(together):
            peak = jnp.maximum(peak, one(number * together + n))
        return peak

    peak = lax.fori_loop(0, blocks // together, body, jnp.zeros((1, 2 * BLK), f32))

    @pl.when(jnp.logical_not(jnp.max(peak) <= TOTAL_CAP))
    def _():
        def whole_row(index, carry):
            query = queries(index)

            def largest(n, shift):
                return jnp.maximum(shift, jnp.max(score(index, 2 * n, 2, query), axis=0, keepdims=True))

            shift = lax.fori_loop(0, count // 2, largest, jnp.full((1, 2 * BLK), -jnp.inf, f32))

            def add(n, total):
                raised = jnp.exp(score(index, 2 * n, 2, query) - shift).astype(bf16)
                return total + gather(index, 2 * n, 2, raised)

            finish(index, lax.fori_loop(0, count // 2, add, jnp.zeros((LANES + 16, 2 * BLK), f32)))
            return carry

        lax.fori_loop(0, blocks, whole_row, 0)


def attend(table, query, keys, values, chunk, together):
    rows = query.shape[1]
    blocks = rows // BLK
    count = table.shape[1]
    while blocks % together:
        together //= 2
    total_rows = sum(key.shape[0] for key in keys)
    scores = rows * count * BLK * H
    scratch = 8 * total_rows * LANES
    return pl.pallas_call(
        functools.partial(attend_kernel, blocks, count, chunk, together, len(keys)),
        grid=(PAIRS,),
        in_specs=[pl.BlockSpec(memory_space=pltpu.SMEM), pl.BlockSpec((LANES, rows), lambda p: (p, 0))]
        + [pl.BlockSpec(memory_space=pl.ANY)] * (2 * len(keys)),
        out_specs=pl.BlockSpec((rows, LANES), lambda p: (0, p)),
        out_shape=jax.ShapeDtypeStruct((rows, D), jnp.bfloat16),
        scratch_shapes=[
            pltpu.VMEM((2, total_rows, LANES), jnp.bfloat16),
            pltpu.VMEM((2, LANES, total_rows), jnp.bfloat16),
            pltpu.VMEM((blocks, 2 * BLK), jnp.float32),
            pltpu.SemaphoreType.DMA((2, 2 * len(keys))),
        ],
        compiler_params=pltpu.CompilerParams(vmem_limit_bytes=scratch + 10 * 2**20),
        cost_estimate=pl.CostEstimate(
            flops=24 * scores * HD, bytes_accessed=4 * total_rows * D + 4 * rows * D, transcendentals=scores
        ),
        name="attend",
    )(table, query, *keys, *values)


def project_rows(rows, weight):
    return jnp.dot(rows, weight, preferred_element_type=jnp.float32).astype(jnp.bfloat16)


def project_columns(weight, rows, scale=1.0):
    wide = lax.dot_general(weight, rows, (((1,), (1,)), ((), ())), preferred_element_type=jnp.float32)
    return (wide * scale).astype(jnp.bfloat16)


def rows_by_axes(own, weights, place, stride, strides):
    summary = SUMB * BLK
    half = summary // 2
    cut = own.shape[0] - summary
    chips = strides // 2
    low = place == 0
    swap = lambda rows: lax.ppermute(rows, "head", [(0, 1), (1, 0)])
    beside = lambda rows: lax.ppermute(rows, "blk", [(s, s ^ 1) for s in range(strides)])

    def along(rows, k):
        return lax.ppermute(rows, "blk", [(s, (s + 2 * k) % strides) for s in range(strides)])

    steps = []
    for s in range(strides - 1):
        steps += [(s, s + 1), (strides + s + 1, strides + s)]
    to_next = lambda rows: lax.ppermute(rows, ("head", "blk"), steps)

    other_end = swap(own[-half:])
    other_end, own, weights = lax.optimization_barrier((other_end, own, weights))
    carried = jnp.where(low, other_end, own[cut : cut + half])
    other = swap(own[:-half])
    edge_end = to_next(other_end)
    ends = [along(carried, 1), along(carried, chips - 1)]
    ends, after = lax.optimization_barrier((jnp.concatenate(ends, axis=0), carried))
    middle = jnp.concatenate([along(after, k) for k in range(2, chips - 1)], axis=0)
    own, other, other_end, released = lax.optimization_barrier((own, other, other_end, ends))
    across_ends = swap(released)
    edge = to_next(other)
    query = project_columns(weights[0], own, HD**-0.5)
    across_ends, middle = lax.optimization_barrier((across_ends, middle))
    across_middle, edge = lax.optimization_barrier((swap(middle), edge))
    nearby = jnp.where(low, jnp.concatenate([other_end, other[-half:]], axis=0), own[cut:])
    pieces = [own, other, other_end, edge, edge_end, beside(nearby)]
    pieces += [ends, middle, beside(ends), beside(middle)]
    pieces += [across_ends, across_middle, beside(across_ends), beside(across_middle)]
    span = 2 * (chips - 1)

    def position(block):
        of, inside = block // SB, block % SB
        rel = block - stride * SB
        mine = inside % 8 + jnp.where(inside // 8 == place, 0, 8)
        edge = jnp.where(rel < 0, rel + SB + 8, rel)
        order = inside - (SB - SUMB)
        k = (stride // 2 - of // 2) % chips
        turn = jnp.where(k == chips - 1, 1, jnp.where(k == 1, 0, k))
        turned = (order // 2 ^ (1 - place)) * 2 + order % 2
        part = jnp.where(of % 2 == stride % 2, 0, 1) + jnp.where(order // 2 == 1 - place, 0, 2)
        far = jnp.where(k == 0, 24 + turned, 28 + part * span + turn * 2 + order % 2)
        return jnp.where(of == stride, mine, edge), jnp.where(of == stride, mine, far)

    return pieces, weights, query, position


def rows_by_gather(own, place, stride, strides, heads):
    summary = SUMB * BLK
    share = summary // heads
    lower = place < heads // 2
    stride_rows = lax.all_gather(own, "head", axis=0, tiled=True)
    piece = lax.dynamic_slice_in_dim(stride_rows[-summary:], place * share, share, 0)
    far_rows = lax.all_gather(piece, ("blk", "head"), axis=0, tiled=True)
    half = stride_rows.shape[0] // 2
    steps = []
    for h in range(heads):
        for s in range(strides - 1):
            ends = (h * strides + s, h * strides + s + 1)
            steps.append(ends if h < heads // 2 else ends[::-1])
    edge = lax.ppermute(jnp.where(lower, stride_rows[half:], stride_rows[:half]), ("head", "blk"), steps)

    def position(block):
        rel = block - stride * SB
        near = jnp.where(rel < 0, rel + SB + REACH, rel)
        return near, SB + REACH + block // SB * SUMB + block % SB - (SB - SUMB)

    return [stride_rows, edge, far_rows], position


def on_device(tokens, proj_weight, out_weight, pattern):
    heads = lax.axis_size("head")
    strides = lax.axis_size("blk")
    place = lax.axis_index("head")
    stride = lax.axis_index("blk")
    own = tokens[0]
    blocks = own.shape[0] // BLK
    weights = split_weights(proj_weight)

    if heads == 2:
        pieces, weights, query, position = rows_by_axes(own, weights, place, stride, strides)
    else:
        pieces, position = rows_by_gather(own, place, stride, strides, heads)
        query = project_columns(weights[0], own, HD**-0.5)
    listed = lax.dynamic_slice_in_dim(pattern, place * blocks, blocks, 0)
    near, far = position(listed)
    table = jnp.where(lax.broadcasted_iota(jnp.int32, listed.shape, 1) < LSEL, near, far)

    _, key_weight, value_weight = weights
    keys = [project_rows(rows, key_weight) for rows in pieces]
    values = [project_columns(value_weight, rows) for rows in pieces]
    mixed = attend(table, query, keys, values, 4, 2)
    out = jnp.dot(mixed, out_weight, preferred_element_type=jnp.float32).astype(jnp.bfloat16)
    return out.reshape(tokens.shape)


def solution(mesh):
    return jax.shard_map(
        on_device,
        mesh=mesh,
        in_specs=(P(("batch", "blk"), "head", None), P(), P(), P(("batch", "blk"), None)),
        out_specs=P(("batch", "blk"), "head", None),
        check_vma=False,
    )
```

```python
import functools

import jax
import jax.numpy as jnp
from jax import lax
from jax.experimental import pallas as pl
from jax.experimental.pallas import tpu as pltpu
from jax.sharding import PartitionSpec as P

D = 1024
H = 16
HD = 64
BLK = 128
REACH = 8
LSEL = 6
SUMB = 4
SB = 16
KSEL = 16
PAIRS = H // 2
LANES = 2 * HD
TOTAL_CAP = 2.0**12


def split_kernel(weight_ref, query_ref, key_ref, value_ref):
    both = weight_ref[...]
    first, second = both[:, : 3 * HD], both[:, 3 * HD :]

    def columns(which):
        lo = which * HD
        return jnp.concatenate([first[:, lo : lo + HD], second[:, lo : lo + HD]], axis=1)

    query_ref[...] = columns(0).T
    key_ref[...] = columns(1)
    value_ref[...] = columns(2).T


def split_weights(proj_weight):
    wide = jax.ShapeDtypeStruct((D, D), jnp.bfloat16)
    across = pl.BlockSpec((LANES, D), lambda p: (p, 0))
    down = pl.BlockSpec((D, LANES), lambda p: (0, p))
    return pl.pallas_call(
        split_kernel,
        grid=(PAIRS,),
        in_specs=[pl.BlockSpec((D, 3 * LANES), lambda p: (0, p))],
        out_specs=[across, down, across],
        out_shape=[wide, wide, wide],
        cost_estimate=pl.CostEstimate(flops=0, bytes_accessed=4 * D * 3 * D, transcendentals=0),
        name="split_weights",
    )(proj_weight)


def attend_kernel(blocks, count, chunk, together, pieces, table_ref, query_ref, *refs):
    f32, bf16 = jnp.float32, jnp.bfloat16
    key_pieces, value_pieces = refs[:pieces], refs[pieces : 2 * pieces]
    out_ref, key_ref, value_ref, shift_ref, arrived = refs[2 * pieces :]
    step, steps = pl.program_id(0), pl.num_programs(0)
    slot = lax.rem(step, 2)

    def copies(pair, slot):
        lanes = pl.ds(pl.multiple_of(pair * LANES, LANES), LANES)
        found, start = [], 0
        for n, (key_piece, value_piece) in enumerate(zip(key_pieces, value_pieces)):
            span = pl.ds(start, key_piece.shape[0])
            found += [
                pltpu.make_async_copy(key_piece.at[:, lanes], key_ref.at[slot, span, :], arrived.at[slot, 2 * n]),
                pltpu.make_async_copy(
                    value_piece.at[lanes, :], value_ref.at[slot, :, span], arrived.at[slot, 2 * n + 1]
                ),
            ]
            start += key_piece.shape[0]
        return found

    @pl.when(step == 0)
    def _():
        for copy in copies(0, 0):
            copy.start()

    @pl.when(step + 1 < steps)
    def _():
        for copy in copies(step + 1, 1 - slot):
            copy.start()

    for copy in copies(step, slot):
        copy.wait()

    row = lax.broadcasted_iota(jnp.int32, (LANES, BLK), 0)

    def at(index):
        return pl.ds(pl.multiple_of(index * BLK, BLK), BLK)

    def queries(index):
        own = query_ref[:, at(index)]
        zero = jnp.zeros_like(own)
        return jnp.concatenate([jnp.where(row < HD, own, zero), jnp.where(row < HD, zero, own)], axis=1)

    def places(index, which, size):
        return [at(table_ref[index, which + n]) for n in range(size)]

    def score(index, which, size, query):
        keys = [key_ref[slot, place, :] for place in places(index, which, size)]
        return jnp.dot(jnp.concatenate(keys, axis=0), query, preferred_element_type=f32)

    def gather(index, which, size, raised):
        picked = jnp.concatenate([value_ref[slot, :, place] for place in places(index, which, size)], axis=1)
        ones = jnp.ones((16, raised.shape[0]), bf16)
        return jnp.dot(jnp.concatenate([picked, ones], axis=0), raised, preferred_element_type=f32)

    def finish(index, total):
        count_all = total[LANES : LANES + 1]
        scale = 1.0 / count_all
        mine = jnp.concatenate([total[:HD, :BLK] * scale[:, :BLK], total[HD:LANES, BLK:] * scale[:, BLK:]], axis=0)
        out_ref[at(index), :] = mine.T.astype(bf16)
        return count_all

    for index in range(blocks):
        shift_ref[index : index + 1, :] = jnp.max(score(index, 0, 1, queries(index)), axis=0, keepdims=True)

    def one(index):
        query = queries(index)
        total = None
        shift = shift_ref[pl.ds(index, 1), :]
        for which in range(0, count, chunk):
            raised = jnp.exp((score(index, which, chunk, query) - shift).astype(bf16))
            part = gather(index, which, chunk, raised)
            total = part if total is None else total + part
        return finish(index, total)

    def body(number, peak):
        for n in range(together):
            peak = jnp.maximum(peak, one(number * together + n))
        return peak

    peak = lax.fori_loop(0, blocks // together, body, jnp.zeros((1, 2 * BLK), f32))

    @pl.when(jnp.logical_not(jnp.max(peak) <= TOTAL_CAP))
    def _():
        def whole_row(index, carry):
            query = queries(index)

            def largest(n, shift):
                return jnp.maximum(shift, jnp.max(score(index, 2 * n, 2, query), axis=0, keepdims=True))

            shift = lax.fori_loop(0, count // 2, largest, jnp.full((1, 2 * BLK), -jnp.inf, f32))

            def add(n, total):
                raised = jnp.exp(score(index, 2 * n, 2, query) - shift).astype(bf16)
                return total + gather(index, 2 * n, 2, raised)

            finish(index, lax.fori_loop(0, count // 2, add, jnp.zeros((LANES + 16, 2 * BLK), f32)))
            return carry

        lax.fori_loop(0, blocks, whole_row, 0)


def attend(table, query, keys, values, chunk, together):
    rows = query.shape[1]
    blocks = rows // BLK
    count = table.shape[1]
    while blocks % together:
        together //= 2
    total_rows = sum(key.shape[0] for key in keys)
    scores = rows * count * BLK * H
    scratch = 8 * total_rows * LANES
    return pl.pallas_call(
        functools.partial(attend_kernel, blocks, count, chunk, together, len(keys)),
        grid=(PAIRS,),
        in_specs=[pl.BlockSpec(memory_space=pltpu.SMEM), pl.BlockSpec((LANES, rows), lambda p: (p, 0))]
        + [pl.BlockSpec(memory_space=pl.ANY)] * (2 * len(keys)),
        out_specs=pl.BlockSpec((rows, LANES), lambda p: (0, p)),
        out_shape=jax.ShapeDtypeStruct((rows, D), jnp.bfloat16),
        scratch_shapes=[
            pltpu.VMEM((2, total_rows, LANES), jnp.bfloat16),
            pltpu.VMEM((2, LANES, total_rows), jnp.bfloat16),
            pltpu.VMEM((blocks, 2 * BLK), jnp.float32),
            pltpu.SemaphoreType.DMA((2, 2 * len(keys))),
        ],
        compiler_params=pltpu.CompilerParams(vmem_limit_bytes=scratch + 10 * 2**20),
        cost_estimate=pl.CostEstimate(
            flops=24 * scores * HD, bytes_accessed=4 * total_rows * D + 4 * rows * D, transcendentals=scores
        ),
        name="attend",
    )(table, query, *keys, *values)


def project_rows(rows, weight):
    return jnp.dot(rows, weight, preferred_element_type=jnp.float32).astype(jnp.bfloat16)


def project_columns(weight, rows, scale=1.0):
    wide = lax.dot_general(weight, rows, (((1,), (1,)), ((), ())), preferred_element_type=jnp.float32)
    return (wide * scale).astype(jnp.bfloat16)


def rows_by_axes(own, weights, place, stride, strides):
    summary = SUMB * BLK
    half = summary // 2
    cut = own.shape[0] - summary
    chips = strides // 2
    low = place == 0
    swap = lambda rows: lax.ppermute(rows, "head", [(0, 1), (1, 0)])
    beside = lambda rows: lax.ppermute(rows, "blk", [(s, s ^ 1) for s in range(strides)])

    def along(rows, k):
        return lax.ppermute(rows, "blk", [(s, (s + 2 * k) % strides) for s in range(strides)])

    steps = []
    for s in range(strides - 1):
        steps += [(s, s + 1), (strides + s + 1, strides + s)]
    to_next = lambda rows: lax.ppermute(rows, ("head", "blk"), steps)

    other_end = swap(own[-half:])
    other_end, own, weights = lax.optimization_barrier((other_end, own, weights))
    carried = jnp.where(low, other_end, own[cut : cut + half])
    other = swap(own[:-half])
    edge_end = to_next(other_end)
    ends = [along(carried, 1), along(carried, chips - 1)]
    ends, after = lax.optimization_barrier((jnp.concatenate(ends, axis=0), carried))
    middle = jnp.concatenate([along(after, k) for k in range(2, chips - 1)], axis=0)
    own, other, other_end, released = lax.optimization_barrier((own, other, other_end, ends))
    across_ends = swap(released)
    edge = to_next(other)
    query = project_columns(weights[0], own, HD**-0.5)
    across_ends, middle = lax.optimization_barrier((across_ends, middle))
    across_middle, edge = lax.optimization_barrier((swap(middle), edge))
    nearby = jnp.where(low, jnp.concatenate([other_end, other[-half:]], axis=0), own[cut:])
    pieces = [own, other, other_end, edge, edge_end, beside(nearby)]
    pieces += [ends, middle, beside(ends), beside(middle)]
    pieces += [across_ends, across_middle, beside(across_ends), beside(across_middle)]
    span = 2 * (chips - 1)

    def position(block):
        of, inside = block // SB, block % SB
        rel = block - stride * SB
        mine = inside % 8 + jnp.where(inside // 8 == place, 0, 8)
        edge = jnp.where(rel < 0, rel + SB + 8, rel)
        order = inside - (SB - SUMB)
        k = (stride // 2 - of // 2) % chips
        turn = jnp.where(k == chips - 1, 1, jnp.where(k == 1, 0, k))
        turned = (order // 2 ^ (1 - place)) * 2 + order % 2
        part = jnp.where(of % 2 == stride % 2, 0, 1) + jnp.where(order // 2 == 1 - place, 0, 2)
        far = jnp.where(k == 0, 24 + turned, 28 + part * span + turn * 2 + order % 2)
        return jnp.where(of == stride, mine, edge), jnp.where(of == stride, mine, far)

    return pieces, weights, query, position


def rows_by_gather(own, place, stride, strides, heads):
    summary = SUMB * BLK
    share = summary // heads
    lower = place < heads // 2
    stride_rows = lax.all_gather(own, "head", axis=0, tiled=True)
    piece = lax.dynamic_slice_in_dim(stride_rows[-summary:], place * share, share, 0)
    far_rows = lax.all_gather(piece, ("blk", "head"), axis=0, tiled=True)
    half = stride_rows.shape[0] // 2
    steps = []
    for h in range(heads):
        for s in range(strides - 1):
            ends = (h * strides + s, h * strides + s + 1)
            steps.append(ends if h < heads // 2 else ends[::-1])
    edge = lax.ppermute(jnp.where(lower, stride_rows[half:], stride_rows[:half]), ("head", "blk"), steps)

    def position(block):
        rel = block - stride * SB
        near = jnp.where(rel < 0, rel + SB + REACH, rel)
        return near, SB + REACH + block // SB * SUMB + block % SB - (SB - SUMB)

    return [stride_rows, edge, far_rows], position


def on_device(tokens, proj_weight, out_weight, pattern):
    heads = lax.axis_size("head")
    strides = lax.axis_size("blk")
    place = lax.axis_index("head")
    stride = lax.axis_index("blk")
    own = tokens[0]
    blocks = own.shape[0] // BLK
    weights = split_weights(proj_weight)

    if heads == 2:
        pieces, weights, query, position = rows_by_axes(own, weights, place, stride, strides)
    else:
        pieces, position = rows_by_gather(own, place, stride, strides, heads)
        query = project_columns(weights[0], own, HD**-0.5)
    listed = lax.dynamic_slice_in_dim(pattern, place * blocks, blocks, 0)
    near, far = position(listed)
    table = jnp.where(lax.broadcasted_iota(jnp.int32, listed.shape, 1) < LSEL, near, far)

    _, key_weight, value_weight = weights
    keys = [project_rows(rows, key_weight) for rows in pieces]
    values = [project_columns(value_weight, rows) for rows in pieces]
    mixed = attend(table, query, keys, values, 4, 2)
    out = jnp.dot(mixed, out_weight, preferred_element_type=jnp.float32).astype(jnp.bfloat16)
    return out.reshape(tokens.shape)


def solution(mesh):
    return jax.shard_map(
        on_device,
        mesh=mesh,
        in_specs=(P(("batch", "blk"), "head", None), P(), P(), P(("batch", "blk"), None)),
        out_specs=P(("batch", "blk"), "head", None),
        check_vma=False,
    )
```

```python
import functools

import jax
import jax.numpy as jnp
from jax import lax
from jax.experimental import pallas as pl
from jax.experimental.pallas import tpu as pltpu
from jax.sharding import PartitionSpec as P

D = 1024
H = 16
HD = 64
BLK = 128
REACH = 8
LSEL = 6
SUMB = 4
SB = 16
KSEL = 16
PAIRS = H // 2
LANES = 2 * HD
TOTAL_CAP = 2.0**100


def split_kernel(weight_ref, query_ref, key_ref, value_ref):
    both = weight_ref[...]
    first, second = both[:, : 3 * HD], both[:, 3 * HD :]

    def columns(which):
        lo = which * HD
        return jnp.concatenate([first[:, lo : lo + HD], second[:, lo : lo + HD]], axis=1)

    query_ref[...] = columns(0).T
    key_ref[...] = columns(1)
    value_ref[...] = columns(2).T


def split_weights(proj_weight):
    wide = jax.ShapeDtypeStruct((D, D), jnp.bfloat16)
    across = pl.BlockSpec((LANES, D), lambda p: (p, 0))
    down = pl.BlockSpec((D, LANES), lambda p: (0, p))
    return pl.pallas_call(
        split_kernel,
        grid=(PAIRS,),
        in_specs=[pl.BlockSpec((D, 3 * LANES), lambda p: (0, p))],
        out_specs=[across, down, across],
        out_shape=[wide, wide, wide],
        cost_estimate=pl.CostEstimate(flops=0, bytes_accessed=4 * D * 3 * D, transcendentals=0),
        name="split_weights",
    )(proj_weight)


def attend_kernel(blocks, count, chunk, together, pieces, table_ref, query_ref, *refs):
    f32, bf16 = jnp.float32, jnp.bfloat16
    key_pieces, value_pieces = refs[:pieces], refs[pieces : 2 * pieces]
    out_ref, key_ref, value_ref, shift_ref, arrived = refs[2 * pieces :]
    step, steps = pl.program_id(0), pl.num_programs(0)
    slot = lax.rem(step, 2)

    def copies(pair, slot):
        lanes = pl.ds(pl.multiple_of(pair * LANES, LANES), LANES)
        found, start = [], 0
        for n, (key_piece, value_piece) in enumerate(zip(key_pieces, value_pieces)):
            span = pl.ds(start, key_piece.shape[0])
            found += [
                pltpu.make_async_copy(key_piece.at[:, lanes], key_ref.at[slot, span, :], arrived.at[slot, 2 * n]),
                pltpu.make_async_copy(
                    value_piece.at[lanes, :], value_ref.at[slot, :, span], arrived.at[slot, 2 * n + 1]
                ),
            ]
            start += key_piece.shape[0]
        return found

    @pl.when(step == 0)
    def _():
        for copy in copies(0, 0):
            copy.start()

    @pl.when(step + 1 < steps)
    def _():
        for copy in copies(step + 1, 1 - slot):
            copy.start()

    for copy in copies(step, slot):
        copy.wait()

    row = lax.broadcasted_iota(jnp.int32, (LANES, BLK), 0)

    def at(index):
        return pl.ds(pl.multiple_of(index * BLK, BLK), BLK)

    def queries(index):
        own = query_ref[:, at(index)]
        zero = jnp.zeros_like(own)
        return jnp.concatenate([jnp.where(row < HD, own, zero), jnp.where(row < HD, zero, own)], axis=1)

    def places(index, which, size):
        return [at(table_ref[index, which + n]) for n in range(size)]

    def score(index, which, size, query):
        keys = [key_ref[slot, place, :] for place in places(index, which, size)]
        return jnp.dot(jnp.concatenate(keys, axis=0), query, preferred_element_type=f32)

    def gather(index, which, size, raised):
        picked = jnp.concatenate([value_ref[slot, :, place] for place in places(index, which, size)], axis=1)
        ones = jnp.ones((16, raised.shape[0]), bf16)
        return jnp.dot(jnp.concatenate([picked, ones], axis=0), raised, preferred_element_type=f32)

    def finish(index, total):
        count_all = total[LANES : LANES + 1]
        scale = 1.0 / count_all
        mine = jnp.concatenate([total[:HD, :BLK] * scale[:, :BLK], total[HD:LANES, BLK:] * scale[:, BLK:]], axis=0)
        out_ref[at(index), :] = mine.T.astype(bf16)
        return count_all

    for index in range(blocks):
        shift_ref[index : index + 1, :] = jnp.max(score(index, 0, 1, queries(index)), axis=0, keepdims=True)

    def one(index):
        query = queries(index)
        total = None
        shift = shift_ref[pl.ds(index, 1), :]
        for which in range(0, count, chunk):
            raised = jnp.exp(score(index, which, chunk, query) - shift).astype(bf16)
            part = gather(index, which, chunk, raised)
            total = part if total is None else total + part
        return finish(index, total)

    def body(number, peak):
        for n in range(together):
            peak = jnp.maximum(peak, one(number * together + n))
        return peak

    peak = lax.fori_loop(0, blocks // together, body, jnp.zeros((1, 2 * BLK), f32))

    @pl.when(jnp.logical_not(jnp.max(peak) <= TOTAL_CAP))
    def _():
        def whole_row(index, carry):
            query = queries(index)

            def largest(n, shift):
                return jnp.maximum(shift, jnp.max(score(index, 2 * n, 2, query), axis=0, keepdims=True))

            shift = lax.fori_loop(0, count // 2, largest, jnp.full((1, 2 * BLK), -jnp.inf, f32))

            def add(n, total):
                raised = jnp.exp(score(index, 2 * n, 2, query) - shift).astype(bf16)
                return total + gather(index, 2 * n, 2, raised)

            finish(index, lax.fori_loop(0, count // 2, add, jnp.zeros((LANES + 16, 2 * BLK), f32)))
            return carry

        lax.fori_loop(0, blocks, whole_row, 0)


def attend(table, query, keys, values, chunk, together):
    rows = query.shape[1]
    blocks = rows // BLK
    count = table.shape[1]
    while blocks % together:
        together //= 2
    total_rows = sum(key.shape[0] for key in keys)
    scores = rows * count * BLK * H
    scratch = 8 * total_rows * LANES
    return pl.pallas_call(
        functools.partial(attend_kernel, blocks, count, chunk, together, len(keys)),
        grid=(PAIRS,),
        in_specs=[pl.BlockSpec(memory_space=pltpu.SMEM), pl.BlockSpec((LANES, rows), lambda p: (p, 0))]
        + [pl.BlockSpec(memory_space=pl.ANY)] * (2 * len(keys)),
        out_specs=pl.BlockSpec((rows, LANES), lambda p: (0, p)),
        out_shape=jax.ShapeDtypeStruct((rows, D), jnp.bfloat16),
        scratch_shapes=[
            pltpu.VMEM((2, total_rows, LANES), jnp.bfloat16),
            pltpu.VMEM((2, LANES, total_rows), jnp.bfloat16),
            pltpu.VMEM((blocks, 2 * BLK), jnp.float32),
            pltpu.SemaphoreType.DMA((2, 2 * len(keys))),
        ],
        compiler_params=pltpu.CompilerParams(vmem_limit_bytes=scratch + 10 * 2**20),
        cost_estimate=pl.CostEstimate(
            flops=24 * scores * HD, bytes_accessed=4 * total_rows * D + 4 * rows * D, transcendentals=scores
        ),
        name="attend",
    )(table, query, *keys, *values)


def project_rows(rows, weight):
    return jnp.dot(rows, weight, preferred_element_type=jnp.float32).astype(jnp.bfloat16)


def project_columns(weight, rows, scale=1.0):
    wide = lax.dot_general(weight, rows, (((1,), (1,)), ((), ())), preferred_element_type=jnp.float32)
    return (wide * scale).astype(jnp.bfloat16)


def rows_by_axes(own, weights, place, stride, strides):
    summary = SUMB * BLK
    half = summary // 2
    cut = own.shape[0] - summary
    chips = strides // 2
    low = place == 0
    swap = lambda rows: lax.ppermute(rows, "head", [(0, 1), (1, 0)])
    beside = lambda rows: lax.ppermute(rows, "blk", [(s, s ^ 1) for s in range(strides)])

    def along(rows, k):
        return lax.ppermute(rows, "blk", [(s, (s + 2 * k) % strides) for s in range(strides)])

    steps = []
    for s in range(strides - 1):
        steps += [(s, s + 1), (strides + s + 1, strides + s)]
    to_next = lambda rows: lax.ppermute(rows, ("head", "blk"), steps)

    other_end = swap(own[-half:])
    other_end, own, weights = lax.optimization_barrier((other_end, own, weights))
    carried = jnp.where(low, other_end, own[cut : cut + half])
    other = swap(own[:-half])
    edge_end = to_next(other_end)
    ends = [along(carried, 1), along(carried, chips - 1)]
    ends, after = lax.optimization_barrier((jnp.concatenate(ends, axis=0), carried))
    middle = jnp.concatenate([along(after, k) for k in range(2, chips - 1)], axis=0)
    other, other_end, released = lax.optimization_barrier((other, other_end, ends))
    across_ends = swap(released)
    edge = to_next(other)
    nearby = jnp.where(low, jnp.concatenate([other_end, other[-half:]], axis=0), own[cut:])
    across_ends, middle, own = lax.optimization_barrier((across_ends, middle, own))
    query = project_columns(weights[0], own, HD**-0.5)
    across_middle = swap(middle)
    pieces = [own, other, other_end, edge, edge_end, beside(nearby)]
    pieces += [ends, middle, beside(ends), beside(middle)]
    pieces += [across_ends, across_middle, beside(across_ends), beside(across_middle)]
    span = 2 * (chips - 1)

    def position(block):
        of, inside = block // SB, block % SB
        rel = block - stride * SB
        mine = inside % 8 + jnp.where(inside // 8 == place, 0, 8)
        edge = jnp.where(rel < 0, rel + SB + 8, rel)
        order = inside - (SB - SUMB)
        k = (stride // 2 - of // 2) % chips
        turn = jnp.where(k == chips - 1, 1, jnp.where(k == 1, 0, k))
        turned = (order // 2 ^ (1 - place)) * 2 + order % 2
        part = jnp.where(of % 2 == stride % 2, 0, 1) + jnp.where(order // 2 == 1 - place, 0, 2)
        far = jnp.where(k == 0, 24 + turned, 28 + part * span + turn * 2 + order % 2)
        return jnp.where(of == stride, mine, edge), jnp.where(of == stride, mine, far)

    return pieces, weights, query, position


def rows_by_gather(own, place, stride, strides, heads):
    summary = SUMB * BLK
    share = summary // heads
    lower = place < heads // 2
    stride_rows = lax.all_gather(own, "head", axis=0, tiled=True)
    piece = lax.dynamic_slice_in_dim(stride_rows[-summary:], place * share, share, 0)
    far_rows = lax.all_gather(piece, ("blk", "head"), axis=0, tiled=True)
    half = stride_rows.shape[0] // 2
    steps = []
    for h in range(heads):
        for s in range(strides - 1):
            ends = (h * strides + s, h * strides + s + 1)
            steps.append(ends if h < heads // 2 else ends[::-1])
    edge = lax.ppermute(jnp.where(lower, stride_rows[half:], stride_rows[:half]), ("head", "blk"), steps)

    def position(block):
        rel = block - stride * SB
        near = jnp.where(rel < 0, rel + SB + REACH, rel)
        return near, SB + REACH + block // SB * SUMB + block % SB - (SB - SUMB)

    return [stride_rows, edge, far_rows], position


def on_device(tokens, proj_weight, out_weight, pattern):
    heads = lax.axis_size("head")
    strides = lax.axis_size("blk")
    place = lax.axis_index("head")
    stride = lax.axis_index("blk")
    own = tokens[0]
    blocks = own.shape[0] // BLK
    weights = split_weights(proj_weight)

    if heads == 2:
        pieces, weights, query, position = rows_by_axes(own, weights, place, stride, strides)
    else:
        pieces, position = rows_by_gather(own, place, stride, strides, heads)
        query = project_columns(weights[0], own, HD**-0.5)
    listed = lax.dynamic_slice_in_dim(pattern, place * blocks, blocks, 0)
    near, far = position(listed)
    table = jnp.where(lax.broadcasted_iota(jnp.int32, listed.shape, 1) < LSEL, near, far)

    _, key_weight, value_weight = weights
    keys = [project_rows(rows, key_weight) for rows in pieces]
    values = [project_columns(value_weight, rows) for rows in pieces]
    mixed = attend(table, query, keys, values, 4, 2)
    out = jnp.dot(mixed, out_weight, preferred_element_type=jnp.float32).astype(jnp.bfloat16)
    return out.reshape(tokens.shape)


def solution(mesh):
    return jax.shard_map(
        on_device,
        mesh=mesh,
        in_specs=(P(("batch", "blk"), "head", None), P(), P(), P(("batch", "blk"), None)),
        out_specs=P(("batch", "blk"), "head", None),
        check_vma=False,
    )
```

```python
import functools

import jax
import jax.numpy as jnp
from jax import lax
from jax.experimental import pallas as pl
from jax.experimental.pallas import tpu as pltpu
from jax.sharding import PartitionSpec as P

D = 1024
H = 16
HD = 64
BLK = 128
REACH = 8
LSEL = 6
SUMB = 4
SB = 16
KSEL = 16
PAIRS = H // 2
LANES = 2 * HD
TOTAL_CAP = 2.0**100


def split_kernel(weight_ref, query_ref, key_ref, value_ref):
    both = weight_ref[...]
    first, second = both[:, : 3 * HD], both[:, 3 * HD :]

    def columns(which):
        lo = which * HD
        return jnp.concatenate([first[:, lo : lo + HD], second[:, lo : lo + HD]], axis=1)

    query_ref[...] = columns(0).T
    key_ref[...] = columns(1)
    value_ref[...] = columns(2).T


def split_weights(proj_weight):
    wide = jax.ShapeDtypeStruct((D, D), jnp.bfloat16)
    across = pl.BlockSpec((LANES, D), lambda p: (p, 0))
    down = pl.BlockSpec((D, LANES), lambda p: (0, p))
    return pl.pallas_call(
        split_kernel,
        grid=(PAIRS,),
        in_specs=[pl.BlockSpec((D, 3 * LANES), lambda p: (0, p))],
        out_specs=[across, down, across],
        out_shape=[wide, wide, wide],
        cost_estimate=pl.CostEstimate(flops=0, bytes_accessed=4 * D * 3 * D, transcendentals=0),
        name="split_weights",
    )(proj_weight)


def attend_kernel(blocks, count, chunk, together, pieces, table_ref, query_ref, *refs):
    f32, bf16 = jnp.float32, jnp.bfloat16
    key_pieces, value_pieces = refs[:pieces], refs[pieces : 2 * pieces]
    out_ref, key_ref, value_ref, shift_ref, arrived = refs[2 * pieces :]
    step, steps = pl.program_id(0), pl.num_programs(0)
    slot = lax.rem(step, 2)

    def copies(pair, slot):
        lanes = pl.ds(pl.multiple_of(pair * LANES, LANES), LANES)
        found, start = [], 0
        for n, (key_piece, value_piece) in enumerate(zip(key_pieces, value_pieces)):
            span = pl.ds(start, key_piece.shape[0])
            found += [
                pltpu.make_async_copy(key_piece.at[:, lanes], key_ref.at[slot, span, :], arrived.at[slot, 2 * n]),
                pltpu.make_async_copy(
                    value_piece.at[lanes, :], value_ref.at[slot, :, span], arrived.at[slot, 2 * n + 1]
                ),
            ]
            start += key_piece.shape[0]
        return found

    @pl.when(step == 0)
    def _():
        for copy in copies(0, 0):
            copy.start()

    @pl.when(step + 1 < steps)
    def _():
        for copy in copies(step + 1, 1 - slot):
            copy.start()

    for copy in copies(step, slot):
        copy.wait()

    row = lax.broadcasted_iota(jnp.int32, (LANES, BLK), 0)

    def at(index):
        return pl.ds(pl.multiple_of(index * BLK, BLK), BLK)

    def queries(index):
        own = query_ref[:, at(index)]
        zero = jnp.zeros_like(own)
        return jnp.concatenate([jnp.where(row < HD, own, zero), jnp.where(row < HD, zero, own)], axis=1)

    def places(index, which, size):
        return [at(table_ref[index, which + n]) for n in range(size)]

    def score(index, which, size, query):
        keys = [key_ref[slot, place, :] for place in places(index, which, size)]
        return jnp.dot(jnp.concatenate(keys, axis=0), query, preferred_element_type=f32)

    def gather(index, which, size, raised):
        picked = jnp.concatenate([value_ref[slot, :, place] for place in places(index, which, size)], axis=1)
        ones = jnp.ones((16, raised.shape[0]), bf16)
        return jnp.dot(jnp.concatenate([picked, ones], axis=0), raised, preferred_element_type=f32)

    def finish(index, total):
        count_all = total[LANES : LANES + 1]
        scale = 1.0 / count_all
        mine = jnp.concatenate([total[:HD, :BLK] * scale[:, :BLK], total[HD:LANES, BLK:] * scale[:, BLK:]], axis=0)
        out_ref[at(index), :] = mine.T.astype(bf16)
        return count_all

    for index in range(blocks):
        shift_ref[index : index + 1, :] = jnp.max(score(index, 0, 1, queries(index)), axis=0, keepdims=True)

    def one(index):
        query = queries(index)
        total = None
        shift = shift_ref[pl.ds(index, 1), :]
        for which in range(0, count, chunk):
            raised = jnp.exp(score(index, which, chunk, query) - shift).astype(bf16)
            part = gather(index, which, chunk, raised)
            total = part if total is None else total + part
        return finish(index, total)

    def body(number, peak):
        for n in range(together):
            peak = jnp.maximum(peak, one(number * together + n))
        return peak

    peak = lax.fori_loop(0, blocks // together, body, jnp.zeros((1, 2 * BLK), f32))

    @pl.when(jnp.logical_not(jnp.max(peak) <= TOTAL_CAP))
    def _():
        def whole_row(index, carry):
            query = queries(index)

            def largest(n, shift):
                return jnp.maximum(shift, jnp.max(score(index, 2 * n, 2, query), axis=0, keepdims=True))

            shift = lax.fori_loop(0, count // 2, largest, jnp.full((1, 2 * BLK), -jnp.inf, f32))

            def add(n, total):
                raised = jnp.exp(score(index, 2 * n, 2, query) - shift).astype(bf16)
                return total + gather(index, 2 * n, 2, raised)

            finish(index, lax.fori_loop(0, count // 2, add, jnp.zeros((LANES + 16, 2 * BLK), f32)))
            return carry

        lax.fori_loop(0, blocks, whole_row, 0)


def attend(table, query, keys, values, chunk, together):
    rows = query.shape[1]
    blocks = rows // BLK
    count = table.shape[1]
    while blocks % together:
        together //= 2
    total_rows = sum(key.shape[0] for key in keys)
    scores = rows * count * BLK * H
    scratch = 8 * total_rows * LANES
    return pl.pallas_call(
        functools.partial(attend_kernel, blocks, count, chunk, together, len(keys)),
        grid=(PAIRS,),
        in_specs=[pl.BlockSpec(memory_space=pltpu.SMEM), pl.BlockSpec((LANES, rows), lambda p: (p, 0))]
        + [pl.BlockSpec(memory_space=pl.ANY)] * (2 * len(keys)),
        out_specs=pl.BlockSpec((rows, LANES), lambda p: (0, p)),
        out_shape=jax.ShapeDtypeStruct((rows, D), jnp.bfloat16),
        scratch_shapes=[
            pltpu.VMEM((2, total_rows, LANES), jnp.bfloat16),
            pltpu.VMEM((2, LANES, total_rows), jnp.bfloat16),
            pltpu.VMEM((blocks, 2 * BLK), jnp.float32),
            pltpu.SemaphoreType.DMA((2, 2 * len(keys))),
        ],
        compiler_params=pltpu.CompilerParams(vmem_limit_bytes=scratch + 10 * 2**20),
        cost_estimate=pl.CostEstimate(
            flops=24 * scores * HD, bytes_accessed=4 * total_rows * D + 4 * rows * D, transcendentals=scores
        ),
        name="attend",
    )(table, query, *keys, *values)


def project_rows(rows, weight):
    return jnp.dot(rows, weight, preferred_element_type=jnp.float32).astype(jnp.bfloat16)


def project_columns(weight, rows, scale=1.0):
    wide = lax.dot_general(weight, rows, (((1,), (1,)), ((), ())), preferred_element_type=jnp.float32)
    return (wide * scale).astype(jnp.bfloat16)


def rows_by_axes(own, weights, place, stride, strides):
    summary = SUMB * BLK
    half = summary // 2
    cut = own.shape[0] - summary
    chips = strides // 2
    low = place == 0
    swap = lambda rows: lax.ppermute(rows, "head", [(0, 1), (1, 0)])
    beside = lambda rows: lax.ppermute(rows, "blk", [(s, s ^ 1) for s in range(strides)])

    def along(rows, k):
        return lax.ppermute(rows, "blk", [(s, (s + 2 * k) % strides) for s in range(strides)])

    steps = []
    for s in range(strides - 1):
        steps += [(s, s + 1), (strides + s + 1, strides + s)]
    to_next = lambda rows: lax.ppermute(rows, ("head", "blk"), steps)

    other_end = swap(own[-half:])
    other_end, own, weights = lax.optimization_barrier((other_end, own, weights))
    carried = jnp.where(low, other_end, own[cut : cut + half])
    other = swap(own[:-half])
    edge_end = to_next(other_end)
    ends = [along(carried, 1), along(carried, chips - 1)]
    ends, after = lax.optimization_barrier((jnp.concatenate(ends, axis=0), carried))
    middle = jnp.concatenate([along(after, k) for k in range(2, chips - 1)], axis=0)
    other, other_end, released = lax.optimization_barrier((other, other_end, ends))
    across_ends = swap(released)
    edge = to_next(other)
    nearby = jnp.where(low, jnp.concatenate([other_end, other[-half:]], axis=0), own[cut:])
    beside_nearby, own = lax.optimization_barrier((beside(nearby), own))
    query = project_columns(weights[0], own, HD**-0.5)
    across_ends, middle = lax.optimization_barrier((across_ends, middle))
    across_middle = swap(middle)
    pieces = [own, other, other_end, edge, edge_end, beside_nearby]
    pieces += [ends, middle, beside(ends), beside(middle)]
    pieces += [across_ends, across_middle, beside(across_ends), beside(across_middle)]
    span = 2 * (chips - 1)

    def position(block):
        of, inside = block // SB, block % SB
        rel = block - stride * SB
        mine = inside % 8 + jnp.where(inside // 8 == place, 0, 8)
        edge = jnp.where(rel < 0, rel + SB + 8, rel)
        order = inside - (SB - SUMB)
        k = (stride // 2 - of // 2) % chips
        turn = jnp.where(k == chips - 1, 1, jnp.where(k == 1, 0, k))
        turned = (order // 2 ^ (1 - place)) * 2 + order % 2
        part = jnp.where(of % 2 == stride % 2, 0, 1) + jnp.where(order // 2 == 1 - place, 0, 2)
        far = jnp.where(k == 0, 24 + turned, 28 + part * span + turn * 2 + order % 2)
        return jnp.where(of == stride, mine, edge), jnp.where(of == stride, mine, far)

    return pieces, weights, query, position


def rows_by_gather(own, place, stride, strides, heads):
    summary = SUMB * BLK
    share = summary // heads
    lower = place < heads // 2
    stride_rows = lax.all_gather(own, "head", axis=0, tiled=True)
    piece = lax.dynamic_slice_in_dim(stride_rows[-summary:], place * share, share, 0)
    far_rows = lax.all_gather(piece, ("blk", "head"), axis=0, tiled=True)
    half = stride_rows.shape[0] // 2
    steps = []
    for h in range(heads):
        for s in range(strides - 1):
            ends = (h * strides + s, h * strides + s + 1)
            steps.append(ends if h < heads // 2 else ends[::-1])
    edge = lax.ppermute(jnp.where(lower, stride_rows[half:], stride_rows[:half]), ("head", "blk"), steps)

    def position(block):
        rel = block - stride * SB
        near = jnp.where(rel < 0, rel + SB + REACH, rel)
        return near, SB + REACH + block // SB * SUMB + block % SB - (SB - SUMB)

    return [stride_rows, edge, far_rows], position


def on_device(tokens, proj_weight, out_weight, pattern):
    heads = lax.axis_size("head")
    strides = lax.axis_size("blk")
    place = lax.axis_index("head")
    stride = lax.axis_index("blk")
    own = tokens[0]
    blocks = own.shape[0] // BLK
    weights = split_weights(proj_weight)

    if heads == 2:
        pieces, weights, query, position = rows_by_axes(own, weights, place, stride, strides)
    else:
        pieces, position = rows_by_gather(own, place, stride, strides, heads)
        query = project_columns(weights[0], own, HD**-0.5)
    listed = lax.dynamic_slice_in_dim(pattern, place * blocks, blocks, 0)
    near, far = position(listed)
    table = jnp.where(lax.broadcasted_iota(jnp.int32, listed.shape, 1) < LSEL, near, far)

    _, key_weight, value_weight = weights
    keys = [project_rows(rows, key_weight) for rows in pieces]
    values = [project_columns(value_weight, rows) for rows in pieces]
    mixed = attend(table, query, keys, values, 4, 2)
    out = jnp.dot(mixed, out_weight, preferred_element_type=jnp.float32).astype(jnp.bfloat16)
    return out.reshape(tokens.shape)


def solution(mesh):
    return jax.shard_map(
        on_device,
        mesh=mesh,
        in_specs=(P(("batch", "blk"), "head", None), P(), P(), P(("batch", "blk"), None)),
        out_specs=P(("batch", "blk"), "head", None),
        check_vma=False,
    )
```

```python
import functools

import jax
import jax.numpy as jnp
from jax import lax
from jax.experimental import pallas as pl
from jax.experimental.pallas import tpu as pltpu
from jax.sharding import PartitionSpec as P

D = 1024
H = 16
HD = 64
BLK = 128
REACH = 8
LSEL = 6
SUMB = 4
SB = 16
KSEL = 16
PAIRS = H // 2
LANES = 2 * HD
TOTAL_CAP = 2.0**100


def split_kernel(weight_ref, query_ref, key_ref, value_ref):
    both = weight_ref[...]
    first, second = both[:, : 3 * HD], both[:, 3 * HD :]

    def columns(which):
        lo = which * HD
        return jnp.concatenate([first[:, lo : lo + HD], second[:, lo : lo + HD]], axis=1)

    query_ref[...] = columns(0).T
    key_ref[...] = columns(1)
    value_ref[...] = columns(2).T


def split_weights(proj_weight):
    wide = jax.ShapeDtypeStruct((D, D), jnp.bfloat16)
    across = pl.BlockSpec((LANES, D), lambda p: (p, 0))
    down = pl.BlockSpec((D, LANES), lambda p: (0, p))
    return pl.pallas_call(
        split_kernel,
        grid=(PAIRS,),
        in_specs=[pl.BlockSpec((D, 3 * LANES), lambda p: (0, p))],
        out_specs=[across, down, across],
        out_shape=[wide, wide, wide],
        cost_estimate=pl.CostEstimate(flops=0, bytes_accessed=4 * D * 3 * D, transcendentals=0),
        name="split_weights",
    )(proj_weight)


def attend_kernel(blocks, count, chunk, together, pieces, table_ref, query_ref, *refs):
    f32, bf16 = jnp.float32, jnp.bfloat16
    key_pieces, value_pieces = refs[:pieces], refs[pieces : 2 * pieces]
    out_ref, key_ref, value_ref, shift_ref, arrived = refs[2 * pieces :]
    step, steps = pl.program_id(0), pl.num_programs(0)
    slot = lax.rem(step, 2)

    def copies(pair, slot):
        lanes = pl.ds(pl.multiple_of(pair * LANES, LANES), LANES)
        found, start = [], 0
        for n, (key_piece, value_piece) in enumerate(zip(key_pieces, value_pieces)):
            span = pl.ds(start, key_piece.shape[0])
            found += [
                pltpu.make_async_copy(key_piece.at[:, lanes], key_ref.at[slot, span, :], arrived.at[slot, 2 * n]),
                pltpu.make_async_copy(
                    value_piece.at[lanes, :], value_ref.at[slot, :, span], arrived.at[slot, 2 * n + 1]
                ),
            ]
            start += key_piece.shape[0]
        return found

    @pl.when(step == 0)
    def _():
        for copy in copies(0, 0):
            copy.start()

    @pl.when(step + 1 < steps)
    def _():
        for copy in copies(step + 1, 1 - slot):
            copy.start()

    for copy in copies(step, slot):
        copy.wait()

    row = lax.broadcasted_iota(jnp.int32, (LANES, BLK), 0)

    def at(index):
        return pl.ds(pl.multiple_of(index * BLK, BLK), BLK)

    def queries(index):
        own = query_ref[:, at(index)]
        zero = jnp.zeros_like(own)
        return jnp.concatenate([jnp.where(row < HD, own, zero), jnp.where(row < HD, zero, own)], axis=1)

    def places(index, which, size):
        return [at(table_ref[index, which + n]) for n in range(size)]

    def score(index, which, size, query):
        keys = [key_ref[slot, place, :] for place in places(index, which, size)]
        return jnp.dot(jnp.concatenate(keys, axis=0), query, preferred_element_type=f32)

    def gather(index, which, size, raised):
        picked = jnp.concatenate([value_ref[slot, :, place] for place in places(index, which, size)], axis=1)
        ones = jnp.ones((16, raised.shape[0]), bf16)
        return jnp.dot(jnp.concatenate([picked, ones], axis=0), raised, preferred_element_type=f32)

    def finish(index, total):
        count_all = total[LANES : LANES + 1]
        scale = 1.0 / count_all
        mine = jnp.concatenate([total[:HD, :BLK] * scale[:, :BLK], total[HD:LANES, BLK:] * scale[:, BLK:]], axis=0)
        out_ref[at(index), :] = mine.T.astype(bf16)
        return count_all

    for index in range(blocks):
        shift_ref[index : index + 1, :] = jnp.max(score(index, 0, 1, queries(index)), axis=0, keepdims=True)

    def one(index):
        query = queries(index)
        total = None
        shift = shift_ref[pl.ds(index, 1), :]
        for which in range(0, count, chunk):
            raised = jnp.exp(score(index, which, chunk, query) - shift).astype(bf16)
            part = gather(index, which, chunk, raised)
            total = part if total is None else total + part
        return finish(index, total)

    def body(number, peak):
        for n in range(together):
            peak = jnp.maximum(peak, one(number * together + n))
        return peak

    peak = lax.fori_loop(0, blocks // together, body, jnp.zeros((1, 2 * BLK), f32))

    @pl.when(jnp.logical_not(jnp.max(peak) <= TOTAL_CAP))
    def _():
        def whole_row(index, carry):
            query = queries(index)

            def largest(n, shift):
                return jnp.maximum(shift, jnp.max(score(index, 2 * n, 2, query), axis=0, keepdims=True))

            shift = lax.fori_loop(0, count // 2, largest, jnp.full((1, 2 * BLK), -jnp.inf, f32))

            def add(n, total):
                raised = jnp.exp(score(index, 2 * n, 2, query) - shift).astype(bf16)
                return total + gather(index, 2 * n, 2, raised)

            finish(index, lax.fori_loop(0, count // 2, add, jnp.zeros((LANES + 16, 2 * BLK), f32)))
            return carry

        lax.fori_loop(0, blocks, whole_row, 0)


def attend(table, query, keys, values, chunk, together):
    rows = query.shape[1]
    blocks = rows // BLK
    count = table.shape[1]
    while blocks % together:
        together //= 2
    total_rows = sum(key.shape[0] for key in keys)
    scores = rows * count * BLK * H
    scratch = 8 * total_rows * LANES
    return pl.pallas_call(
        functools.partial(attend_kernel, blocks, count, chunk, together, len(keys)),
        grid=(PAIRS,),
        in_specs=[pl.BlockSpec(memory_space=pltpu.SMEM), pl.BlockSpec((LANES, rows), lambda p: (p, 0))]
        + [pl.BlockSpec(memory_space=pl.ANY)] * (2 * len(keys)),
        out_specs=pl.BlockSpec((rows, LANES), lambda p: (0, p)),
        out_shape=jax.ShapeDtypeStruct((rows, D), jnp.bfloat16),
        scratch_shapes=[
            pltpu.VMEM((2, total_rows, LANES), jnp.bfloat16),
            pltpu.VMEM((2, LANES, total_rows), jnp.bfloat16),
            pltpu.VMEM((blocks, 2 * BLK), jnp.float32),
            pltpu.SemaphoreType.DMA((2, 2 * len(keys))),
        ],
        compiler_params=pltpu.CompilerParams(vmem_limit_bytes=scratch + 10 * 2**20),
        cost_estimate=pl.CostEstimate(
            flops=24 * scores * HD, bytes_accessed=4 * total_rows * D + 4 * rows * D, transcendentals=scores
        ),
        name="attend",
    )(table, query, *keys, *values)


def project_rows(rows, weight):
    return jnp.dot(rows, weight, preferred_element_type=jnp.float32).astype(jnp.bfloat16)


def project_columns(weight, rows, scale=1.0):
    wide = lax.dot_general(weight, rows, (((1,), (1,)), ((), ())), preferred_element_type=jnp.float32)
    return (wide * scale).astype(jnp.bfloat16)


def rows_by_axes(own, weights, place, stride, strides):
    summary = SUMB * BLK
    half = summary // 2
    cut = own.shape[0] - summary
    chips = strides // 2
    low = place == 0
    swap = lambda rows: lax.ppermute(rows, "head", [(0, 1), (1, 0)])
    beside = lambda rows: lax.ppermute(rows, "blk", [(s, s ^ 1) for s in range(strides)])

    def along(rows, k):
        return lax.ppermute(rows, "blk", [(s, (s + 2 * k) % strides) for s in range(strides)])

    steps = []
    for s in range(strides - 1):
        steps += [(s, s + 1), (strides + s + 1, strides + s)]
    to_next = lambda rows: lax.ppermute(rows, ("head", "blk"), steps)

    other_end = swap(own[-half:])
    other_end, own, weights = lax.optimization_barrier((other_end, own, weights))
    carried = jnp.where(low, other_end, own[cut : cut + half])
    other = swap(own[:-half])
    edge_end = to_next(other_end)
    ends = [along(carried, 1), along(carried, chips - 1)]
    ends, after = lax.optimization_barrier((jnp.concatenate(ends, axis=0), carried))
    middle = jnp.concatenate([along(after, k) for k in range(2, chips - 1)], axis=0)
    other, other_end, released = lax.optimization_barrier((other, other_end, ends))
    across_ends = swap(released)
    edge = to_next(other)
    nearby = jnp.where(low, jnp.concatenate([other_end, other[-half:]], axis=0), own[cut:])
    beside_nearby, own = lax.optimization_barrier((beside(nearby), own))
    query = project_columns(weights[0], own, HD**-0.5)
    across_ends, middle = lax.optimization_barrier((across_ends, middle))
    across_middle = swap(middle)
    pieces = [own, other, other_end, edge, edge_end, beside_nearby]
    pieces += [ends, middle, beside(ends), beside(middle)]
    pieces += [across_ends, across_middle, beside(across_ends), beside(across_middle)]
    span = 2 * (chips - 1)

    def position(block):
        of, inside = block // SB, block % SB
        rel = block - stride * SB
        mine = inside % 8 + jnp.where(inside // 8 == place, 0, 8)
        edge = jnp.where(rel < 0, rel + SB + 8, rel)
        order = inside - (SB - SUMB)
        k = (stride // 2 - of // 2) % chips
        turn = jnp.where(k == chips - 1, 1, jnp.where(k == 1, 0, k))
        turned = (order // 2 ^ (1 - place)) * 2 + order % 2
        part = jnp.where(of % 2 == stride % 2, 0, 1) + jnp.where(order // 2 == 1 - place, 0, 2)
        far = jnp.where(k == 0, 24 + turned, 28 + part * span + turn * 2 + order % 2)
        return jnp.where(of == stride, mine, edge), jnp.where(of == stride, mine, far)

    return pieces, weights, query, position


def rows_by_gather(own, place, stride, strides, heads):
    summary = SUMB * BLK
    share = summary // heads
    lower = place < heads // 2
    stride_rows = lax.all_gather(own, "head", axis=0, tiled=True)
    piece = lax.dynamic_slice_in_dim(stride_rows[-summary:], place * share, share, 0)
    far_rows = lax.all_gather(piece, ("blk", "head"), axis=0, tiled=True)
    half = stride_rows.shape[0] // 2
    steps = []
    for h in range(heads):
        for s in range(strides - 1):
            ends = (h * strides + s, h * strides + s + 1)
            steps.append(ends if h < heads // 2 else ends[::-1])
    edge = lax.ppermute(jnp.where(lower, stride_rows[half:], stride_rows[:half]), ("head", "blk"), steps)

    def position(block):
        rel = block - stride * SB
        near = jnp.where(rel < 0, rel + SB + REACH, rel)
        return near, SB + REACH + block // SB * SUMB + block % SB - (SB - SUMB)

    return [stride_rows, edge, far_rows], position


def on_device(tokens, proj_weight, out_weight, pattern):
    heads = lax.axis_size("head")
    strides = lax.axis_size("blk")
    place = lax.axis_index("head")
    stride = lax.axis_index("blk")
    own = tokens[0]
    blocks = own.shape[0] // BLK
    weights = split_weights(proj_weight)

    if heads == 2:
        pieces, weights, query, position = rows_by_axes(own, weights, place, stride, strides)
    else:
        pieces, position = rows_by_gather(own, place, stride, strides, heads)
        query = project_columns(weights[0], own, HD**-0.5)
    listed = lax.dynamic_slice_in_dim(pattern, place * blocks, blocks, 0)
    near, far = position(listed)
    table = jnp.where(lax.broadcasted_iota(jnp.int32, listed.shape, 1) < LSEL, near, far)

    _, key_weight, value_weight = weights
    keys = [project_rows(rows, key_weight) for rows in pieces]
    values = [project_columns(value_weight, rows) for rows in pieces]
    mixed = attend(table, query, keys, values, 4, 4)
    out = jnp.dot(mixed, out_weight, preferred_element_type=jnp.float32).astype(jnp.bfloat16)
    return out.reshape(tokens.shape)


def solution(mesh):
    return jax.shard_map(
        on_device,
        mesh=mesh,
        in_specs=(P(("batch", "blk"), "head", None), P(), P(), P(("batch", "blk"), None)),
        out_specs=P(("batch", "blk"), "head", None),
        check_vma=False,
    )
```
